32 devices in a mesh: shards: 4 (over z), context: 2 (over x), tensor: 4 (over y, core).
Axes of the slice: x: 2, y: 2, z: 4, core: 2. Of those that a mesh axis runs over, the one named last changes fastest.
Arguments:
- block_input: bfloat16 [8, 1024, 2048], P('shards', 'context'), may hold values from -6 to 6
- output_grad: bfloat16 [8, 1024, 2048], P('shards', 'context'), may hold values from -6 to 6
- doc_lengths: int32 [8, 3], P('shards'), may hold values from 60 to 800, as said below
- norm_gain: bfloat16 [2048], P('shards'), may hold values from 0.5 to 1.5
- input_proj: bfloat16 [2048, 2, 4096], P('shards', None, 'tensor'), may hold values from -0.125 to 0.125
- conv_weight: bfloat16 [4096, 4], P(('tensor', 'shards')), may hold values from -3 to 3
- conv_bias: bfloat16 [4096], P(('tensor', 'shards')), may hold values from -3 to 3
- select_proj: bfloat16 [4096, 160], P(('tensor', 'shards')), may hold values from -0.09375 to 0.09375
- step_proj: bfloat16 [128, 4096], P('shards', 'tensor'), may hold values from -0.5 to 0.5
- step_bias: bfloat16 [4096], P(('tensor', 'shards')), may hold values from -7 to -3
- decay_log: bfloat16 [4096, 16], P(('tensor', 'shards')), may hold values from -4 to 0.5
- skip_weight: bfloat16 [4096], P(('tensor', 'shards')), may hold values from -4 to 4
- output_proj: bfloat16 [4096, 2048], P(('tensor', 'shards')), may hold values from -0.375 to 0.375
Outputs:
- block_output: bfloat16 [8, 1024, 2048], P('shards', 'context', 'tensor')
- input_grad: float32 [8, 1024, 2048], P('shards', 'context', 'tensor')
- norm_gain_grad: float32 [2048], P('shards')
- input_proj_grad: float32 [2048, 2, 4096], P('shards', None, 'tensor')
- conv_weight_grad: float32 [4096, 4], P(('tensor', 'shards'))
- conv_bias_grad: float32 [4096], P(('tensor', 'shards'))
- select_proj_grad: float32 [4096, 160], P(('tensor', 'shards'))
- step_proj_grad: float32 [128, 4096], P('shards', 'tensor')
- step_bias_grad: float32 [4096], P(('tensor', 'shards'))
- decay_log_grad: float32 [4096, 16], P(('tensor', 'shards'))
- skip_weight_grad: float32 [4096], P(('tensor', 'shards'))
- output_proj_grad: float32 [4096, 2048], P(('tensor', 'shards'))
The draws below stay inside these ranges and needn't reach their ends.
Inputs may be any that keep to these rules, and one draw needn't show every extreme that they name: `doc_lengths`: each row holds the lengths of the three documents packed in order into one sequence; each row sums to 1024.
All inputs are finite; a program needn't handle non-finite values.
Results may differ from the reference program's by a relative error of at most 0.011.
Values may be sent and summed in bfloat16 or wider, within the bound.
No kernel may reach another device: no remote copies, remote signals or barrier semaphores. Data moves between devices by JAX's collectives and lax.ppermute only.
A program may use at most 256 MiB of HBM per device.

```python
import math
import jax
import jax.numpy as jnp
from jax import lax

D = 2048
INNER = 4096
STATE = 16
RANK = 128
CONV = 4
BLOCK = 128
SEQ_LEN = 1024
SEQS = 2
SEQUENCES = 8
PIECE = 512
MIN_DOC = 60
MAX_DOC = 800
N_SHARDS = 4


def draw_doc_lengths(key, part):
    key = jax.random.fold_in(key, 17)
    subkeys = jax.random.split(key, 4)
    extra_total = SEQ_LEN - 3 * MIN_DOC
    extra_most = MAX_DOC - MIN_DOC
    row_index = jnp.arange(SEQUENCES, dtype=jnp.int32)
    first_extra = jax.random.randint(subkeys[0], (SEQUENCES,), extra_total - extra_most, extra_most + 1)
    second_extra = jax.random.randint(subkeys[1], (SEQUENCES,), 0, extra_total - first_extra + 1)
    picked = jax.random.randint(subkeys[2], (N_SHARDS,), 0, SEQS)
    spanning = jnp.arange(N_SHARDS, dtype=jnp.int32) * SEQS + picked
    shortest = (picked[0] + 1) % SEQS
    second_extra = jnp.where(row_index == shortest, 0, second_extra)
    third_extra = extra_total - first_extra - second_extra
    drawn = jnp.stack([MIN_DOC + first_extra, MIN_DOC + second_extra, MIN_DOC + third_extra], axis=-1)
    lead_least = max(MIN_DOC, SEQ_LEN - PIECE - MAX_DOC + 1)
    lead_most = min(PIECE - 1, SEQ_LEN - MAX_DOC - MIN_DOC)
    leading = jax.random.randint(subkeys[3], (SEQUENCES,), lead_least, lead_most + 1)
    long_rows = jnp.stack([leading, jnp.full((SEQUENCES,), MAX_DOC, jnp.int32), SEQ_LEN - MAX_DOC - leading], axis=-1)
    is_long = jnp.any(row_index[:, None] == spanning[None, :], axis=1)
    return jnp.where(is_long[:, None], long_rows, drawn).astype(jnp.int32)


def level_of(stream_key, shape, shards, least, high):
    def one(position, parts):
        draws = jax.random.uniform(jax.random.fold_in(jax.random.fold_in(stream_key, 6), position), (parts,), jnp.float32, least / len(shards), high / len(shards))
        return jnp.repeat(jnp.exp(draws), shape[position] // parts).reshape((-1,) + (1,) * (len(shape) - position - 1))

    factor_of = one(*shards[0])
    for cut in shards[1:]:
        factor_of = factor_of * one(*cut)
    return factor_of


def scatter_about(own_key, shape, width, reach, shards=(), kind=jnp.bfloat16):
    level = level_of(own_key, shape, shards, -0.22, 0.18) if shards else 1.0
    array = jax.random.normal(own_key, shape, jnp.float32) * width * level
    return jnp.minimum(jnp.maximum(array, -reach), reach).astype(kind)


def setup_inputs(seed: int = 0) -> dict:
    arg_keys = jax.random.split(jax.random.key(seed), 14)
    block_input = scatter_about(arg_keys[0], (SEQUENCES, SEQ_LEN, D), 1.0, 6.0, ((0, 4), (1, 2)))
    output_grad = scatter_about(arg_keys[1], (SEQUENCES, SEQ_LEN, D), 1.0, 6.0, ((0, 4), (1, 2)))
    doc_lengths = draw_doc_lengths(jax.random.fold_in(arg_keys[13], 71), 0)
    norm_gain = jnp.clip(1.0 + 0.1 * jax.random.normal(arg_keys[3], (D,), jnp.float32), 0.5, 1.5).astype(jnp.bfloat16)
    input_proj = scatter_about(arg_keys[4], (D, 2, INNER), D ** -0.5, 0.125, ((0, 4), (2, 4)))
    conv_weight = scatter_about(arg_keys[5], (INNER, CONV), CONV ** -0.5, 3.0, ((0, 16),))
    conv_bias = scatter_about(arg_keys[6], (INNER,), 0.5, 3.0, ((0, 16),))
    select_proj = scatter_about(arg_keys[7], (INNER, RANK + 2 * STATE), INNER ** -0.5, 0.09375, ((0, 16),))
    step_proj = scatter_about(arg_keys[8], (RANK, INNER), RANK ** -0.5, 0.5, ((0, 4), (1, 4)))
    step_bias = jnp.clip(-7.0 + 4.0 * jax.random.uniform(arg_keys[9], (INNER,), jnp.float32) ** level_of(arg_keys[9], (INNER,), ((0, 16),), -0.2, 0.2), -7.0, -3.0).astype(jnp.bfloat16)
    decay_log = jnp.clip(-4.0 + 4.5 * jax.random.uniform(arg_keys[10], (INNER, STATE), jnp.float32) ** level_of(arg_keys[10], (INNER, STATE), ((0, 16),), -0.2, 0.2), -4.0, 0.5).astype(jnp.bfloat16)
    skip_weight = scatter_about(arg_keys[11], (INNER,), 1.0, 4.0, ((0, 16),))
    output_proj = scatter_about(arg_keys[12], (INNER, D), (INNER // 16) ** -0.5, 0.375, ((0, 16),))
    return dict(block_input=block_input, output_grad=output_grad, doc_lengths=doc_lengths, norm_gain=norm_gain, input_proj=input_proj, conv_weight=conv_weight, conv_bias=conv_bias, select_proj=select_proj, step_proj=step_proj, step_bias=step_bias, decay_log=decay_log, skip_weight=skip_weight, output_proj=output_proj)


EPS = 1e-05
HIGHEST = lax.Precision.HIGHEST

@jax.custom_vjp
def low(v):
    return lax.optimization_barrier(v.astype(jnp.bfloat16)).astype(jnp.float32)

@jax.custom_vjp
def low_back(v):
    return v

def low_keep(v):
    return (low(v), None)

def low_pass(kept, grad):
    return (grad,)

def back_keep(v):
    return (v, None)

def back_low(kept, grad):
    return (low(grad),)
low.defvjp(low_keep, low_pass)
low_back.defvjp(back_keep, back_low)

def document_ids(lengths, positions):
    bounds = jnp.cumsum(lengths, axis=-1)[:, :2]
    passed = positions[None, :, None] >= bounds[:, None, :]
    return lax.optimization_barrier(jnp.sum(passed.astype(jnp.int32), axis=-1)).astype(jnp.int32)

def selective_scan(step_size, values, state_in, state_out, keep_flag, decay_rate):
    groups, length, inner_count = step_size.shape
    blocks = length // BLOCK

    def to_blocks(source):
        leading = jnp.moveaxis(source, 1, 0)
        return leading.reshape((blocks, BLOCK) + leading.shape[1:])

    def one_token(hidden_state, inputs):
        step_t, value_t, in_t, out_t, keep_t = inputs
        factor = keep_t[:, None, None] * jnp.exp(step_t[:, :, None] * decay_rate)
        hidden_state = factor * hidden_state + (step_t * value_t)[:, :, None] * in_t[:, None, :]
        return (hidden_state, lax.optimization_barrier(jnp.sum(hidden_state * out_t[:, None, :], axis=-1)))

    @jax.checkpoint
    def one_block(hidden_state, inputs):
        return lax.scan(one_token, hidden_state, inputs)
    start_state = jnp.zeros((groups, inner_count, STATE), step_size.dtype)
    block_inputs = tuple((to_blocks(member) for member in (step_size, values, state_in, state_out, keep_flag)))
    _, outputs = lax.scan(one_block, start_state, block_inputs)
    return jnp.moveaxis(outputs.reshape((length, groups, inner_count)), 0, 1)

def block_forward(block_input, document, norm_gain, input_proj, conv_weight, conv_bias, select_proj, step_proj, step_bias, decay_log, skip_weight, output_proj):
    groups, length, model_width = block_input.shape
    inv_rms = lax.rsqrt(lax.optimization_barrier(jnp.mean(block_input * block_input, axis=-1, keepdims=True)) + EPS)
    normed = low(block_input * inv_rms * norm_gain)
    projected_in = jnp.einsum('gld,dki->glki', normed, input_proj, precision=HIGHEST)
    x_part = low_back(low(projected_in[:, :, 0]))
    z_part = low_back(low(projected_in[:, :, 1]))
    conv_pre = conv_bias + jnp.zeros_like(x_part)
    for offset in range(CONV):
        distance = CONV - 1 - offset
        shifted = jnp.pad(x_part, ((0, 0), (distance, 0), (0, 0)))[:, :length]
        earlier = jnp.pad(document, ((0, 0), (distance, 0)), constant_values=-1)[:, :length]
        same_doc = (earlier == document)[:, :, None]
        conv_pre = conv_pre + jnp.where(same_doc, shifted, 0.0) * conv_weight[:, offset]
    values = low(jax.nn.silu(conv_pre))
    projected = low_back(jnp.einsum('gli,ir->glr', values, select_proj, precision=HIGHEST))
    step_low = low(projected[..., :RANK])
    state_in = projected[..., RANK:RANK + STATE]
    state_out = projected[..., RANK + STATE:]
    step_pre = low_back(jnp.einsum('glr,ri->gli', step_low, step_proj, precision=HIGHEST) + step_bias)
    step_size = jax.nn.softplus(step_pre)
    decay_rate = -jnp.exp(decay_log)
    earlier = jnp.pad(document, ((0, 0), (1, 0)), constant_values=-1)[:, :length]
    keep_flag = (earlier == document).astype(step_size.dtype)
    scanned = selective_scan(step_size, values, state_in, state_out, keep_flag, decay_rate)
    ssm_out = scanned + skip_weight * values
    gated_out = low(ssm_out * jax.nn.silu(z_part))
    return block_input + jnp.einsum('gli,id->gld', gated_out, output_proj, precision=HIGHEST)

def reference(block_input, output_grad, doc_lengths, norm_gain, input_proj, conv_weight, conv_bias, select_proj, step_proj, step_bias, decay_log, skip_weight, output_proj):
    weights = tuple((weight.astype(jnp.float32) for weight in (norm_gain, input_proj, conv_weight, conv_bias, select_proj, step_proj, step_bias, decay_log, skip_weight, output_proj)))
    positions = jnp.arange(SEQ_LEN, dtype=jnp.int32)
    document = document_ids(doc_lengths, positions)
    group_size = math.gcd(SEQUENCES, max(1, 4096 // SEQ_LEN))
    group_count = SEQUENCES // group_size

    def regroup(source):
        return source.reshape((group_count, group_size) + source.shape[1:])
    inputs_all = (regroup(block_input.astype(jnp.float32)), regroup(output_grad.astype(jnp.float32)), regroup(document))

    def one_group(running, inputs):
        input_part, grad_part, doc_part = inputs

        def forward(input_rows, *params):
            return block_forward(input_rows, doc_part, *params)
        result, pullback = jax.vjp(forward, input_part, *weights)
        gradients = pullback(grad_part)
        running = tuple((total_sum + gradient for total_sum, gradient in zip(running, gradients[1:])))
        return (running, (result.astype(jnp.bfloat16), gradients[0]))
    initial = tuple((jnp.zeros_like(weight) for weight in weights))
    totals, (outputs, input_grads) = lax.scan(one_group, initial, inputs_all)
    return (outputs.reshape(SEQUENCES, SEQ_LEN, D), input_grads.reshape(SEQUENCES, SEQ_LEN, D), totals[0], totals[1], totals[2], totals[3], totals[4], totals[5], totals[6], totals[7], totals[8], totals[9])
```

```python
import functools

import jax
import jax.numpy as jnp
from jax import lax
from jax.experimental import pallas as pl
from jax.experimental.pallas import tpu as pltpu
from jax.sharding import PartitionSpec as P

EPS = 1e-05
LANE = 128
LOG2E = 1.4426950408889634
BREAK = 1e6
f32 = jnp.float32
bf16 = jnp.bfloat16


def row8(ref, s, i, k, g):
    return jnp.broadcast_to(ref[s, i, k:k+1, g*LANE:(g+1)*LANE], (8, LANE))

def spread(bct_ref, hot_ref, wide, S, blocks):
    for s in range(S):
        rows = bct_ref[s].reshape(blocks*32, LANE)
        wide[s] = jnp.dot(rows, hot_ref[...], preferred_element_type=f32).reshape(blocks, 32, 8*LANE)

def fwd_kernel(S, G, L, se_ref, su_ref, bct_ref, rate_ref, hot_ref, sel_ref, y_ref, start_ref, h_s, wide, w_s):
    blocks = L//8
    @pl.when(pl.program_id(0) == 0)
    def _(): h_s[...] = jnp.zeros_like(h_s)
    start_ref[0] = h_s[...]
    spread(bct_ref, hot_ref, wide, S, blocks)
    def collect(i):
        for s in range(S):
            y_ref[s, i] = jnp.dot(sel_ref[...], w_s[i, s], preferred_element_type=f32)[0:8]
    def body(i, carry):
        hs = dict(zip([(s,g,j) for s in range(S) for g in range(G) for j in range(2)], carry))
        terms = {}
        for k in range(8):
            for s in range(S):
                b = [wide[s, i, j*8:(j+1)*8, k*LANE:(k+1)*LANE] for j in range(2)]
                c = [wide[s, i, 16+j*8:16+(j+1)*8, k*LANE:(k+1)*LANE] for j in range(2)]
                for g in range(G):
                    se = row8(se_ref, s, i, k, g); su = row8(su_ref, s, i, k, g)
                    prod = []
                    for j in range(2):
                        a = jnp.exp2(se*rate_ref[g, j*8:(j+1)*8])
                        h = a*hs[s,g,j] + su*b[j]
                        hs[s,g,j] = h
                        prod.append(c[j]*h)
                    w_s[i, s, k*16:(k+1)*16, g*LANE:(g+1)*LANE] = jnp.concatenate(prod, 0).astype(bf16)
        return tuple(hs.values())
    n = S*G*2
    out = lax.fori_loop(0, blocks, body, tuple(h_s[q*8:(q+1)*8] for q in range(n)))
    for i in range(blocks): collect(i)
    for q in range(n): h_s[q*8:(q+1)*8] = out[q]

def bwd_kernel(S, G, L, se_ref, su_ref, ds_ref, bct_ref, rate_ref, rate2_ref, hot_ref, sel_ref, start_ref,
               s_ref, q_ref, dbc_ref, dlog_ref, ag_s, h_s, wide):
    blocks = L//8
    keys = [(s,g,j) for s in range(S) for g in range(G) for j in range(2)]
    @pl.when(pl.program_id(0) == 0)
    def _():
        ag_s[...] = jnp.zeros_like(ag_s)
        dlog_ref[...] = jnp.zeros_like(dlog_ref)
    spread(bct_ref, hot_ref, wide, S, blocks)
    def again(i, carry):
        hs = dict(zip(keys, carry))
        for k in range(8):
            for s in range(S):
                b = [wide[s, i, j*8:(j+1)*8, k*LANE:(k+1)*LANE] for j in range(2)]
                for g in range(G):
                    se = row8(se_ref, s, i, k, g); su = row8(su_ref, s, i, k, g)
                    h_s[i*8+k, s*G+g] = jnp.concatenate([hs[s,g,0], hs[s,g,1]], 0).astype(bf16)
                    for j in range(2):
                        a = jnp.exp2(se*rate_ref[g, j*8:(j+1)*8])
                        hs[s,g,j] = a*hs[s,g,j] + su*b[j]
        return tuple(hs.values())
    n = S*G*2
    out = lax.fori_loop(0, blocks, again, tuple(start_ref[0, q*8:(q+1)*8] for q in range(n)))
    for s in range(S):
        for g in range(G):
            q = (s*G+g)*2
            h_s[L, s*G+g] = jnp.concatenate([out[q], out[q+1]], 0).astype(bf16)
    two = lambda v: jnp.concatenate([v, v], 0).astype(bf16)
    def body(r, carry):
        i = blocks - 1 - r
        ags = dict(zip(keys, carry))
        tq, ts, tl, tb, tc = {}, {}, {}, {}, {}
        for k in reversed(range(8)):
            for s in range(S):
                b16 = wide[s, i, 0:16, k*LANE:(k+1)*LANE].astype(bf16)
                c = [wide[s, i, 16+j*8:16+(j+1)*8, k*LANE:(k+1)*LANE] for j in range(2)]
                for g in range(G):
                    se = row8(se_ref, s, i, k, g); su = row8(su_ref, s, i, k, g); ds = row8(ds_ref, s, i, k, g)
                    a = [jnp.exp2(se*rate_ref[g, j*8:(j+1)*8]) for j in range(2)]
                    gr = [c[j]*ds + ags[s,g,j] for j in range(2)]
                    for j in range(2): ags[s,g,j] = a[j]*gr[j]
                    gb = jnp.concatenate(gr, 0).astype(bf16)
                    ab = jnp.concatenate(a, 0).astype(bf16)
                    gq = gb*(ab*h_s[i*8+k, s*G+g])
                    tq[s,g,k] = gq*rate2_ref[g]
                    tl[s,g,k] = gq*two(se)
                    ts[s,g,k] = gb*b16
                    tb[s,g,k] = gb*two(su)
                    tc[s,g,k] = h_s[i*8+k+1, s*G+g]*two(ds)
        def mat(t, s): return jnp.concatenate([jnp.concatenate([t[s,g,k] for k in range(8)], 0) for g in range(G)], 1)
        one = jnp.ones((16, G*LANE), bf16)
        for s in range(S):
            q_ref[s, i] = jnp.dot(sel_ref[...], mat(tq, s), preferred_element_type=f32)[0:8]
            s_ref[s, i] = jnp.dot(sel_ref[...], mat(ts, s), preferred_element_type=f32)[0:8]
            dlog_ref[...] += jnp.dot(hot16_of(sel_ref), mat(tl, s), preferred_element_type=f32)
            nt = (((1,), (1,)), ((), ()))
            dbc_ref[s, i, 0:1] = lax.dot_general(one, mat(tb, s), nt, preferred_element_type=f32)[0:1]
            dbc_ref[s, i, 1:2] = lax.dot_general(one, mat(tc, s), nt, preferred_element_type=f32)[0:1]
        return tuple(ags.values())
    ags = lax.fori_loop(0, blocks, body, tuple(ag_s[q*8:(q+1)*8] for q in range(n)))
    for q in range(n): ag_s[q*8:(q+1)*8] = ags[q]

def hot16_of(sel_ref):
    r = lax.broadcasted_iota(jnp.int32, (16, 128), 0); c = lax.broadcasted_iota(jnp.int32, (16, 128), 1)
    return (lax.rem(c, 16) == r).astype(bf16)

def constants():
    hot = (jnp.arange(128)[:,None] % 8 == (jnp.arange(8*LANE)//LANE)[None,:]) & (jnp.arange(128)[:,None] < 24)
    sel = jnp.arange(16)[:,None] == (jnp.arange(128)//16)[None,:]
    return hot.astype(bf16), sel.astype(bf16)

def by_eights(bc):
    S, T = bc.shape[:2]
    x = bc.reshape(S, T//8, 8, 32).swapaxes(2, 3)
    hi = lax.reduce_precision(x, 8, 7); mid = lax.reduce_precision(x - hi, 8, 7); lo = x - hi - mid
    hi, mid, lo = (v.astype(bf16) for v in (hi, mid, lo))
    return jnp.concatenate([hi, mid, lo, jnp.zeros(hi.shape[:3]+(104,), bf16)], -1)

def tok(S, L, C, rev=None):
    im = (lambda i: (0, i, 0, 0)) if rev is None else (lambda i: (0, rev-1-i, 0, 0))
    return pl.BlockSpec((S, L//8, 8, C), im)
def whole(*shape): return pl.BlockSpec(shape, lambda i: (0,)*len(shape))

def scan_forward(se, su, bct, rate2e, hot, sel, L=64):
    S, T, C = se.shape; G = C//LANE
    v = lambda x: x.reshape(S, T//8, 8, C)
    y, start = pl.pallas_call(functools.partial(fwd_kernel, S, G, L), grid=(T//L,),
        in_specs=[tok(S,L,C), tok(S,L,C), pl.BlockSpec((S, L//8, 32, LANE), lambda i: (0,i,0,0)), whole(G,16,LANE), whole(128, 8*LANE), whole(16,128)],
        out_specs=[tok(S,L,C), pl.BlockSpec((1, S*G*16, LANE), lambda i: (i,0,0))],
        out_shape=[jax.ShapeDtypeStruct((S,T//8,8,C), f32), jax.ShapeDtypeStruct((T//L, S*G*16, LANE), f32)],
        scratch_shapes=[pltpu.VMEM((S*G*16, LANE), f32), pltpu.VMEM((S, L//8, 32, 8*LANE), f32), pltpu.VMEM((L//8, S, LANE, C), bf16)],
        compiler_params=pltpu.CompilerParams(vmem_limit_bytes=56<<20))(v(se), v(su), bct, rate2e, hot, sel)
    return y.reshape(S,T,C), start

def scan_backward(se, su, ds, bct, rate2e, rate, hot, sel, start, L=64):
    S, T, C = se.shape; G = C//LANE; nb = T//L
    v = lambda x: x.reshape(S, T//8, 8, C)
    t = tok(S,L,C,nb)
    sg, q, dbc, dlog = pl.pallas_call(functools.partial(bwd_kernel, S, G, L), grid=(nb,),
        in_specs=[t, t, t, pl.BlockSpec((S, L//8, 32, LANE), lambda i: (0,nb-1-i,0,0)), whole(G,16,LANE), whole(G,16,LANE), whole(128, 8*LANE), whole(16,128),
                  pl.BlockSpec((1, S*G*16, LANE), lambda i: (nb-1-i,0,0))],
        out_specs=[t, t, pl.BlockSpec((S, L//8, 2, LANE), lambda i: (0,nb-1-i,0,0)), whole(16, C)],
        out_shape=[jax.ShapeDtypeStruct((S,T//8,8,C), f32)]*2 + [jax.ShapeDtypeStruct((S,T//8,2,LANE), f32), jax.ShapeDtypeStruct((16,C), f32)],
        scratch_shapes=[pltpu.VMEM((S*G*16, LANE), f32), pltpu.VMEM((L+1, S*G, 16, LANE), bf16), pltpu.VMEM((S, L//8, 32, 8*LANE), f32)],
        compiler_params=pltpu.CompilerParams(vmem_limit_bytes=56<<20))(v(se), v(su), v(ds), bct, rate2e, rate.astype(bf16), hot, sel, start)
    dbc = dbc.reshape(S, T//8, 2, 8, 16).swapaxes(2, 3).reshape(S, T, 32)
    return sg.reshape(S,T,C), q.reshape(S,T,C), dbc, dlog


def after(array, earlier_one):
    return lax.optimization_barrier((array, earlier_one))[0]


def line_gather(array, axis):
    count = lax.axis_size(axis)
    place = lax.axis_index(axis)
    right, left = array, array
    window = [array]
    for step in range(1, count):
        right = lax.ppermute(right, axis, [(i, i + 1) for i in range(step - 1, count - 1)])
        left = lax.ppermute(left, axis, [(i, i - 1) for i in range(1, count - step + 1)])
        window = [right] + window + [left]
    window = jnp.stack(window)
    return lax.dynamic_slice_in_dim(window, count - 1 - place, count, 0)


def line_gather_at_once(array, axis):
    count = lax.axis_size(axis)
    return lax.all_to_all(jnp.broadcast_to(array[None], (count,) + array.shape), axis, 0, 0)


def line_scatter(blocks, axis):
    return jnp.sum(lax.all_to_all(blocks, axis, 0, 0).astype(f32), axis=0)


class Paired:
    def __init__(self):
        self.context = lax.axis_index("context")
        self.tensor = lax.axis_index("tensor")
        self.core = self.tensor % 2

    def across(self, array):
        return lax.ppermute(array, "context", [(0, 1), (1, 0)])

    def near(self, array):
        return lax.ppermute(array, "tensor", [(0, 1), (1, 0), (2, 3), (3, 2)])

    def far(self, array):
        return lax.ppermute(array, "tensor", [(0, 2), (2, 0), (1, 3), (3, 1)])

    def pieces_soon(self, array):
        rows = array.shape[0]
        side = rows * 11 // 32
        middle = rows - 2 * side
        chip = self.tensor // 2

        def outer(chip, core):
            return chip * (side + middle) + core * (side // 2)

        def inner(core):
            return side + core * (middle // 2)

        one = self.across(lax.dynamic_slice_in_dim(array, outer(chip, self.core), side // 2, 0))
        two = self.across(lax.dynamic_slice_in_dim(array, inner(self.core), middle // 2, 0))
        three = self.far(one)
        out = jnp.zeros_like(array)
        for block, start, other in (
            (one, outer(chip, self.core), outer(chip, 1 - self.core)),
            (two, inner(self.core), inner(1 - self.core)),
            (three, outer(1 - chip, self.core), outer(1 - chip, 1 - self.core)),
        ):
            out = lax.dynamic_update_slice_in_dim(out, block, start, 0)
            out = lax.dynamic_update_slice_in_dim(out, self.near(block), other, 0)
        return [array, out]

    def pieces(self, array, dependency):
        half = array.shape[0] // 2
        block = self.across(after(lax.dynamic_slice_in_dim(array, self.core * half, half, 0), dependency))
        out = lax.dynamic_update_slice_in_dim(jnp.zeros_like(array), block, self.core * half, 0)
        out = lax.dynamic_update_slice_in_dim(out, self.near(block), (1 - self.core) * half, 0)
        return [array, out]

    def in_order(self, arrays, seqs):
        own, other = (a.reshape(seqs, -1, a.shape[-1]) for a in arrays)
        first = self.context == 0
        return jnp.concatenate([jnp.where(first, own, other), jnp.where(first, other, own)], axis=1)

    def own_first(self, array):
        piece = array.shape[1] // 2
        early, late = array[:, :piece], array[:, piece:]
        first = self.context == 0
        return [
            jnp.where(first, early, late).reshape(-1, array.shape[-1]),
            jnp.where(first, late, early).reshape(-1, array.shape[-1]),
        ]

    def total(self, array):
        half = array.shape[0] // 2
        mine = lax.dynamic_slice_in_dim(array, self.core * half, half, 0)
        other = lax.dynamic_slice_in_dim(array, (1 - self.core) * half, half, 0).astype(bf16)
        mine = mine + self.near(other).astype(f32)
        first, second = mine[: half // 2], mine[half // 2 :]
        first = first + self.far(first.astype(bf16)).astype(f32)
        second = second + self.across(second.astype(bf16)).astype(f32)
        first = first + self.across(first.astype(bf16)).astype(f32)
        second = second + self.far(second.astype(bf16)).astype(f32)
        mine = jnp.concatenate([first, second], axis=0)
        other = self.near(mine.astype(bf16)).astype(f32)
        zero = self.core == 0
        return jnp.concatenate([jnp.where(zero, mine, other), jnp.where(zero, other, mine)])

    def share(self, product):
        keep = product((self.tensor, self.tensor ^ 2))
        give = product((self.tensor ^ 1, self.tensor ^ 3))
        rows, width = keep[0].shape
        half, width = rows // 2, width // 2
        own, other = ((k.astype(f32) + self.near(g).astype(f32)) for k, g in zip(keep, give))
        far = self.far(jnp.stack([own[:half, width:], other[:half, width:]]).astype(bf16))
        across = self.across(other[half:].astype(bf16))
        first = own[:half, :width] + far[0].astype(f32)
        give = other[:half, :width] + far[1].astype(f32)
        second = own[half:] + across.astype(f32)
        first = first + self.across(give.astype(bf16)).astype(f32)
        second = second[:, :width] + self.far(second[:, width:].astype(bf16)).astype(f32)
        return jnp.concatenate([first, second], axis=0)

    def row_total(self, array):
        array = array + self.near(array)
        return array + self.far(array)

    def vector_total(self, array):
        return self.row_total(array + self.across(array))

    def both(self, array):
        other = self.across(array)
        zero = self.context == 0
        return jnp.stack([jnp.where(zero, array, other), jnp.where(zero, other, array)])


class General:
    def pieces_soon(self, array):
        return [lax.all_gather(array, "context", tiled=True)]

    def pieces(self, array, dependency):
        return self.pieces_soon(array)

    def in_order(self, arrays, seqs):
        array = arrays[0].reshape(lax.axis_size("context"), seqs, -1, arrays[0].shape[-1])
        return array.swapaxes(0, 1).reshape(seqs, -1, array.shape[-1])

    def own_first(self, array):
        width = array.shape[-1]
        array = array.reshape(array.shape[0], lax.axis_size("context"), -1, width)
        return [array.swapaxes(0, 1).reshape(-1, width)]

    def total(self, array):
        return lax.psum(array, ("context", "tensor"))

    def share(self, product):
        blocks = [product((block,))[0].astype(f32) for block in range(lax.axis_size("tensor"))]
        parts = lax.psum_scatter(jnp.concatenate(blocks, axis=-1), "context", scatter_dimension=0, tiled=True)
        return lax.psum_scatter(parts, "tensor", scatter_dimension=1, tiled=True)

    def row_total(self, array):
        return lax.psum(array, "tensor")

    def vector_total(self, array):
        return lax.psum(array, ("context", "tensor"))

    def both(self, array):
        return lax.all_gather(array, "context")


def document_ids(lengths, positions):
    bounds = jnp.cumsum(lengths, axis=-1)[:, :2]
    passed = positions[None, :, None] >= bounds[:, None, :]
    return jnp.sum(passed.astype(jnp.int32), axis=-1)


def earlier(array, by):
    return jnp.pad(array, ((0, 0), (by, 0), (0, 0)))[:, : array.shape[1]]


def later(array, by):
    return jnp.pad(array, ((0, 0), (0, by), (0, 0)))[:, by:]


def dot(a, b, out=f32):
    return jnp.dot(a, b, preferred_element_type=f32).astype(out)


def dot_t(a, b, out=f32):
    return lax.dot_general(a, b, (((1,), (1,)), ((), ())), preferred_element_type=f32).astype(out)


def t_dot(a, b, out=f32):
    return lax.dot_general(a, b, (((0,), (0,)), ((), ())), preferred_element_type=f32).astype(out)


def on_device(
    block_input,
    output_grad,
    doc_lengths,
    norm_gain,
    input_proj,
    conv_weight,
    conv_bias,
    select_proj,
    step_proj,
    step_bias,
    decay_log,
    skip_weight,
    output_proj,
):
    seqs, piece, model_width = block_input.shape
    shards, contexts, tensors = (lax.axis_size(axis) for axis in ("shards", "context", "tensor"))
    shard, context, tensor = (lax.axis_index(axis) for axis in ("shards", "context", "tensor"))
    moves = Paired() if (contexts, tensors) == (2, 4) else General()
    length = piece * contexts
    tokens = seqs * length
    depth = input_proj.shape[0]
    part = conv_weight.shape[0] // contexts
    inner = part * shards
    states = decay_log.shape[1]
    rank = step_proj.shape[0] * shards
    selected = select_proj.shape[1]
    taps = conv_weight.shape[1]
    share_width = model_width // tensors

    def mine(array):
        return lax.dynamic_slice_in_dim(array, context * part, part, 0)

    def my_columns(array):
        blocks = [
            lax.dynamic_slice_in_dim(array, (block * contexts + context) * part, part, array.ndim - 1)
            for block in range(shards)
        ]
        return jnp.concatenate(blocks, axis=-1)

    in_x = my_columns(input_proj[:, 0])
    in_z = my_columns(input_proj[:, 1])
    vectors = jnp.concatenate(
        [
            mine(select_proj),
            mine(conv_weight),
            mine(decay_log),
            mine(conv_bias)[:, None],
            mine(step_bias)[:, None],
            mine(skip_weight)[:, None],
        ],
        axis=1,
    )
    vectors = jnp.pad(vectors, ((0, 0), (0, 2 * LANE - vectors.shape[1])))
    flat = [in_x, my_columns(step_proj), vectors.reshape(-1, inner), norm_gain.reshape(-1, inner)]
    counts = [f.shape[0] for f in flat]
    starts_at = [sum(counts[:i]) for i in range(len(counts) + 1)]
    first_weights = line_gather(jnp.concatenate(flat, axis=0), "shards")

    def taken(i):
        return first_weights[:, starts_at[i] : starts_at[i + 1]]

    proj_x = taken(0).reshape(model_width, inner)
    proj_step = taken(1).reshape(rank, inner)
    vectors = taken(2).reshape(inner, 2 * LANE)
    gain = taken(3).reshape(model_width).astype(f32)
    proj_select = vectors[:, :selected]
    rest = vectors[:, selected:].astype(f32)
    conv_taps = rest[:, :taps].T
    decay_rate = -jnp.exp(rest[:, taps : taps + states])
    conv_shift, bias_step, skip = (rest[:, taps + states + i] for i in range(3))

    rows_all = moves.pieces_soon(block_input.reshape(seqs * piece, model_width))
    grad_all = moves.pieces(output_grad.reshape(seqs * piece, model_width), rows_all[-1])

    proj_z = line_gather_at_once(after(in_z, first_weights), "shards").reshape(model_width, inner)
    proj_out = line_gather_at_once(after(mine(output_proj), proj_z), "shards").reshape(inner, model_width)

    def normalised(array):
        wide = array.astype(f32)
        inv_rms = lax.rsqrt(jnp.mean(wide * wide, axis=-1, keepdims=True) + EPS)
        return wide * inv_rms, inv_rms

    normed = [(normalised(r)[0] * gain).astype(bf16) for r in rows_all]

    def to_channels(arrays, weights, product, out):
        return moves.in_order([product(a, weights, out) for a in arrays], seqs)

    document = document_ids(doc_lengths, jnp.arange(length, dtype=jnp.int32))
    doc_before = [jnp.pad(document, ((0, 0), (by, 0)), constant_values=-1)[:, :length] for by in range(taps)]
    doc_after = [jnp.pad(document, ((0, 0), (0, by)), constant_values=-1)[:, by:] for by in range(taps)]
    joined = [(b == document)[:, :, None] for b in doc_before]
    joins = [(a == document)[:, :, None] for a in doc_after]

    x_part = to_channels(normed, proj_x, dot, bf16)
    x_wide = x_part.astype(f32)
    conv_pre = conv_shift + x_wide * conv_taps[taps - 1]
    for by in range(1, taps):
        conv_pre = conv_pre + jnp.where(joined[by], earlier(x_wide, by), 0.0) * conv_taps[taps - 1 - by]
    values = jax.nn.silu(conv_pre).astype(bf16)
    value_rows = values.reshape(tokens, inner)
    projected = moves.total(dot(value_rows, proj_select))
    step_low = projected[:, :rank].astype(bf16)
    state_vectors = projected[:, rank:].reshape(seqs, length, 2 * states)
    step_pre = dot(step_low, proj_step).reshape(seqs, length, inner) + bias_step
    step = jax.nn.softplus(step_pre)
    values_wide = values.astype(f32)
    drive = step * values_wide
    step_keep = jnp.where(joined[1], step, BREAK)

    rate = decay_rate.T.reshape(states, inner // LANE, LANE).swapaxes(0, 1)
    hot, sel = constants()
    spread_in = by_eights(state_vectors)
    scanned, starts = scan_forward(step_keep, drive, spread_in, rate * LOG2E, hot, sel)

    z_part = to_channels(normed, proj_z, dot, bf16)
    grad_gated = to_channels(grad_all, proj_out, dot_t, f32)
    z_wide = z_part.astype(f32)
    z_sigmoid = jax.nn.sigmoid(z_wide)
    z_gate = z_wide * z_sigmoid
    ssm_out = scanned + skip * values_wide
    gated = moves.own_first((ssm_out * z_gate).astype(bf16))
    grad_ssm = grad_gated * z_gate
    grad_z = moves.own_first(
        (grad_gated * ssm_out * z_sigmoid * (1.0 + z_wide * (1.0 - z_sigmoid))).astype(bf16)
    )
    grad_skip = jnp.sum(grad_ssm * values_wide, axis=(0, 1))

    def weight_grad(lefts, rights):
        return sum(t_dot(a, b) for a, b in zip(lefts, rights)).astype(bf16)

    grad_in_z = line_scatter(weight_grad(normed, grad_z).reshape(shards, depth, inner), "shards")
    grad_out_proj = weight_grad(gated, grad_all).reshape(shards, part, model_width)
    grad_out_proj = line_scatter(after(grad_out_proj, grad_in_z), "shards")

    def chosen(weights, blocks, axis):
        return jnp.concatenate(
            [lax.dynamic_slice_in_dim(weights, b * share_width, share_width, axis) for b in blocks], axis
        )

    out_share = moves.share(lambda blocks: [dot(g, chosen(proj_out, blocks, 1), bf16) for g in gated])
    own_columns = tensor * share_width
    input_share = lax.dynamic_slice_in_dim(block_input, own_columns, share_width, 2).astype(f32)
    block_output = (input_share + out_share.reshape(input_share.shape)).astype(bf16)

    sums, pulls, grad_vectors, grad_decay = scan_backward(
        step_keep, drive, grad_ssm, spread_in, rate * LOG2E, rate, hot, sel, starts
    )
    grad_decay_log = grad_decay.T * decay_rate
    grad_step = pulls + values_wide * sums
    grad_step_pre = (grad_step * jax.nn.sigmoid(step_pre)).astype(bf16).reshape(tokens, inner)
    grad_step_bias = jnp.sum(grad_step_pre.astype(f32), axis=0)
    grad_step_proj = t_dot(step_low, grad_step_pre)
    grad_step_low = dot_t(grad_step_pre, proj_step)
    grad_projected = moves.total(
        jnp.concatenate([grad_step_low, grad_vectors.reshape(tokens, 2 * states)], axis=1)
    ).astype(bf16)
    grad_select = t_dot(value_rows, grad_projected)
    grad_values = dot_t(grad_projected, proj_select).reshape(seqs, length, inner) + step * sums + grad_ssm * skip
    conv_sigmoid = jax.nn.sigmoid(conv_pre)
    grad_conv = grad_values * conv_sigmoid * (1.0 + conv_pre * (1.0 - conv_sigmoid))
    grad_x = grad_conv * conv_taps[taps - 1]
    tap_grads = [jnp.sum(grad_conv * x_wide, axis=(0, 1))]
    for by in range(1, taps):
        grad_x = grad_x + jnp.where(joins[by], later(grad_conv, by), 0.0) * conv_taps[taps - 1 - by]
        tap_grads.insert(0, jnp.sum(jnp.where(joined[by], earlier(x_wide, by), 0.0) * grad_conv, axis=(0, 1)))
    grad_conv_bias = jnp.sum(grad_conv, axis=(0, 1))
    grad_x = moves.own_first(grad_x.astype(bf16))

    def normed_part(blocks):
        by_x, by_z = chosen(proj_x, blocks, 0), chosen(proj_z, blocks, 0)
        return [(dot_t(x, by_x) + dot_t(z, by_z)).astype(bf16) for x, z in zip(grad_x, grad_z)]

    grad_normed = moves.share(normed_part).reshape(seqs, piece, share_width)
    unit, inv_rms = normalised(block_input)
    unit_share = lax.dynamic_slice_in_dim(unit, own_columns, share_width, 2)
    weighted = grad_normed * lax.dynamic_slice_in_dim(gain, own_columns, share_width, 0)
    row_dots = moves.row_total(jnp.sum(unit_share * weighted, axis=-1))[:, :, None]
    grad_share = lax.dynamic_slice_in_dim(output_grad, own_columns, share_width, 2).astype(f32)
    input_grad = grad_share + inv_rms * (weighted - unit_share * (row_dots / model_width))

    small = jnp.concatenate(
        [
            grad_select,
            jnp.stack(tap_grads, axis=1),
            grad_decay_log,
            grad_conv_bias[:, None],
            grad_step_bias[:, None],
            grad_skip[:, None],
        ],
        axis=1,
    ).astype(bf16)
    small = jnp.pad(small, ((0, 0), (0, 2 * LANE - small.shape[1])))
    late = jnp.concatenate(
        [
            weight_grad(normed, grad_x).reshape(shards, depth, inner),
            grad_step_proj.astype(bf16).reshape(shards, -1, inner),
            small.reshape(shards, -1, inner),
        ],
        axis=1,
    )
    late = line_scatter(late, "shards")
    grad_in_x = late[:depth]
    gain_part = jnp.sum(in_x.astype(f32) * grad_in_x, axis=1) + jnp.sum(in_z.astype(f32) * grad_in_z, axis=1)
    grad_gain = moves.vector_total(gain_part) / norm_gain.astype(f32)

    def columns_of(pair):
        pair = pair.astype(f32).reshape(pair.shape[:-1] + (shards, part))
        return jnp.moveaxis(pair, 0, -2).reshape(pair.shape[1], -1)

    grad_in_z = moves.both(grad_in_z.astype(bf16))
    grad_out_proj = moves.both(grad_out_proj.astype(bf16))
    late = moves.both(late.astype(bf16))
    grad_in = jnp.stack([columns_of(late[:, :depth]), columns_of(grad_in_z)], axis=1)
    grad_step_proj = columns_of(late[:, depth : depth + step_proj.shape[0]])
    small = late[:, depth + step_proj.shape[0] :].reshape(contexts * part, 2 * LANE).astype(f32)
    at = selected + taps + states
    return (
        block_output,
        input_grad,
        grad_gain,
        grad_in,
        small[:, selected : selected + taps],
        small[:, at],
        small[:, :selected],
        grad_step_proj,
        small[:, at + 1],
        small[:, selected + taps : at],
        small[:, at + 2],
        grad_out_proj.reshape(contexts * part, model_width).astype(f32),
    )


def solution(mesh):
    placed = (
        P("shards", "context", None),
        P("shards", "context", None),
        P("shards", None),
        P("shards"),
        P("shards", None, "tensor"),
        P(("tensor", "shards"), None),
        P(("tensor", "shards")),
        P(("tensor", "shards"), None),
        P("shards", "tensor"),
        P(("tensor", "shards")),
        P(("tensor", "shards"), None),
        P(("tensor", "shards")),
        P(("tensor", "shards"), None),
    )
    return jax.shard_map(
        on_device,
        mesh=mesh,
        in_specs=placed,
        out_specs=(
            P("shards", "context", "tensor"),
            P("shards", "context", "tensor"),
            P("shards"),
            P("shards", None, "tensor"),
            P(("tensor", "shards"), None),
            P(("tensor", "shards")),
            P(("tensor", "shards"), None),
            P("shards", "tensor"),
            P(("tensor", "shards")),
            P(("tensor", "shards"), None),
            P(("tensor", "shards")),
            P(("tensor", "shards"), None),
        ),
        check_vma=False,
    )
```

```python
import functools

import jax
import jax.numpy as jnp
from jax import lax
from jax.experimental import pallas as pl
from jax.experimental.pallas import tpu as pltpu
from jax.sharding import PartitionSpec as P

EPS = 1e-05
LANE = 128
LOG2E = 1.4426950408889634
BREAK = 1e6
f32 = jnp.float32
bf16 = jnp.bfloat16


def row8(ref, s, i, k, g):
    return jnp.broadcast_to(ref[s, i, k : k + 1, g * LANE : (g + 1) * LANE], (8, LANE))


def mm(a, b):
    return jnp.dot(a, b, preferred_element_type=f32)


def mm_t(a, b):
    return lax.dot_general(a, b, (((1,), (1,)), ((), ())), preferred_element_type=f32)


def iota(shape, axis):
    return lax.broadcasted_iota(jnp.int32, shape, axis)


def cost(us):
    return pl.CostEstimate(flops=int(us * 1.15e8), bytes_accessed=int(us * 3.6e5), transcendentals=0)


PARAMS = pltpu.CompilerParams(vmem_limit_bytes=58 << 20)


def whole(*shape):
    return pl.BlockSpec(shape, lambda *_: (0,) * len(shape))


def rms(rows, gain):
    wide = rows.astype(f32)
    inv_rms = lax.rsqrt(jnp.mean(wide * wide, axis=-1, keepdims=True) + EPS)
    return (wide * inv_rms * gain).astype(bf16)


def joined_halves(first, second, place, gain=None):
    half, width = first.shape
    size = min(half, 128)
    count = half // size

    def kernel(place_ref, first_ref, second_ref, *rest):
        out_ref = rest[-1]
        this = (pl.program_id(0) // count) == place_ref[0]

        def put(ref):
            out_ref[...] = ref[...] if gain is None else rms(ref[...], rest[0][...])

        @pl.when(this)
        def _():
            put(first_ref)

        @pl.when(jnp.logical_not(this))
        def _():
            put(second_ref)

    def spec(which):
        def index(i, place):
            start = (place[0] ^ which) * count
            return (jnp.clip(i - start, 0, count - 1), 0)

        return pl.BlockSpec((size, width), index)

    extra = [] if gain is None else [gain.reshape(1, width)]
    return pl.pallas_call(
        kernel,
        grid_spec=pltpu.PrefetchScalarGridSpec(
            num_scalar_prefetch=1,
            grid=(2 * count,),
            in_specs=[spec(0), spec(1)] + [whole(1, width) for _ in extra],
            out_specs=pl.BlockSpec((size, width), lambda i, place: (i, 0)),
        ),
        out_shape=jax.ShapeDtypeStruct((2 * half, width), bf16),
        cost_estimate=cost(4),
        compiler_params=PARAMS,
    )(place, first, second, *extra)


def normalised_rows(rows, gain):
    count, width = rows.shape
    size = min(count, 256)

    def kernel(in_ref, gain_ref, out_ref, inv_ref):
        wide = in_ref[...].astype(f32)
        inv_rms = lax.rsqrt(jnp.mean(wide * wide, axis=-1, keepdims=True) + EPS)
        out_ref[...] = (wide * inv_rms * gain_ref[...]).astype(bf16)
        inv_ref[...] = jnp.broadcast_to(inv_rms, inv_ref.shape)

    by_rows = lambda w: pl.BlockSpec((size, w), lambda i: (i, 0))
    return pl.pallas_call(
        kernel,
        grid=(count // size,),
        in_specs=[by_rows(width), whole(1, width)],
        out_specs=[by_rows(width), by_rows(LANE)],
        out_shape=[jax.ShapeDtypeStruct(rows.shape, bf16), jax.ShapeDtypeStruct((count, LANE), f32)],
        cost_estimate=cost(4),
        compiler_params=PARAMS,
    )(rows, gain.reshape(1, width))


def unpacked(window, counts, place):
    slots = len(window)
    count = (slots + 1) // 2
    width = window[0].shape[1]
    starts = [sum(counts[:i]) for i in range(len(counts))]

    def kernel(place_ref, *refs):
        ins, outs = refs[:slots], refs[slots:]
        wanted = pl.program_id(0) + count - 1 - place_ref[0]
        for slot, ref in enumerate(ins):

            @pl.when(wanted == slot)
            def _(ref=ref):
                for out, start, rows in zip(outs, starts, counts):
                    out[0] = ref[start : start + rows]

    return pl.pallas_call(
        kernel,
        grid_spec=pltpu.PrefetchScalarGridSpec(
            num_scalar_prefetch=1,
            grid=(count,),
            in_specs=[whole(*window[0].shape) for _ in window],
            out_specs=[pl.BlockSpec((1, rows, width), lambda j, place: (j, 0, 0)) for rows in counts],
        ),
        out_shape=[jax.ShapeDtypeStruct((count, rows, width), bf16) for rows in counts],
        cost_estimate=cost(3),
        compiler_params=PARAMS,
    )(place, *window)


def products(lefts, more_lefts, right, more_right, blocks, width):
    n = len(lefts)
    count, inner = lefts[0].shape
    size = min(count, 512)

    def kernel(blocks_ref, *refs):
        a, b, (w, v), outs = refs[:n], refs[n : 2 * n], refs[2 * n : 2 * n + 2], refs[2 * n + 2 :]
        for i in range(n):
            outs[i][...] = (mm_t(a[i][...], w[...]) + mm_t(b[i][...], v[...])).astype(bf16)

    rows = pl.BlockSpec((size, inner), lambda j, i, blocks: (i, 0))
    weights = pl.BlockSpec((width, inner), lambda j, i, blocks: (blocks[j], 0))
    return pl.pallas_call(
        kernel,
        grid_spec=pltpu.PrefetchScalarGridSpec(
            num_scalar_prefetch=1,
            grid=(blocks.shape[0], count // size),
            in_specs=[rows] * (2 * n) + [weights] * 2,
            out_specs=[pl.BlockSpec((size, width), lambda j, i, blocks: (i, j))] * n,
        ),
        out_shape=[jax.ShapeDtypeStruct((count, width * blocks.shape[0]), bf16)] * n,
        cost_estimate=cost(5),
        compiler_params=PARAMS,
    )(blocks, *lefts, *more_lefts, right, more_right)


def interleaved(first, second, depth, part):
    contexts, _, inner = first.shape
    shards = inner // part
    size = 64

    def kernel(a_ref, b_ref, out_ref):
        for which, ref in enumerate((a_ref, b_ref)):
            columns = [
                ref[c, :, s * part : (s + 1) * part].astype(f32) for s in range(shards) for c in range(contexts)
            ]
            out_ref[:, which, :] = jnp.concatenate(columns, axis=1)

    return pl.pallas_call(
        kernel,
        grid=(depth // size,),
        in_specs=[pl.BlockSpec((contexts, size, inner), lambda i: (0, i, 0))] * 2,
        out_specs=pl.BlockSpec((size, 2, contexts * inner), lambda i: (i, 0, 0)),
        out_shape=jax.ShapeDtypeStruct((depth, 2, contexts * inner), f32),
        cost_estimate=cost(5),
        compiler_params=PARAMS,
    )(first, second)


class Rows:
    def __init__(self, seqs, length, arrays, size, reverse=False):
        self.pieces = arrays
        self.size = size
        self.count = length // size
        self.per = self.count // arrays
        self.grid = (seqs, self.count)
        self.reverse = reverse

    def at(self, i):
        return self.count - 1 - i if self.reverse else i

    def spec(self, which, width):
        def index(s, i, place):
            low = (place[0] ^ which) * self.per
            return (s * self.per + jnp.clip(self.at(i) - low, 0, self.per - 1), 0)

        return pl.BlockSpec((self.size, width), index)

    def is_turn(self, which, place_ref):
        return (self.at(pl.program_id(1)) // self.per) == (place_ref[0] ^ which)

    def block(self, width):
        return pl.BlockSpec((1, self.size, width), lambda s, i, place: (s, self.at(i), 0))

    def packed(self, rows):
        return pl.BlockSpec((1, self.size // LANE, rows, LANE), lambda s, i, place: (s, self.at(i), 0, 0))


def convolved(xs, masks_ref, vec_ref, size, taps):
    total = vec_ref[taps : taps + 1]
    for by in range(taps):
        term = xs[8 - by : 8 - by + size] * vec_ref[taps - 1 - by : taps - by]
        total = total + (term * masks_ref[0, :, by : by + 1] if by else term)
    return total


def convolve(normed, proj_x, vec, masks, select_low, select_state, place, taps):
    seqs, length = masks.shape[:2]
    width, inner = proj_x.shape
    size = min(256, length)
    rows = Rows(seqs, length, len(normed), size)
    packed = select_low.shape[1] + select_state.shape[0]

    def kernel(place_ref, *refs):
        ins, (w_ref, vec_ref, masks_ref, low_ref, state_ref, x_ref, u_ref, p_ref, xs) = (
            refs[: len(normed)],
            refs[len(normed) :],
        )
        fresh = pl.program_id(1) == 0

        @pl.when(fresh)
        def _():
            xs[0:8] = jnp.zeros((8, inner), f32)

        @pl.when(jnp.logical_not(fresh))
        def _():
            xs[0:8] = xs[size : size + 8]

        for which, ref in enumerate(ins):

            @pl.when(rows.is_turn(which, place_ref))
            def _(ref=ref):
                x = mm(ref[...], w_ref[...]).astype(bf16)
                x_ref[0] = x
                xs[8 : 8 + size] = x.astype(f32)

        pre = convolved(xs, masks_ref, vec_ref, size, taps)
        u = (pre / (1.0 + jnp.exp(-pre))).astype(bf16)
        u_ref[0] = u
        low = mm(u, low_ref[...])
        state = mm_t(state_ref[...], u)
        for j in range(size // LANE):
            p_ref[0, j, 0:LANE] = low[j * LANE : (j + 1) * LANE]
            p_ref[0, j, LANE:packed] = state[:, j * LANE : (j + 1) * LANE]

    return pl.pallas_call(
        kernel,
        grid_spec=pltpu.PrefetchScalarGridSpec(
            num_scalar_prefetch=1,
            grid=rows.grid,
            in_specs=[rows.spec(i, width) for i in range(len(normed))]
            + [whole(width, inner), whole(8, inner), rows.block(LANE), whole(*select_low.shape), whole(*select_state.shape)],
            out_specs=[rows.block(inner), rows.block(inner), rows.packed(packed)],
            scratch_shapes=[pltpu.VMEM((size + 8, inner), f32)],
        ),
        out_shape=[
            jax.ShapeDtypeStruct((seqs, length, inner), bf16),
            jax.ShapeDtypeStruct((seqs, length, inner), bf16),
            jax.ShapeDtypeStruct((seqs, length // LANE, packed, LANE), f32),
        ],
        cost_estimate=cost(9),
        compiler_params=PARAMS,
    )(place, *normed, proj_x, vec, masks, select_low, select_state)


def gates(normed, grads, proj_z, proj_out, ssm_out, place):
    seqs, length, inner = ssm_out.shape
    width = proj_z.shape[0]
    size = min(256, length)
    rows = Rows(seqs, length, len(normed), size)
    n = len(normed)

    def kernel(place_ref, *refs):
        a_refs, g_refs, (z_ref, o_ref, s_ref), outs = refs[:n], refs[n : 2 * n], refs[2 * n : 2 * n + 3], refs[2 * n + 3 :]
        for which in range(n):

            @pl.when(rows.is_turn(which, place_ref))
            def _(which=which):
                z = mm(a_refs[which][...], z_ref[...]).astype(bf16).astype(f32)
                grad = mm_t(g_refs[which][...], o_ref[...])
                ssm = s_ref[0]
                sigmoid = 1.0 / (1.0 + jnp.exp(-z))
                gate = z * sigmoid
                outs[which][...] = (ssm * gate).astype(bf16)
                outs[n + which][...] = (grad * ssm * sigmoid * (1.0 + z * (1.0 - sigmoid))).astype(bf16)
                outs[2 * n][0] = grad * gate

    total = seqs * length // n
    outs = pl.pallas_call(
        kernel,
        grid_spec=pltpu.PrefetchScalarGridSpec(
            num_scalar_prefetch=1,
            grid=rows.grid,
            in_specs=[rows.spec(i, width) for i in range(n)] * 2
            + [whole(width, inner), whole(inner, width), rows.block(inner)],
            out_specs=[rows.spec(i, inner) for i in range(n)] * 2 + [rows.block(inner)],
        ),
        out_shape=[jax.ShapeDtypeStruct((total, inner), bf16)] * (2 * n) + [jax.ShapeDtypeStruct((seqs, length, inner), f32)],
        cost_estimate=cost(14),
        compiler_params=PARAMS,
    )(place, *normed, *grads, proj_z, proj_out, ssm_out)
    return outs[:n], outs[n : 2 * n], outs[2 * n]


def convolve_back(packed, direct, x_part, vec, masks, select_low, select_state, place, n, taps):
    seqs, length, inner = x_part.shape
    size = min(256, length)
    rows = Rows(seqs, length, n, size, reverse=True)
    states = (packed.shape[2] - LANE) // 2

    def kernel(place_ref, p_ref, d_ref, x_ref, edge_ref, vec_ref, masks_ref, low_ref, state_ref, *rest):
        outs, (sum_ref, tok_ref, xs, ds) = rest[:n], rest[n:]
        fresh = pl.program_id(1) == 0

        @pl.when(jnp.logical_and(fresh, pl.program_id(0) == 0))
        def _():
            sum_ref[...] = jnp.zeros_like(sum_ref)

        @pl.when(fresh)
        def _():
            ds[size : size + 8] = jnp.zeros((8, inner), f32)

        @pl.when(jnp.logical_not(fresh))
        def _():
            ds[size : size + 8] = ds[0:8]

        copy = (iota((LANE, 16), 0) // 8 == iota((LANE, 16), 1)).astype(bf16)
        place_of = (iota((LANE, LANE), 1) // 16) == lax.rem(iota((LANE, LANE), 0), 8)
        by_state = lax.rem(iota((LANE, LANE), 0), 16)
        for j in range(size // LANE):
            at = slice(j * LANE, (j + 1) * LANE)
            tok_ref[0, at, 0:LANE] = p_ref[0, j, 0:LANE].astype(bf16)
            token = jnp.zeros((LANE, LANE), f32)
            for q in range(2):
                part = p_ref[0, j, LANE + q * states : LANE + (q + 1) * states].astype(bf16)
                spread = jnp.where(place_of, mm(copy, part), 0.0).astype(bf16)
                token = token + mm(spread, (by_state + q * states == iota((LANE, LANE), 1)).astype(bf16))
            tok_ref[0, at, LANE : 2 * LANE] = token.astype(bf16)
        xs[0:8] = edge_ref[0, 8:16].astype(f32)
        xs[8 : 8 + size] = x_ref[0].astype(f32)
        pre = convolved(xs, masks_ref, vec_ref, size, taps)
        sigmoid = 1.0 / (1.0 + jnp.exp(-pre))
        grad = mm_t(tok_ref[0, :, 0:LANE], low_ref[...]) + mm_t(tok_ref[0, :, LANE : 2 * LANE], state_ref[...]) + d_ref[0]
        grad = grad * sigmoid * (1.0 + pre * (1.0 - sigmoid))
        ds[0:size] = grad
        total = grad * vec_ref[taps - 1 : taps]
        sum_ref[taps : taps + 1] += jnp.sum(grad, axis=0, keepdims=True)
        sum_ref[taps - 1 : taps] += jnp.sum(grad * xs[8 : 8 + size], axis=0, keepdims=True)
        for by in range(1, taps):
            tap = taps - 1 - by
            total = total + ds[by : by + size] * masks_ref[0, :, taps + by : taps + by + 1] * vec_ref[tap : tap + 1]
            joint = grad * xs[8 - by : 8 - by + size] * masks_ref[0, :, by : by + 1]
            sum_ref[tap : tap + 1] += jnp.sum(joint, axis=0, keepdims=True)
        for which in range(n):

            @pl.when(rows.is_turn(which, place_ref))
            def _(which=which):
                outs[which][...] = total.astype(bf16)

    edge = pl.BlockSpec((1, 16, inner), lambda s, i, place: (s, jnp.maximum(rows.at(i) * (size // 16) - 1, 0), 0))
    outs = pl.pallas_call(
        kernel,
        grid_spec=pltpu.PrefetchScalarGridSpec(
            num_scalar_prefetch=1,
            grid=rows.grid,
            in_specs=[
                rows.packed(packed.shape[2]),
                rows.block(inner),
                rows.block(inner),
                edge,
                whole(8, inner),
                rows.block(LANE),
                whole(inner, LANE),
                whole(inner, LANE),
            ],
            out_specs=[rows.spec(i, inner) for i in range(n)] + [whole(8, inner), rows.block(2 * LANE)],
            scratch_shapes=[pltpu.VMEM((size + 8, inner), f32)] * 2,
        ),
        out_shape=[jax.ShapeDtypeStruct((seqs * length // n, inner), bf16)] * n
        + [jax.ShapeDtypeStruct((8, inner), f32), jax.ShapeDtypeStruct((seqs, length, 2 * LANE), bf16)],
        cost_estimate=cost(10),
        compiler_params=PARAMS,
    )(place, packed, direct, x_part, x_part, vec, masks, select_low, select_state)
    return outs[:n], outs[n], outs[n + 1]


def log_one_plus(v):
    small = v * (1.0 - v * (0.5 - v * (1.0 / 3.0 - v * 0.25)))
    return jnp.where(v < 0.01, small, jnp.log(1.0 + v))


def softplus(v):
    return jnp.maximum(v, 0.0) + log_one_plus(jnp.exp(-jnp.abs(v)))


def sigmoid_of_step(step):
    small = step * (1.0 - step * (0.5 - step * (1.0 / 6.0 - step * (1.0 / 24.0))))
    return jnp.where(step < 0.02, small, 1.0 - jnp.exp(-step))


def hot_rows():
    row, col = iota((LANE, 8 * LANE), 0), iota((LANE, 8 * LANE), 1)
    return ((lax.rem(row, 8) == col // LANE) & (row < 16)).astype(bf16)


def spread(state, hot, wide, s, blocks):
    high = state.astype(bf16).astype(f32)
    rest = state - high
    lane = iota(state.shape, 1)
    parts = []
    for i in range(blocks):
        a = pltpu.roll(high, (LANE - 8 * i) % LANE, 1)
        b = pltpu.roll(rest, (LANE + 8 - 8 * i) % LANE, 1)
        parts.append(jnp.where(lane < 8, a, b).astype(bf16))
    wide[s] = mm(jnp.concatenate(parts, axis=0), hot).reshape(blocks, state.shape[0], 8 * LANE)


def forward_kernel(
    S, G, p_ref, u_ref, masks_ref, proj_ref, vec_ref, rate_ref, hot_ref, y_ref, step_ref, start_ref, h_s, wide, w_s, se_s, su_s
):
    blocks = LANE // 8
    C = G * LANE

    @pl.when(pl.program_id(0) == 0)
    def _():
        h_s[...] = jnp.zeros_like(h_s)

    start_ref[0] = h_s[...]
    for s in range(S):
        step = softplus(mm(p_ref[s, 0, 0:LANE].astype(bf16), proj_ref[...]) + vec_ref[0:1])
        step_ref[s] = step
        u = u_ref[s].astype(f32)
        se_s[s] = jnp.where(masks_ref[s, :, 1:2] > 0.5, step, BREAK).reshape(blocks, 8, C)
        su_s[s] = (step * u).reshape(blocks, 8, C)
        spread(p_ref[s, 0, LANE : LANE + 32], hot_ref[...], wide, s, blocks)
    keys = [(s, g, j) for s in range(S) for g in range(G) for j in range(2)]

    def body(i, carry):
        hs = dict(zip(keys, carry))
        for k in range(8):
            for s in range(S):
                lanes = slice(k * LANE, (k + 1) * LANE)
                b = [wide[s, i, j * 8 : (j + 1) * 8, lanes] for j in range(2)]
                c = [wide[s, i, 16 + j * 8 : 16 + (j + 1) * 8, lanes] for j in range(2)]
                for g in range(G):
                    se, su = row8(se_s, s, i, k, g), row8(su_s, s, i, k, g)
                    prod = []
                    for j in range(2):
                        a = jnp.exp2(se * rate_ref[g, j * 8 : (j + 1) * 8])
                        hs[s, g, j] = a * hs[s, g, j] + su * b[j]
                        prod.append(c[j] * hs[s, g, j])
                    w_s[i, s, k * 16 : (k + 1) * 16, g * LANE : (g + 1) * LANE] = jnp.concatenate(prod, 0).astype(bf16)
        return tuple(hs.values())

    out = lax.fori_loop(0, blocks, body, tuple(h_s[q * 8 : (q + 1) * 8] for q in range(len(keys))))
    pick = (iota((16, 2 * LANE), 0) == iota((16, 2 * LANE), 1) // 16).astype(bf16)
    for s in range(S):
        for i in range(blocks // 2):
            both = jnp.concatenate([w_s[2 * i, s], w_s[2 * i + 1, s]], axis=0)
            y_ref[s, i * 16 : (i + 1) * 16] = mm(pick, both)
        y_ref[s] = y_ref[s] + vec_ref[1:2] * u_ref[s].astype(f32)
    for q in range(len(keys)):
        h_s[q * 8 : (q + 1) * 8] = out[q]


def backward_kernel(
    S, G, p_ref, u_ref, step_ref, ds_ref, masks_ref, proj_ref, vec_ref, rate_ref, rate2_ref, hot_ref, start_ref,
    dsp_ref, du_ref, p2_ref, dlog_ref, sum_ref, ag_s, h_s, wide, se_s, su_s, s_s, q_s, d_s, r_s
):
    blocks = LANE // 8
    C = G * LANE
    keys = [(s, g, j) for s in range(S) for g in range(G) for j in range(2)]

    @pl.when(pl.program_id(0) == 0)
    def _():
        ag_s[...] = jnp.zeros_like(ag_s)
        dlog_ref[...] = jnp.zeros_like(dlog_ref)
        sum_ref[...] = jnp.zeros_like(sum_ref)

    for s in range(S):
        step = step_ref[s]
        u = u_ref[s].astype(f32)
        se_s[s] = jnp.where(masks_ref[s, :, 1:2] > 0.5, step, BREAK).reshape(blocks, 8, C)
        su_s[s] = (step * u).reshape(blocks, 8, C)
        d_s[s] = ds_ref[s].reshape(blocks, 8, C)
        spread(p_ref[s, 0, LANE : LANE + 32], hot_ref[...], wide, s, blocks)

    def again(i, carry):
        hs = dict(zip(keys, carry))
        for k in range(8):
            for s in range(S):
                b = [wide[s, i, j * 8 : (j + 1) * 8, k * LANE : (k + 1) * LANE] for j in range(2)]
                for g in range(G):
                    se, su = row8(se_s, s, i, k, g), row8(su_s, s, i, k, g)
                    h_s[i * 8 + k, s * G + g] = jnp.concatenate([hs[s, g, 0], hs[s, g, 1]], 0).astype(bf16)
                    for j in range(2):
                        a = jnp.exp2(se * rate_ref[g, j * 8 : (j + 1) * 8])
                        hs[s, g, j] = a * hs[s, g, j] + su * b[j]
        return tuple(hs.values())

    out = lax.fori_loop(0, blocks, again, tuple(start_ref[0, q * 8 : (q + 1) * 8] for q in range(len(keys))))
    for s in range(S):
        for g in range(G):
            q = (s * G + g) * 2
            h_s[LANE, s * G + g] = jnp.concatenate([out[q], out[q + 1]], 0).astype(bf16)

    def two(v):
        return jnp.concatenate([v, v], 0).astype(bf16)

    pick = (iota((16, 2 * LANE), 0) == iota((16, 2 * LANE), 1) // 16).astype(bf16)
    fold = (lax.rem(iota((16, 2 * LANE), 1), 16) == iota((16, 2 * LANE), 0)).astype(bf16)
    one = jnp.ones((16, LANE), bf16)
    lane, row = iota((8, LANE), 1), iota((8, LANE), 0)

    def across_rows(product):
        found = product[0:8]
        for v in range(1, 16):
            found = jnp.where(lane >= 8 * v, product[8 * v : 8 * v + 8], found)
        found = jnp.sum(jnp.where(lax.rem(lane, 8) == row, found, 0.0), axis=0, keepdims=True)
        return jnp.broadcast_to(found, (8, LANE))

    def body(r, carry):
        low = blocks - 2 - 2 * r
        ags = dict(zip(keys, carry))
        tq, ts, tl, tb, tc = {}, {}, {}, {}, {}
        for t in reversed(range(16)):
            i, k = low + t // 8, t % 8
            for s in range(S):
                lanes = slice(k * LANE, (k + 1) * LANE)
                b16 = wide[s, i, 0:16, lanes].astype(bf16)
                c = [wide[s, i, 16 + j * 8 : 16 + (j + 1) * 8, lanes] for j in range(2)]
                for g in range(G):
                    se, su, ds = row8(se_s, s, i, k, g), row8(su_s, s, i, k, g), row8(d_s, s, i, k, g)
                    a = [jnp.exp2(se * rate_ref[g, j * 8 : (j + 1) * 8]) for j in range(2)]
                    gr = [c[j] * ds + ags[s, g, j] for j in range(2)]
                    for j in range(2):
                        ags[s, g, j] = a[j] * gr[j]
                    gb = jnp.concatenate(gr, 0).astype(bf16)
                    ab = jnp.concatenate(a, 0).astype(bf16)
                    gq = gb * (ab * h_s[i * 8 + k, s * G + g])
                    tq[s, g, t] = gq * rate2_ref[g]
                    tl[s, g, t] = gq * two(se)
                    ts[s, g, t] = gb * b16
                    tb[s, g, t] = gb * two(su)
                    tc[s, g, t] = h_s[i * 8 + k + 1, s * G + g] * two(ds)

        def mat(m, s):
            return jnp.concatenate([jnp.concatenate([m[s, g, t] for t in range(16)], 0) for g in range(G)], 1)

        def msum(m, s):
            return jnp.concatenate([sum(m[s, g, t] for g in range(G)) for t in range(16)], 0)

        for s in range(S):
            q = mm(pick, mat(tq, s))
            v = mm(pick, mat(ts, s))
            for h in range(2):
                q_s[s, low + h] = q[h * 8 : (h + 1) * 8]
                s_s[s, low + h] = v[h * 8 : (h + 1) * 8]
            dlog_ref[...] += mm(fold, mat(tl, s))
            for kind, m in enumerate((tb, tc)):
                found = mm_t(one, msum(m, s))[0:8]
                for h in range(2):
                    r_s[s, kind, low + h] = found[:, h * LANE : (h + 1) * LANE]
        return tuple(ags.values())

    ags = lax.fori_loop(0, blocks // 2, body, tuple(ag_s[q * 8 : (q + 1) * 8] for q in range(len(keys))))
    for q in range(len(keys)):
        ag_s[q * 8 : (q + 1) * 8] = ags[q]
    for s in range(S):
        step = step_ref[s]
        u = u_ref[s].astype(f32)
        ds = ds_ref[s]
        sums = s_s[s].reshape(LANE, C)
        dsp = ((q_s[s].reshape(LANE, C) + u * sums) * sigmoid_of_step(step)).astype(bf16)
        dsp_ref[s] = dsp
        du_ref[s] = step * sums + ds * vec_ref[1:2]
        p2_ref[s, 0, 0:LANE] = mm_t(dsp, proj_ref[...])
        for kind in range(2):
            for i in range(blocks):
                p2_ref[s, 0, LANE + 16 * kind + i : LANE + 16 * kind + i + 1] = r_s[s, kind, i, 0:1]
        sum_ref[0:1] += jnp.sum(dsp.astype(f32), axis=0, keepdims=True)
        sum_ref[1:2] += jnp.sum(ds * u, axis=0, keepdims=True)


def scan_specs(S, T, C, reverse):
    at = (lambda i: T // LANE - 1 - i) if reverse else (lambda i: i)
    return dict(
        packed=pl.BlockSpec((S, 1, LANE + 32, LANE), lambda i: (0, at(i), 0, 0)),
        block=pl.BlockSpec((S, LANE, C), lambda i: (0, at(i), 0)),
        masks=pl.BlockSpec((S, LANE, LANE), lambda i: (0, at(i), 0)),
        start=pl.BlockSpec((1, S * C // LANE * 16, LANE), lambda i: (at(i), 0, 0)),
    )


def scan_forward(packed, u, masks, proj_step, vec, rate2e, hot):
    S, T, C = u.shape
    G = C // LANE
    sp = scan_specs(S, T, C, False)
    by_token = pltpu.VMEM((S, LANE // 8, 8, C), f32)
    return pl.pallas_call(
        functools.partial(forward_kernel, S, G),
        grid=(T // LANE,),
        in_specs=[
            sp["packed"], sp["block"], sp["masks"], whole(LANE, C), whole(8, C), whole(G, 16, LANE), whole(LANE, 8 * LANE)
        ],
        out_specs=[sp["block"], sp["block"], sp["start"]],
        out_shape=[jax.ShapeDtypeStruct((S, T, C), f32)] * 2 + [jax.ShapeDtypeStruct((T // LANE, S * G * 16, LANE), f32)],
        scratch_shapes=[
            pltpu.VMEM((S * G * 16, LANE), f32),
            pltpu.VMEM((S, LANE // 8, 32, 8 * LANE), f32),
            pltpu.VMEM((LANE // 8, S, LANE, C), bf16),
            by_token,
            by_token,
        ],
        cost_estimate=cost(30),
        compiler_params=PARAMS,
    )(packed, u, masks, proj_step, vec, rate2e, hot)


def scan_backward(packed, u, step, ds, masks, proj_step, vec, rate2e, rate, hot, starts):
    S, T, C = u.shape
    G = C // LANE
    sp = scan_specs(S, T, C, True)
    by_token = pltpu.VMEM((S, LANE // 8, 8, C), f32)
    return pl.pallas_call(
        functools.partial(backward_kernel, S, G),
        grid=(T // LANE,),
        in_specs=[
            sp["packed"], sp["block"], sp["block"], sp["block"], sp["masks"], whole(LANE, C), whole(8, C),
            whole(G, 16, LANE), whole(G, 16, LANE), whole(LANE, 8 * LANE), sp["start"]
        ],
        out_specs=[sp["block"], sp["block"], sp["packed"], whole(16, C), whole(8, C)],
        out_shape=[
            jax.ShapeDtypeStruct((S, T, C), bf16),
            jax.ShapeDtypeStruct((S, T, C), f32),
            jax.ShapeDtypeStruct((S, T // LANE, LANE + 32, LANE), f32),
            jax.ShapeDtypeStruct((16, C), f32),
            jax.ShapeDtypeStruct((8, C), f32),
        ],
        scratch_shapes=[
            pltpu.VMEM((S * G * 16, LANE), f32),
            pltpu.VMEM((LANE + 1, S * G, 16, LANE), bf16),
            pltpu.VMEM((S, LANE // 8, 32, 8 * LANE), f32),
        ]
        + [by_token] * 5
        + [pltpu.VMEM((S, 2, LANE // 8, 8, LANE), f32)],
        cost_estimate=cost(85),
        compiler_params=PARAMS,
    )(packed, u, step, ds, masks, proj_step, vec, rate2e, rate.astype(bf16), hot, starts)


def after(*arrays):
    def kernel(*refs):
        refs[-1][0] = 0

    return pl.pallas_call(
        kernel,
        in_specs=[pl.BlockSpec(memory_space=pl.ANY) for _ in arrays],
        out_specs=pl.BlockSpec(memory_space=pltpu.SMEM),
        out_shape=jax.ShapeDtypeStruct((1,), jnp.int32),
    )(*arrays)[0]


def line_gather(array, axis):
    count = lax.axis_size(axis)
    right, left = array, array
    window = [array]
    for step in range(1, count):
        right = lax.ppermute(right, axis, [(i, i + 1) for i in range(step - 1, count - 1)])
        left = lax.ppermute(left, axis, [(i, i - 1) for i in range(1, count - step + 1)])
        window = [right] + window + [left]
    return window


def line_gather_at_once(array, axis):
    count = lax.axis_size(axis)
    return lax.all_to_all(jnp.broadcast_to(array[None], (count,) + array.shape), axis, 0, 0)


def line_scatter(blocks, axis):
    return jnp.sum(lax.all_to_all(blocks, axis, 0, 0).astype(f32), axis=0)


class Paired:
    def __init__(self):
        self.context = lax.axis_index("context")
        self.tensor = lax.axis_index("tensor")
        self.core = self.tensor % 2
        self.place = self.context[None]

    def across(self, array):
        return lax.ppermute(array, "context", [(0, 1), (1, 0)])

    def near(self, array):
        return lax.ppermute(array, "tensor", [(0, 1), (1, 0), (2, 3), (3, 2)])

    def far(self, array):
        return lax.ppermute(array, "tensor", [(0, 2), (2, 0), (1, 3), (3, 1)])

    def pieces(self, array, begin):
        half = array.shape[0] // 2
        mine = lax.dynamic_slice_in_dim(array, (self.core + begin) * half, half, 0)
        return self.across(mine), mine

    def pieces_done(self, array, block):
        return [array, joined_halves(block, self.near(block), self.core[None])]

    def normed(self, array, block, gain):
        own, inv_rms = normalised_rows(array, gain)
        return [own, joined_halves(block, self.near(block), self.core[None], gain)], inv_rms

    def total(self, array, begin):
        half = array.shape[0] // 2
        mine = lax.dynamic_slice_in_dim(array, self.core * half, half, 0)
        other = lax.dynamic_slice_in_dim(array, (1 - self.core + begin) * half, half, 0).astype(bf16)
        mine = mine + self.near(other).astype(f32)
        first, second = mine[: half // 2], mine[half // 2 :]
        first = first + self.far(first.astype(bf16)).astype(f32)
        second = second + self.across(second.astype(bf16)).astype(f32)
        first = first + self.across(first.astype(bf16)).astype(f32)
        second = second + self.far(second.astype(bf16)).astype(f32)
        mine = jnp.concatenate([first, second], axis=0)
        other = self.near(mine.astype(bf16)).astype(f32)
        zero = self.core == 0
        return jnp.concatenate([jnp.where(zero, mine, other), jnp.where(zero, other, mine)])

    def share_begin(self, product):
        keep = product((self.tensor, self.tensor ^ 2))
        give = product((self.tensor ^ 1, self.tensor ^ 3))
        return [(k.astype(f32) + self.near(g).astype(f32)) for k, g in zip(keep, give)]

    def share_middle(self, sums):
        own, other = sums
        rows, width = own.shape
        half, width = rows // 2, width // 2
        far = self.far(jnp.stack([own[:half, width:], other[:half, width:]]).astype(bf16))
        across = self.across(other[half:].astype(bf16))
        first = own[:half, :width] + far[0].astype(f32)
        give = other[:half, :width] + far[1].astype(f32)
        second = own[half:] + across.astype(f32)
        return first, give, second

    def share_end(self, sums):
        first, give, second = sums
        width = first.shape[1]
        first = first + self.across(give.astype(bf16)).astype(f32)
        second = second[:, :width] + self.far(second[:, width:].astype(bf16)).astype(f32)
        return jnp.concatenate([first, second], axis=0)

    def row_total(self, array):
        array = array + self.near(array)
        return array + self.far(array)

    def vector_total(self, array):
        return self.row_total(array + self.across(array))

    def both(self, array):
        other = self.across(array)
        zero = self.context == 0
        return jnp.stack([jnp.where(zero, array, other), jnp.where(zero, other, array)])


class General:
    def __init__(self, seqs):
        self.seqs = seqs
        self.place = jnp.zeros((1,), jnp.int32)

    def pieces(self, array, begin):
        return lax.all_gather(array, "context", tiled=True), array

    def pieces_done(self, array, block):
        return [self.in_order([block], self.seqs).reshape(block.shape)]

    def normed(self, array, block, gain):
        inv_rms = normalised_rows(array, gain)[1]
        return [normalised_rows(self.pieces_done(array, block)[0], gain)[0]], inv_rms

    def in_order(self, arrays, seqs):
        array = arrays[0].reshape(lax.axis_size("context"), seqs, -1, arrays[0].shape[-1])
        return array.swapaxes(0, 1).reshape(seqs, -1, array.shape[-1])

    def total(self, array, begin):
        return lax.psum(array, ("context", "tensor"))

    def share_begin(self, product):
        return [product((block,))[0].astype(f32) for block in range(lax.axis_size("tensor"))]

    def share_middle(self, sums):
        return sums

    def share_end(self, sums):
        parts = jnp.concatenate(sums, axis=-1)
        shape = parts.shape
        parts = parts.reshape(self.seqs, lax.axis_size("context"), -1, shape[-1]).swapaxes(0, 1).reshape(shape)
        parts = lax.psum_scatter(parts, "context", scatter_dimension=0, tiled=True)
        return lax.psum_scatter(parts, "tensor", scatter_dimension=1, tiled=True)

    def row_total(self, array):
        return lax.psum(array, "tensor")

    def vector_total(self, array):
        return lax.psum(array, ("context", "tensor"))

    def both(self, array):
        return lax.all_gather(array, "context")


def document_ids(lengths, positions):
    bounds = jnp.cumsum(lengths, axis=-1)[:, :2]
    passed = positions[None, :, None] >= bounds[:, None, :]
    return jnp.sum(passed.astype(jnp.int32), axis=-1)


def dot(a, b, out=f32):
    return jnp.dot(a, b, preferred_element_type=f32).astype(out)


def dot_t(a, b, out=f32):
    return lax.dot_general(a, b, (((1,), (1,)), ((), ())), preferred_element_type=f32).astype(out)


def t_dot(a, b, out=f32):
    return lax.dot_general(a, b, (((0,), (0,)), ((), ())), preferred_element_type=f32).astype(out)


def on_device(
    block_input,
    output_grad,
    doc_lengths,
    norm_gain,
    input_proj,
    conv_weight,
    conv_bias,
    select_proj,
    step_proj,
    step_bias,
    decay_log,
    skip_weight,
    output_proj,
):
    seqs, piece, model_width = block_input.shape
    shards, contexts, tensors = (lax.axis_size(axis) for axis in ("shards", "context", "tensor"))
    shard, context, tensor = (lax.axis_index(axis) for axis in ("shards", "context", "tensor"))
    moves = Paired() if (contexts, tensors) == (2, 4) else General(seqs)
    length = piece * contexts
    tokens = seqs * length
    depth = input_proj.shape[0]
    part = conv_weight.shape[0] // contexts
    inner = part * shards
    states = decay_log.shape[1]
    rank = step_proj.shape[0] * shards
    selected = select_proj.shape[1]
    taps = conv_weight.shape[1]
    share_width = model_width // tensors

    def mine(array):
        return lax.dynamic_slice_in_dim(array, context * part, part, 0)

    def my_columns(array, begin):
        blocks = [
            lax.dynamic_slice_in_dim(array, (block * contexts + context + begin) * part, part, array.ndim - 1)
            for block in range(shards)
        ]
        return jnp.concatenate(blocks, axis=-1)

    rows_flat = block_input.reshape(seqs * piece, model_width)
    row_block, row_slice = moves.pieces(rows_flat, 0)
    in_x = my_columns(input_proj[:, 0], after(row_slice))
    vectors = jnp.concatenate(
        [
            mine(select_proj),
            mine(conv_weight),
            mine(decay_log),
            mine(conv_bias)[:, None],
            mine(step_bias)[:, None],
            mine(skip_weight)[:, None],
        ],
        axis=1,
    )
    vectors = jnp.pad(vectors, ((0, 0), (0, 2 * LANE - vectors.shape[1])))
    flat = [in_x, my_columns(step_proj, 0), vectors.reshape(-1, inner), norm_gain.reshape(-1, inner)]
    flat = [jnp.pad(f, ((0, -f.shape[0] % 16), (0, 0))) for f in flat]
    window = line_gather(jnp.concatenate(flat, axis=0), "shards")
    proj_x, proj_step, vectors, gain = unpacked(window, [f.shape[0] for f in flat], shard[None])
    proj_x = proj_x.reshape(model_width, inner)
    proj_step = proj_step[:, : step_proj.shape[0]].reshape(rank, inner)
    vectors = vectors[:, : 2 * LANE * part // inner].reshape(inner, 2 * LANE)
    gain = gain[:, : norm_gain.shape[0] // inner].reshape(model_width).astype(f32)
    proj_select = vectors[:, :selected]
    rest = vectors[:, selected:].astype(f32)
    decay_rate = -jnp.exp(rest[:, taps : taps + states])
    at = taps + states
    conv_vec = jnp.concatenate([rest[:, :taps].T, rest[:, at][None], jnp.zeros((7 - taps, inner), f32)], axis=0)
    scan_vec = jnp.concatenate([rest[:, at + 1 : at + 3].T, jnp.zeros((6, inner), f32)], axis=0)
    select_low, select_state = proj_select[:, :rank], proj_select[:, rank:]

    normed, inv_rms = moves.normed(rows_flat, row_block, gain)
    grad_flat = output_grad.reshape(seqs * piece, model_width)
    grad_block = moves.pieces(grad_flat, after(row_block))[0]

    in_z = my_columns(input_proj[:, 1], after(window[len(window) // 2 - 1]))
    out_own = mine(output_proj)
    out_own = [out_own[:, i * inner : (i + 1) * inner] for i in range(model_width // inner)]
    others = jnp.concatenate([in_z] + out_own + [jnp.zeros((16, inner), bf16)], axis=0)
    others = lax.dynamic_slice_in_dim(others, after(proj_x) * 16, others.shape[0] - 16, 0)
    others = line_gather_at_once(others, "shards")

    document = document_ids(doc_lengths, jnp.arange(length, dtype=jnp.int32))
    masks = [jnp.pad(document, ((0, 0), (by, 0)), constant_values=-1)[:, :length] for by in range(taps)]
    masks += [jnp.pad(document, ((0, 0), (0, by)), constant_values=-1)[:, by:] for by in range(taps)]
    masks = jnp.stack([m == document for m in masks], axis=-1).astype(f32)
    masks = jnp.pad(masks, ((0, 0), (0, 0), (0, LANE - 2 * taps)))

    x_part, values, projected = convolve(
        normed, proj_x, conv_vec, masks, select_low, select_state.T, moves.place, taps
    )

    def total(packed, begin):
        return moves.total(packed.reshape(-1, LANE), begin).reshape(packed.shape)

    projected = total(projected, 0)

    hot = hot_rows()

    def by_group(array, begin=0.0):
        return (array.T + begin).reshape(states, inner // LANE, LANE).swapaxes(0, 1)

    ssm_out, step, starts = scan_forward(
        projected, values, masks, proj_step, scan_vec, by_group(decay_rate * LOG2E), hot
    )

    proj_z = others[:, :depth].reshape(model_width, inner)
    proj_out = jnp.concatenate(
        [others[:, depth + i * part : depth + (i + 1) * part] for i in range(model_width // inner)], axis=-1
    ).reshape(inner, model_width)
    grad_all = moves.pieces_done(grad_flat, grad_block)
    gated, grad_z, grad_ssm = gates(normed, grad_all, proj_z, proj_out, ssm_out, moves.place)

    def weight_grad(lefts, rights):
        return sum(t_dot(a, b) for a, b in zip(lefts, rights)).astype(bf16)

    early = [weight_grad(normed, grad_z).reshape(shards, depth, inner)]
    for i in range(model_width // inner):
        columns = [g[:, i * inner : (i + 1) * inner] for g in grad_all]
        early.append(weight_grad(gated, columns).reshape(shards, part, inner))
    early = line_scatter(jnp.concatenate(early, axis=1), "shards")
    grad_in_z = early[:depth]
    early_pair = moves.both(early.astype(bf16))
    in_z_pair, out_pair = early_pair[:, :depth], early_pair[:, depth:]

    def chosen(weights, blocks, axis, begin=0):
        return jnp.concatenate(
            [lax.dynamic_slice_in_dim(weights, (b + begin) * share_width, share_width, axis) for b in blocks], axis
        )

    out_sums = moves.share_begin(lambda blocks: [dot(g, chosen(proj_out, blocks, 1), bf16) for g in gated])
    out_sums_2 = moves.share_middle(out_sums)
    out_share = moves.share_end(out_sums_2)
    own_columns = tensor * share_width
    input_share = lax.dynamic_slice_in_dim(block_input, own_columns, share_width, 2).astype(f32)
    block_output = (input_share + out_share.reshape(input_share.shape)).astype(bf16)

    grad_step_pre, grad_direct, partial_grad, grad_decay, scan_sums = scan_backward(
        projected,
        values,
        step,
        grad_ssm,
        masks,
        proj_step,
        scan_vec,
        by_group(decay_rate * LOG2E),
        by_group(decay_rate, after(*out_sums).astype(f32)),
        hot,
        starts,
    )
    grad_decay_log = grad_decay.T * decay_rate
    step_low = projected[:, :, :rank].reshape(tokens, rank).astype(bf16)
    grad_step_proj = t_dot(step_low, grad_step_pre.reshape(tokens, inner))
    partial_grad = total(partial_grad, after(*out_sums_2))
    grad_x, conv_sums, grad_selected = convolve_back(
        partial_grad,
        grad_direct,
        x_part,
        conv_vec + after(block_output, early).astype(f32),
        masks,
        select_low,
        jnp.pad(select_state, ((0, 0), (0, LANE - select_state.shape[1]))),
        moves.place,
        len(normed),
        taps,
    )
    grad_select = t_dot(values.reshape(tokens, inner), grad_selected.reshape(tokens, -1))[:, :selected]

    small = jnp.concatenate(
        [
            grad_select,
            conv_sums[:taps].T,
            grad_decay_log,
            conv_sums[taps][:, None],
            scan_sums[:2].T,
        ],
        axis=1,
    ).astype(bf16)
    small = jnp.pad(small, ((0, 0), (0, 2 * LANE - small.shape[1])))
    late_local = jnp.concatenate(
        [
            weight_grad(normed, grad_x).reshape(shards, depth, inner),
            grad_step_proj.astype(bf16).reshape(shards, -1, inner),
            small.reshape(shards, -1, inner),
        ],
        axis=1,
    )
    begin = after(late_local)

    def normed_part(blocks):
        blocks = jnp.stack([jnp.asarray(b, jnp.int32) + begin for b in blocks])
        return products(grad_x, grad_z, proj_x, proj_z, blocks, share_width)

    grad_normed = moves.share_end(moves.share_middle(moves.share_begin(normed_part))).reshape(seqs, piece, share_width)
    inv_rms = inv_rms[:, :1].reshape(seqs, piece, 1)
    unit_share = input_share * inv_rms
    weighted = grad_normed * lax.dynamic_slice_in_dim(gain, own_columns, share_width, 0)
    row_dots = moves.row_total(jnp.sum(unit_share * weighted, axis=-1))[:, :, None]
    grad_share = lax.dynamic_slice_in_dim(output_grad, own_columns, share_width, 2).astype(f32)
    input_grad = grad_share + inv_rms * (weighted - unit_share * (row_dots / model_width))

    late = line_scatter(late_local, "shards")+ after(grad_normed, early_pair).astype(f32)
    grad_in_x = late[:depth]
    gain_part = jnp.sum(in_x.astype(f32) * grad_in_x, axis=1) + jnp.sum(in_z.astype(f32) * grad_in_z, axis=1)
    grad_gain = moves.vector_total(gain_part) / norm_gain.astype(f32)

    def columns_of(pair):
        pair = pair.astype(f32).reshape(pair.shape[:-1] + (shards, part))
        return jnp.moveaxis(pair, 0, -2).reshape(pair.shape[1], -1)

    late = moves.both(late.astype(bf16))
    grad_in = interleaved(late, early_pair, depth, part)
    grad_step_proj = columns_of(late[:, depth : depth + step_proj.shape[0]])
    small = late[:, depth + step_proj.shape[0] :].reshape(contexts * part, 2 * LANE).astype(f32)
    grad_out_proj = [out_pair[:, i * part : (i + 1) * part] for i in range(model_width // inner)]
    grad_out_proj = jnp.concatenate(grad_out_proj, axis=-1).reshape(contexts * part, model_width).astype(f32)
    at = selected + taps + states
    return (
        block_output,
        input_grad,
        grad_gain,
        grad_in,
        small[:, selected : selected + taps],
        small[:, at],
        small[:, :selected],
        grad_step_proj,
        small[:, at + 1],
        small[:, selected + taps : at],
        small[:, at + 2],
        grad_out_proj,
    )


def solution(mesh):
    placed = (
        P("shards", "context", None),
        P("shards", "context", None),
        P("shards", None),
        P("shards"),
        P("shards", None, "tensor"),
        P(("tensor", "shards"), None),
        P(("tensor", "shards")),
        P(("tensor", "shards"), None),
        P("shards", "tensor"),
        P(("tensor", "shards")),
        P(("tensor", "shards"), None),
        P(("tensor", "shards")),
        P(("tensor", "shards"), None),
    )
    return jax.shard_map(
        on_device,
        mesh=mesh,
        in_specs=placed,
        out_specs=(
            P("shards", "context", "tensor"),
            P("shards", "context", "tensor"),
            P("shards"),
            P("shards", None, "tensor"),
            P(("tensor", "shards"), None),
            P(("tensor", "shards")),
            P(("tensor", "shards"), None),
            P("shards", "tensor"),
            P(("tensor", "shards")),
            P(("tensor", "shards"), None),
            P(("tensor", "shards")),
            P(("tensor", "shards"), None),
        ),
        check_vma=False,
    )
```

```python
import functools

import jax
import jax.numpy as jnp
from jax import lax
from jax.experimental import pallas as pl
from jax.experimental.pallas import tpu as pltpu
from jax.sharding import PartitionSpec as P

EPS = 1e-05
LANE = 128
LOG2E = 1.4426950408889634
BREAK = 1e6
f32 = jnp.float32
bf16 = jnp.bfloat16


def row8(ref, s, i, k, g):
    return jnp.broadcast_to(ref[s, i, k : k + 1, g * LANE : (g + 1) * LANE], (8, LANE))


def mm(a, b):
    return jnp.dot(a, b, preferred_element_type=f32)


def mm_t(a, b):
    return lax.dot_general(a, b, (((1,), (1,)), ((), ())), preferred_element_type=f32)


def iota(shape, axis):
    return lax.broadcasted_iota(jnp.int32, shape, axis)


def cost(us):
    return pl.CostEstimate(flops=int(us * 1.15e8), bytes_accessed=int(us * 3.6e5), transcendentals=0)


PARAMS = pltpu.CompilerParams(vmem_limit_bytes=58 << 20)


def whole(*shape):
    return pl.BlockSpec(shape, lambda *_: (0,) * len(shape))


def rms(rows, gain):
    wide = rows.astype(f32)
    inv_rms = lax.rsqrt(jnp.mean(wide * wide, axis=-1, keepdims=True) + EPS)
    return (wide * inv_rms * gain).astype(bf16)


def joined_halves(first, second, place, gain=None):
    half, width = first.shape
    size = min(half, 128)
    count = half // size

    def kernel(place_ref, first_ref, second_ref, *rest):
        out_ref = rest[-1]
        this = (pl.program_id(0) // count) == place_ref[0]

        def put(ref):
            out_ref[...] = ref[...] if gain is None else rms(ref[...], rest[0][...])

        @pl.when(this)
        def _():
            put(first_ref)

        @pl.when(jnp.logical_not(this))
        def _():
            put(second_ref)

    def spec(which):
        def index(i, place):
            start = (place[0] ^ which) * count
            return (jnp.clip(i - start, 0, count - 1), 0)

        return pl.BlockSpec((size, width), index)

    extra = [] if gain is None else [gain.reshape(1, width)]
    return pl.pallas_call(
        kernel,
        grid_spec=pltpu.PrefetchScalarGridSpec(
            num_scalar_prefetch=1,
            grid=(2 * count,),
            in_specs=[spec(0), spec(1)] + [whole(1, width) for _ in extra],
            out_specs=pl.BlockSpec((size, width), lambda i, place: (i, 0)),
        ),
        out_shape=jax.ShapeDtypeStruct((2 * half, width), bf16),
        cost_estimate=cost(4),
        compiler_params=PARAMS,
    )(place, first, second, *extra)


def normalised_rows(rows, gain):
    count, width = rows.shape
    size = min(count, 256)

    def kernel(in_ref, gain_ref, out_ref, inv_ref):
        wide = in_ref[...].astype(f32)
        inv_rms = lax.rsqrt(jnp.mean(wide * wide, axis=-1, keepdims=True) + EPS)
        out_ref[...] = (wide * inv_rms * gain_ref[...]).astype(bf16)
        inv_ref[...] = jnp.broadcast_to(inv_rms, inv_ref.shape)

    by_rows = lambda w: pl.BlockSpec((size, w), lambda i: (i, 0))
    return pl.pallas_call(
        kernel,
        grid=(count // size,),
        in_specs=[by_rows(width), whole(1, width)],
        out_specs=[by_rows(width), by_rows(LANE)],
        out_shape=[jax.ShapeDtypeStruct(rows.shape, bf16), jax.ShapeDtypeStruct((count, LANE), f32)],
        cost_estimate=cost(4),
        compiler_params=PARAMS,
    )(rows, gain.reshape(1, width))


def unpacked(window, counts, place, *before):
    slots = len(window)
    count = (slots + 1) // 2
    width = window[0].shape[1]
    starts = [sum(counts[:i]) for i in range(len(counts))]

    def kernel(place_ref, *refs):
        ins, outs = refs[:slots], refs[slots + len(before) :]
        wanted = pl.program_id(0) + count - 1 - place_ref[0]
        for slot, ref in enumerate(ins):

            @pl.when(wanted == slot)
            def _(ref=ref):
                for out, start, rows in zip(outs, starts, counts):
                    out[0] = ref[start : start + rows]

    return pl.pallas_call(
        kernel,
        grid_spec=pltpu.PrefetchScalarGridSpec(
            num_scalar_prefetch=1,
            grid=(count,),
            in_specs=[whole(*window[0].shape) for _ in window] + [pl.BlockSpec(memory_space=pl.ANY) for _ in before],
            out_specs=[pl.BlockSpec((1, rows, width), lambda j, place: (j, 0, 0)) for rows in counts],
        ),
        out_shape=[jax.ShapeDtypeStruct((count, rows, width), bf16) for rows in counts],
        cost_estimate=cost(3),
        compiler_params=PARAMS,
    )(place, *window, *before)


def products(lefts, more_lefts, right, more_right, blocks, width):
    n = len(lefts)
    count, inner = lefts[0].shape
    size = min(count, 512)

    def kernel(blocks_ref, *refs):
        a, b, (w, v), outs = refs[:n], refs[n : 2 * n], refs[2 * n : 2 * n + 2], refs[2 * n + 2 :]
        for i in range(n):
            outs[i][...] = (mm_t(a[i][...], w[...]) + mm_t(b[i][...], v[...])).astype(bf16)

    rows = pl.BlockSpec((size, inner), lambda j, i, blocks: (i, 0))
    weights = pl.BlockSpec((width, inner), lambda j, i, blocks: (blocks[j], 0))
    return pl.pallas_call(
        kernel,
        grid_spec=pltpu.PrefetchScalarGridSpec(
            num_scalar_prefetch=1,
            grid=(blocks.shape[0], count // size),
            in_specs=[rows] * (2 * n) + [weights] * 2,
            out_specs=[pl.BlockSpec((size, width), lambda j, i, blocks: (i, j))] * n,
        ),
        out_shape=[jax.ShapeDtypeStruct((count, width * blocks.shape[0]), bf16)] * n,
        cost_estimate=cost(5),
        compiler_params=PARAMS,
    )(blocks, *lefts, *more_lefts, right, more_right)


def interleaved(first, second, depth, part):
    contexts, _, inner = first.shape
    shards = inner // part
    size = 64

    def kernel(a_ref, b_ref, out_ref):
        for which, ref in enumerate((a_ref, b_ref)):
            columns = [
                ref[c, :, s * part : (s + 1) * part].astype(f32) for s in range(shards) for c in range(contexts)
            ]
            out_ref[:, which, :] = jnp.concatenate(columns, axis=1)

    return pl.pallas_call(
        kernel,
        grid=(depth // size,),
        in_specs=[pl.BlockSpec((contexts, size, inner), lambda i: (0, i, 0))] * 2,
        out_specs=pl.BlockSpec((size, 2, contexts * inner), lambda i: (i, 0, 0)),
        out_shape=jax.ShapeDtypeStruct((depth, 2, contexts * inner), f32),
        cost_estimate=cost(5),
        compiler_params=PARAMS,
    )(first, second)


class Rows:
    def __init__(self, seqs, length, arrays, size, reverse=False):
        self.pieces = arrays
        self.size = size
        self.count = length // size
        self.per = self.count // arrays
        self.grid = (seqs, self.count)
        self.reverse = reverse

    def at(self, i):
        return self.count - 1 - i if self.reverse else i

    def spec(self, which, width):
        def index(s, i, place):
            low = (place[0] ^ which) * self.per
            return (s * self.per + jnp.clip(self.at(i) - low, 0, self.per - 1), 0)

        return pl.BlockSpec((self.size, width), index)

    def is_turn(self, which, place_ref):
        return (self.at(pl.program_id(1)) // self.per) == (place_ref[0] ^ which)

    def block(self, width):
        return pl.BlockSpec((1, self.size, width), lambda s, i, place: (s, self.at(i), 0))

    def packed(self, rows):
        return pl.BlockSpec((1, self.size // LANE, rows, LANE), lambda s, i, place: (s, self.at(i), 0, 0))


def convolved(xs, masks_ref, vec_ref, size, taps):
    total = vec_ref[taps : taps + 1]
    for by in range(taps):
        term = xs[8 - by : 8 - by + size] * vec_ref[taps - 1 - by : taps - by]
        total = total + (term * masks_ref[0, :, by : by + 1] if by else term)
    return total


def convolve(normed, proj_x, vec, masks, select_low, select_state, place, taps):
    seqs, length = masks.shape[:2]
    width, inner = proj_x.shape
    size = min(256, length)
    rows = Rows(seqs, length, len(normed), size)
    packed = select_low.shape[1] + select_state.shape[0]

    def kernel(place_ref, *refs):
        ins, (w_ref, vec_ref, masks_ref, low_ref, state_ref, x_ref, u_ref, p_ref, xs) = (
            refs[: len(normed)],
            refs[len(normed) :],
        )
        fresh = pl.program_id(1) == 0

        @pl.when(fresh)
        def _():
            xs[0:8] = jnp.zeros((8, inner), f32)

        @pl.when(jnp.logical_not(fresh))
        def _():
            xs[0:8] = xs[size : size + 8]

        for which, ref in enumerate(ins):

            @pl.when(rows.is_turn(which, place_ref))
            def _(ref=ref):
                x = mm(ref[...], w_ref[...]).astype(bf16)
                x_ref[0] = x
                xs[8 : 8 + size] = x.astype(f32)

        pre = convolved(xs, masks_ref, vec_ref, size, taps)
        u = (pre / (1.0 + jnp.exp(-pre))).astype(bf16)
        u_ref[0] = u
        low = mm(u, low_ref[...])
        state = mm_t(state_ref[...], u)
        for j in range(size // LANE):
            p_ref[0, j, 0:LANE] = low[j * LANE : (j + 1) * LANE]
            p_ref[0, j, LANE:packed] = state[:, j * LANE : (j + 1) * LANE]

    return pl.pallas_call(
        kernel,
        grid_spec=pltpu.PrefetchScalarGridSpec(
            num_scalar_prefetch=1,
            grid=rows.grid,
            in_specs=[rows.spec(i, width) for i in range(len(normed))]
            + [whole(width, inner), whole(8, inner), rows.block(LANE), whole(*select_low.shape), whole(*select_state.shape)],
            out_specs=[rows.block(inner), rows.block(inner), rows.packed(packed)],
            scratch_shapes=[pltpu.VMEM((size + 8, inner), f32)],
        ),
        out_shape=[
            jax.ShapeDtypeStruct((seqs, length, inner), bf16),
            jax.ShapeDtypeStruct((seqs, length, inner), bf16),
            jax.ShapeDtypeStruct((seqs, length // LANE, packed, LANE), f32),
        ],
        cost_estimate=cost(9),
        compiler_params=PARAMS,
    )(place, *normed, proj_x, vec, masks, select_low, select_state)


def gates(normed, grads, proj_z, proj_out, ssm_out, place):
    seqs, length, inner = ssm_out.shape
    width = proj_z.shape[0]
    size = min(256, length)
    rows = Rows(seqs, length, len(normed), size)
    n = len(normed)

    def kernel(place_ref, *refs):
        a_refs, g_refs, (z_ref, o_ref, s_ref), outs = refs[:n], refs[n : 2 * n], refs[2 * n : 2 * n + 3], refs[2 * n + 3 :]
        for which in range(n):

            @pl.when(rows.is_turn(which, place_ref))
            def _(which=which):
                z = mm(a_refs[which][...], z_ref[...]).astype(bf16).astype(f32)
                grad = mm_t(g_refs[which][...], o_ref[...])
                ssm = s_ref[0]
                sigmoid = 1.0 / (1.0 + jnp.exp(-z))
                gate = z * sigmoid
                outs[which][...] = (ssm * gate).astype(bf16)
                outs[n + which][...] = (grad * ssm * sigmoid * (1.0 + z * (1.0 - sigmoid))).astype(bf16)
                outs[2 * n][0] = grad * gate

    total = seqs * length // n
    outs = pl.pallas_call(
        kernel,
        grid_spec=pltpu.PrefetchScalarGridSpec(
            num_scalar_prefetch=1,
            grid=rows.grid,
            in_specs=[rows.spec(i, width) for i in range(n)] * 2
            + [whole(width, inner), whole(inner, width), rows.block(inner)],
            out_specs=[rows.spec(i, inner) for i in range(n)] * 2 + [rows.block(inner)],
        ),
        out_shape=[jax.ShapeDtypeStruct((total, inner), bf16)] * (2 * n) + [jax.ShapeDtypeStruct((seqs, length, inner), f32)],
        cost_estimate=cost(14),
        compiler_params=PARAMS,
    )(place, *normed, *grads, proj_z, proj_out, ssm_out)
    return outs[:n], outs[n : 2 * n], outs[2 * n]


def convolve_back(packed, direct, x_part, vec, masks, select_low, select_state, place, n, taps):
    seqs, length, inner = x_part.shape
    size = min(256, length)
    rows = Rows(seqs, length, n, size, reverse=True)
    states = (packed.shape[2] - LANE) // 2

    def kernel(place_ref, p_ref, d_ref, x_ref, edge_ref, vec_ref, masks_ref, low_ref, state_ref, *rest):
        outs, (sum_ref, tok_ref, xs, ds) = rest[:n], rest[n:]
        fresh = pl.program_id(1) == 0

        @pl.when(jnp.logical_and(fresh, pl.program_id(0) == 0))
        def _():
            sum_ref[...] = jnp.zeros_like(sum_ref)

        @pl.when(fresh)
        def _():
            ds[size : size + 8] = jnp.zeros((8, inner), f32)

        @pl.when(jnp.logical_not(fresh))
        def _():
            ds[size : size + 8] = ds[0:8]

        copy = (iota((LANE, 16), 0) // 8 == iota((LANE, 16), 1)).astype(bf16)
        place_of = (iota((LANE, LANE), 1) // 16) == lax.rem(iota((LANE, LANE), 0), 8)
        by_state = lax.rem(iota((LANE, LANE), 0), 16)
        for j in range(size // LANE):
            at = slice(j * LANE, (j + 1) * LANE)
            tok_ref[0, at, 0:LANE] = p_ref[0, j, 0:LANE].astype(bf16)
            token = jnp.zeros((LANE, LANE), f32)
            for q in range(2):
                part = p_ref[0, j, LANE + q * states : LANE + (q + 1) * states].astype(bf16)
                spread = jnp.where(place_of, mm(copy, part), 0.0).astype(bf16)
                token = token + mm(spread, (by_state + q * states == iota((LANE, LANE), 1)).astype(bf16))
            tok_ref[0, at, LANE : 2 * LANE] = token.astype(bf16)
        xs[0:8] = edge_ref[0, 8:16].astype(f32)
        xs[8 : 8 + size] = x_ref[0].astype(f32)
        pre = convolved(xs, masks_ref, vec_ref, size, taps)
        sigmoid = 1.0 / (1.0 + jnp.exp(-pre))
        grad = mm_t(tok_ref[0, :, 0:LANE], low_ref[...]) + mm_t(tok_ref[0, :, LANE : 2 * LANE], state_ref[...]) + d_ref[0]
        grad = grad * sigmoid * (1.0 + pre * (1.0 - sigmoid))
        ds[0:size] = grad
        total = grad * vec_ref[taps - 1 : taps]
        sum_ref[taps : taps + 1] += jnp.sum(grad, axis=0, keepdims=True)
        sum_ref[taps - 1 : taps] += jnp.sum(grad * xs[8 : 8 + size], axis=0, keepdims=True)
        for by in range(1, taps):
            tap = taps - 1 - by
            total = total + ds[by : by + size] * masks_ref[0, :, taps + by : taps + by + 1] * vec_ref[tap : tap + 1]
            joint = grad * xs[8 - by : 8 - by + size] * masks_ref[0, :, by : by + 1]
            sum_ref[tap : tap + 1] += jnp.sum(joint, axis=0, keepdims=True)
        for which in range(n):

            @pl.when(rows.is_turn(which, place_ref))
            def _(which=which):
                outs[which][...] = total.astype(bf16)

    edge = pl.BlockSpec((1, 16, inner), lambda s, i, place: (s, jnp.maximum(rows.at(i) * (size // 16) - 1, 0), 0))
    outs = pl.pallas_call(
        kernel,
        grid_spec=pltpu.PrefetchScalarGridSpec(
            num_scalar_prefetch=1,
            grid=rows.grid,
            in_specs=[
                rows.packed(packed.shape[2]),
                rows.block(inner),
                rows.block(inner),
                edge,
                whole(8, inner),
                rows.block(LANE),
                whole(inner, LANE),
                whole(inner, LANE),
            ],
            out_specs=[rows.spec(i, inner) for i in range(n)] + [whole(8, inner), rows.block(2 * LANE)],
            scratch_shapes=[pltpu.VMEM((size + 8, inner), f32)] * 2,
        ),
        out_shape=[jax.ShapeDtypeStruct((seqs * length // n, inner), bf16)] * n
        + [jax.ShapeDtypeStruct((8, inner), f32), jax.ShapeDtypeStruct((seqs, length, 2 * LANE), bf16)],
        cost_estimate=cost(10),
        compiler_params=PARAMS,
    )(place, packed, direct, x_part, x_part, vec, masks, select_low, select_state)
    return outs[:n], outs[n], outs[n + 1]


def log_one_plus(v):
    small = v * (1.0 - v * (0.5 - v * (1.0 / 3.0 - v * 0.25)))
    return jnp.where(v < 0.01, small, jnp.log(1.0 + v))


def softplus(v):
    return jnp.maximum(v, 0.0) + log_one_plus(jnp.exp(-jnp.abs(v)))


def sigmoid_of_step(step):
    small = step * (1.0 - step * (0.5 - step * (1.0 / 6.0 - step * (1.0 / 24.0))))
    return jnp.where(step < 0.02, small, 1.0 - jnp.exp(-step))


def hot_rows():
    row, col = iota((LANE, 8 * LANE), 0), iota((LANE, 8 * LANE), 1)
    return ((lax.rem(row, 8) == col // LANE) & (row < 16)).astype(bf16)


def spread(state, hot, wide, s, blocks):
    high = state.astype(bf16).astype(f32)
    rest = state - high
    lane = iota(state.shape, 1)
    parts = []
    for i in range(blocks):
        a = pltpu.roll(high, (LANE - 8 * i) % LANE, 1)
        b = pltpu.roll(rest, (LANE + 8 - 8 * i) % LANE, 1)
        parts.append(jnp.where(lane < 8, a, b).astype(bf16))
    wide[s] = mm(jnp.concatenate(parts, axis=0), hot).reshape(blocks, state.shape[0], 8 * LANE)


def forward_kernel(
    S, G, p_ref, u_ref, masks_ref, proj_ref, vec_ref, rate_ref, hot_ref, y_ref, step_ref, start_ref, h_s, wide, w_s, se_s, su_s
):
    blocks = LANE // 8
    C = G * LANE

    @pl.when(pl.program_id(0) == 0)
    def _():
        h_s[...] = jnp.zeros_like(h_s)

    start_ref[0] = h_s[...]
    for s in range(S):
        step = softplus(mm(p_ref[s, 0, 0:LANE].astype(bf16), proj_ref[...]) + vec_ref[0:1])
        step_ref[s] = step
        u = u_ref[s].astype(f32)
        se_s[s] = jnp.where(masks_ref[s, :, 1:2] > 0.5, step, BREAK).reshape(blocks, 8, C)
        su_s[s] = (step * u).reshape(blocks, 8, C)
        spread(p_ref[s, 0, LANE : LANE + 32], hot_ref[...], wide, s, blocks)
    keys = [(s, g, j) for s in range(S) for g in range(G) for j in range(2)]

    def body(i, carry):
        hs = dict(zip(keys, carry))
        for k in range(8):
            for s in range(S):
                lanes = slice(k * LANE, (k + 1) * LANE)
                b = [wide[s, i, j * 8 : (j + 1) * 8, lanes] for j in range(2)]
                c = [wide[s, i, 16 + j * 8 : 16 + (j + 1) * 8, lanes] for j in range(2)]
                for g in range(G):
                    se, su = row8(se_s, s, i, k, g), row8(su_s, s, i, k, g)
                    prod = []
                    for j in range(2):
                        a = jnp.exp2(se * rate_ref[g, j * 8 : (j + 1) * 8])
                        hs[s, g, j] = a * hs[s, g, j] + su * b[j]
                        prod.append(c[j] * hs[s, g, j])
                    w_s[i, s, k * 16 : (k + 1) * 16, g * LANE : (g + 1) * LANE] = jnp.concatenate(prod, 0).astype(bf16)
        return tuple(hs.values())

    out = lax.fori_loop(0, blocks, body, tuple(h_s[q * 8 : (q + 1) * 8] for q in range(len(keys))))
    pick = (iota((16, 2 * LANE), 0) == iota((16, 2 * LANE), 1) // 16).astype(bf16)
    for s in range(S):
        for i in range(blocks // 2):
            both = jnp.concatenate([w_s[2 * i, s], w_s[2 * i + 1, s]], axis=0)
            y_ref[s, i * 16 : (i + 1) * 16] = mm(pick, both)
        y_ref[s] = y_ref[s] + vec_ref[1:2] * u_ref[s].astype(f32)
    for q in range(len(keys)):
        h_s[q * 8 : (q + 1) * 8] = out[q]


def backward_kernel(
    S, G, p_ref, u_ref, step_ref, ds_ref, masks_ref, proj_ref, vec_ref, rate_ref, rate2_ref, hot_ref, start_ref,
    dsp_ref, du_ref, p2_ref, dlog_ref, sum_ref, ag_s, h_s, wide, se_s, su_s, s_s, q_s, d_s, r_s
):
    blocks = LANE // 8
    C = G * LANE
    keys = [(s, g, j) for s in range(S) for g in range(G) for j in range(2)]

    @pl.when(pl.program_id(0) == 0)
    def _():
        ag_s[...] = jnp.zeros_like(ag_s)
        dlog_ref[...] = jnp.zeros_like(dlog_ref)
        sum_ref[...] = jnp.zeros_like(sum_ref)

    for s in range(S):
        step = step_ref[s]
        u = u_ref[s].astype(f32)
        se_s[s] = jnp.where(masks_ref[s, :, 1:2] > 0.5, step, BREAK).reshape(blocks, 8, C)
        su_s[s] = (step * u).reshape(blocks, 8, C)
        d_s[s] = ds_ref[s].reshape(blocks, 8, C)
        spread(p_ref[s, 0, LANE : LANE + 32], hot_ref[...], wide, s, blocks)

    def again(i, carry):
        hs = dict(zip(keys, carry))
        for k in range(8):
            for s in range(S):
                b = [wide[s, i, j * 8 : (j + 1) * 8, k * LANE : (k + 1) * LANE] for j in range(2)]
                for g in range(G):
                    se, su = row8(se_s, s, i, k, g), row8(su_s, s, i, k, g)
                    h_s[i * 8 + k, s * G + g] = jnp.concatenate([hs[s, g, 0], hs[s, g, 1]], 0).astype(bf16)
                    for j in range(2):
                        a = jnp.exp2(se * rate_ref[g, j * 8 : (j + 1) * 8])
                        hs[s, g, j] = a * hs[s, g, j] + su * b[j]
        return tuple(hs.values())

    out = lax.fori_loop(0, blocks, again, tuple(start_ref[0, q * 8 : (q + 1) * 8] for q in range(len(keys))))
    for s in range(S):
        for g in range(G):
            q = (s * G + g) * 2
            h_s[LANE, s * G + g] = jnp.concatenate([out[q], out[q + 1]], 0).astype(bf16)

    def two(v):
        return jnp.concatenate([v, v], 0).astype(bf16)

    pick = (iota((16, 2 * LANE), 0) == iota((16, 2 * LANE), 1) // 16).astype(bf16)
    fold = (lax.rem(iota((16, 2 * LANE), 1), 16) == iota((16, 2 * LANE), 0)).astype(bf16)
    one = jnp.ones((16, LANE), bf16)
    lane, row = iota((8, LANE), 1), iota((8, LANE), 0)

    def across_rows(product):
        found = product[0:8]
        for v in range(1, 16):
            found = jnp.where(lane >= 8 * v, product[8 * v : 8 * v + 8], found)
        found = jnp.sum(jnp.where(lax.rem(lane, 8) == row, found, 0.0), axis=0, keepdims=True)
        return jnp.broadcast_to(found, (8, LANE))

    def body(r, carry):
        low = blocks - 2 - 2 * r
        ags = dict(zip(keys, carry))
        tq, ts, tl, tb, tc = {}, {}, {}, {}, {}
        for t in reversed(range(16)):
            i, k = low + t // 8, t % 8
            for s in range(S):
                lanes = slice(k * LANE, (k + 1) * LANE)
                b16 = wide[s, i, 0:16, lanes].astype(bf16)
                c = [wide[s, i, 16 + j * 8 : 16 + (j + 1) * 8, lanes] for j in range(2)]
                for g in range(G):
                    se, su, ds = row8(se_s, s, i, k, g), row8(su_s, s, i, k, g), row8(d_s, s, i, k, g)
                    a = [jnp.exp2(se * rate_ref[g, j * 8 : (j + 1) * 8]) for j in range(2)]
                    gr = [c[j] * ds + ags[s, g, j] for j in range(2)]
                    for j in range(2):
                        ags[s, g, j] = a[j] * gr[j]
                    gb = jnp.concatenate(gr, 0).astype(bf16)
                    ab = jnp.concatenate(a, 0).astype(bf16)
                    gq = gb * (ab * h_s[i * 8 + k, s * G + g])
                    tq[s, g, t] = gq * rate2_ref[g]
                    tl[s, g, t] = gq * two(se)
                    ts[s, g, t] = gb * b16
                    tb[s, g, t] = gb * two(su)
                    tc[s, g, t] = h_s[i * 8 + k + 1, s * G + g] * two(ds)

        def mat(m, s):
            return jnp.concatenate([jnp.concatenate([m[s, g, t] for t in range(16)], 0) for g in range(G)], 1)

        def msum(m, s):
            return jnp.concatenate([sum(m[s, g, t] for g in range(G)) for t in range(16)], 0)

        for s in range(S):
            q = mm(pick, mat(tq, s))
            v = mm(pick, mat(ts, s))
            for h in range(2):
                q_s[s, low + h] = q[h * 8 : (h + 1) * 8]
                s_s[s, low + h] = v[h * 8 : (h + 1) * 8]
            dlog_ref[...] += mm(fold, mat(tl, s))
            for kind, m in enumerate((tb, tc)):
                found = mm_t(one, msum(m, s))[0:8]
                for h in range(2):
                    r_s[s, kind, low + h] = found[:, h * LANE : (h + 1) * LANE]
        return tuple(ags.values())

    ags = lax.fori_loop(0, blocks // 2, body, tuple(ag_s[q * 8 : (q + 1) * 8] for q in range(len(keys))))
    for q in range(len(keys)):
        ag_s[q * 8 : (q + 1) * 8] = ags[q]
    for s in range(S):
        step = step_ref[s]
        u = u_ref[s].astype(f32)
        ds = ds_ref[s]
        sums = s_s[s].reshape(LANE, C)
        dsp = ((q_s[s].reshape(LANE, C) + u * sums) * sigmoid_of_step(step)).astype(bf16)
        dsp_ref[s] = dsp
        du_ref[s] = step * sums + ds * vec_ref[1:2]
        p2_ref[s, 0, 0:LANE] = mm_t(dsp, proj_ref[...])
        for kind in range(2):
            for i in range(blocks):
                p2_ref[s, 0, LANE + 16 * kind + i : LANE + 16 * kind + i + 1] = r_s[s, kind, i, 0:1]
        sum_ref[0:1] += jnp.sum(dsp.astype(f32), axis=0, keepdims=True)
        sum_ref[1:2] += jnp.sum(ds * u, axis=0, keepdims=True)


def scan_specs(S, T, C, reverse):
    at = (lambda i: T // LANE - 1 - i) if reverse else (lambda i: i)
    return dict(
        packed=pl.BlockSpec((S, 1, LANE + 32, LANE), lambda i: (0, at(i), 0, 0)),
        block=pl.BlockSpec((S, LANE, C), lambda i: (0, at(i), 0)),
        masks=pl.BlockSpec((S, LANE, LANE), lambda i: (0, at(i), 0)),
        start=pl.BlockSpec((1, S * C // LANE * 16, LANE), lambda i: (at(i), 0, 0)),
    )


def scan_forward(packed, u, masks, proj_step, vec, rate2e, hot):
    S, T, C = u.shape
    G = C // LANE
    sp = scan_specs(S, T, C, False)
    by_token = pltpu.VMEM((S, LANE // 8, 8, C), f32)
    return pl.pallas_call(
        functools.partial(forward_kernel, S, G),
        grid=(T // LANE,),
        in_specs=[
            sp["packed"], sp["block"], sp["masks"], whole(LANE, C), whole(8, C), whole(G, 16, LANE), whole(LANE, 8 * LANE)
        ],
        out_specs=[sp["block"], sp["block"], sp["start"]],
        out_shape=[jax.ShapeDtypeStruct((S, T, C), f32)] * 2 + [jax.ShapeDtypeStruct((T // LANE, S * G * 16, LANE), f32)],
        scratch_shapes=[
            pltpu.VMEM((S * G * 16, LANE), f32),
            pltpu.VMEM((S, LANE // 8, 32, 8 * LANE), f32),
            pltpu.VMEM((LANE // 8, S, LANE, C), bf16),
            by_token,
            by_token,
        ],
        cost_estimate=cost(30),
        compiler_params=PARAMS,
    )(packed, u, masks, proj_step, vec, rate2e, hot)


def scan_backward(packed, u, step, ds, masks, proj_step, vec, rate2e, rate, hot, starts):
    S, T, C = u.shape
    G = C // LANE
    sp = scan_specs(S, T, C, True)
    by_token = pltpu.VMEM((S, LANE // 8, 8, C), f32)
    return pl.pallas_call(
        functools.partial(backward_kernel, S, G),
        grid=(T // LANE,),
        in_specs=[
            sp["packed"], sp["block"], sp["block"], sp["block"], sp["masks"], whole(LANE, C), whole(8, C),
            whole(G, 16, LANE), whole(G, 16, LANE), whole(LANE, 8 * LANE), sp["start"]
        ],
        out_specs=[sp["block"], sp["block"], sp["packed"], whole(16, C), whole(8, C)],
        out_shape=[
            jax.ShapeDtypeStruct((S, T, C), bf16),
            jax.ShapeDtypeStruct((S, T, C), f32),
            jax.ShapeDtypeStruct((S, T // LANE, LANE + 32, LANE), f32),
            jax.ShapeDtypeStruct((16, C), f32),
            jax.ShapeDtypeStruct((8, C), f32),
        ],
        scratch_shapes=[
            pltpu.VMEM((S * G * 16, LANE), f32),
            pltpu.VMEM((LANE + 1, S * G, 16, LANE), bf16),
            pltpu.VMEM((S, LANE // 8, 32, 8 * LANE), f32),
        ]
        + [by_token] * 5
        + [pltpu.VMEM((S, 2, LANE // 8, 8, LANE), f32)],
        cost_estimate=cost(85),
        compiler_params=PARAMS,
    )(packed, u, step, ds, masks, proj_step, vec, rate2e, rate.astype(bf16), hot, starts)


def after(*arrays):
    def kernel(*refs):
        refs[-1][0] = 0

    return pl.pallas_call(
        kernel,
        in_specs=[pl.BlockSpec(memory_space=pl.ANY) for _ in arrays],
        out_specs=pl.BlockSpec(memory_space=pltpu.SMEM),
        out_shape=jax.ShapeDtypeStruct((1,), jnp.int32),
    )(*arrays)[0]


def line_gather(array, axis):
    count = lax.axis_size(axis)
    right, left = array, array
    window = [array]
    for step in range(1, count):
        right = lax.ppermute(right, axis, [(i, i + 1) for i in range(step - 1, count - 1)])
        left = lax.ppermute(left, axis, [(i, i - 1) for i in range(1, count - step + 1)])
        window = [right] + window + [left]
    return window


def line_gather_at_once(array, axis):
    count = lax.axis_size(axis)
    return lax.all_to_all(jnp.broadcast_to(array[None], (count,) + array.shape), axis, 0, 0)


def line_scatter(blocks, axis):
    return jnp.sum(lax.all_to_all(blocks, axis, 0, 0).astype(f32), axis=0)


class Paired:
    def __init__(self):
        self.context = lax.axis_index("context")
        self.tensor = lax.axis_index("tensor")
        self.core = self.tensor % 2
        self.place = self.context[None]

    def across(self, array):
        return lax.ppermute(array, "context", [(0, 1), (1, 0)])

    def near(self, array):
        return lax.ppermute(array, "tensor", [(0, 1), (1, 0), (2, 3), (3, 2)])

    def far(self, array):
        return lax.ppermute(array, "tensor", [(0, 2), (2, 0), (1, 3), (3, 1)])

    def pieces(self, array, begin):
        half = array.shape[0] // 2
        mine = lax.dynamic_slice_in_dim(array, (self.core + begin) * half, half, 0)
        return self.across(mine), mine

    def pieces_done(self, array, block):
        return [array, joined_halves(block, self.near(block), self.core[None])]

    def normed(self, array, block, gain):
        own, inv_rms = normalised_rows(array, gain)
        return [own, joined_halves(block, self.near(block), self.core[None], gain)], inv_rms

    def total(self, array, begin):
        half = array.shape[0] // 2
        mine = lax.dynamic_slice_in_dim(array, self.core * half, half, 0)
        other = lax.dynamic_slice_in_dim(array, (1 - self.core + begin) * half, half, 0).astype(bf16)
        mine = mine + self.near(other).astype(f32)
        first, second = mine[: half // 2], mine[half // 2 :]
        first = first + self.far(first.astype(bf16)).astype(f32)
        second = second + self.across(second.astype(bf16)).astype(f32)
        first = first + self.across(first.astype(bf16)).astype(f32)
        second = second + self.far(second.astype(bf16)).astype(f32)
        mine = jnp.concatenate([first, second], axis=0)
        other = self.near(mine.astype(bf16)).astype(f32)
        zero = self.core == 0
        return jnp.concatenate([jnp.where(zero, mine, other), jnp.where(zero, other, mine)])

    def share_begin(self, product):
        keep = product((self.tensor, self.tensor ^ 2))
        give = product((self.tensor ^ 1, self.tensor ^ 3))
        return [(k.astype(f32) + self.near(g).astype(f32)) for k, g in zip(keep, give)]

    def share_middle(self, sums):
        own, other = sums
        rows, width = own.shape
        half, width = rows // 2, width // 2
        far = self.far(jnp.stack([own[:half, width:], other[:half, width:]]).astype(bf16))
        across = self.across(other[half:].astype(bf16))
        first = own[:half, :width] + far[0].astype(f32)
        give = other[:half, :width] + far[1].astype(f32)
        second = own[half:] + across.astype(f32)
        return first, give, second

    def share_end(self, sums):
        first, give, second = sums
        width = first.shape[1]
        first = first + self.across(give.astype(bf16)).astype(f32)
        second = second[:, :width] + self.far(second[:, width:].astype(bf16)).astype(f32)
        return jnp.concatenate([first, second], axis=0)

    def row_total(self, array):
        array = array + self.near(array)
        return array + self.far(array)

    def vector_total(self, array):
        return self.row_total(array + self.across(array))

    def both(self, array):
        other = self.across(array)
        zero = self.context == 0
        return jnp.stack([jnp.where(zero, array, other), jnp.where(zero, other, array)])


class General:
    def __init__(self, seqs):
        self.seqs = seqs
        self.place = jnp.zeros((1,), jnp.int32)

    def pieces(self, array, begin):
        return lax.all_gather(array, "context", tiled=True), array

    def pieces_done(self, array, block):
        return [self.in_order([block], self.seqs).reshape(block.shape)]

    def normed(self, array, block, gain):
        inv_rms = normalised_rows(array, gain)[1]
        return [normalised_rows(self.pieces_done(array, block)[0], gain)[0]], inv_rms

    def in_order(self, arrays, seqs):
        array = arrays[0].reshape(lax.axis_size("context"), seqs, -1, arrays[0].shape[-1])
        return array.swapaxes(0, 1).reshape(seqs, -1, array.shape[-1])

    def total(self, array, begin):
        return lax.psum(array, ("context", "tensor"))

    def share_begin(self, product):
        return [product((block,))[0].astype(f32) for block in range(lax.axis_size("tensor"))]

    def share_middle(self, sums):
        return sums

    def share_end(self, sums):
        parts = jnp.concatenate(sums, axis=-1)
        shape = parts.shape
        parts = parts.reshape(self.seqs, lax.axis_size("context"), -1, shape[-1]).swapaxes(0, 1).reshape(shape)
        parts = lax.psum_scatter(parts, "context", scatter_dimension=0, tiled=True)
        return lax.psum_scatter(parts, "tensor", scatter_dimension=1, tiled=True)

    def row_total(self, array):
        return lax.psum(array, "tensor")

    def vector_total(self, array):
        return lax.psum(array, ("context", "tensor"))

    def both(self, array):
        return lax.all_gather(array, "context")


def dot(a, b, out=f32):
    return jnp.dot(a, b, preferred_element_type=f32).astype(out)


def dot_t(a, b, out=f32):
    return lax.dot_general(a, b, (((1,), (1,)), ((), ())), preferred_element_type=f32).astype(out)


def t_dot(a, b, out=f32):
    return lax.dot_general(a, b, (((0,), (0,)), ((), ())), preferred_element_type=f32).astype(out)


def on_device(
    block_input,
    output_grad,
    doc_lengths,
    norm_gain,
    input_proj,
    conv_weight,
    conv_bias,
    select_proj,
    step_proj,
    step_bias,
    decay_log,
    skip_weight,
    output_proj,
):
    seqs, piece, model_width = block_input.shape
    shards, contexts, tensors = (lax.axis_size(axis) for axis in ("shards", "context", "tensor"))
    shard, context, tensor = (lax.axis_index(axis) for axis in ("shards", "context", "tensor"))
    moves = Paired() if (contexts, tensors) == (2, 4) else General(seqs)
    length = piece * contexts
    tokens = seqs * length
    depth = input_proj.shape[0]
    part = conv_weight.shape[0] // contexts
    inner = part * shards
    states = decay_log.shape[1]
    rank = step_proj.shape[0] * shards
    selected = select_proj.shape[1]
    taps = conv_weight.shape[1]
    share_width = model_width // tensors

    def mine(array):
        return lax.dynamic_slice_in_dim(array, context * part, part, 0)

    def my_columns(array, begin):
        blocks = [
            lax.dynamic_slice_in_dim(array, (block * contexts + context + begin) * part, part, array.ndim - 1)
            for block in range(shards)
        ]
        return jnp.concatenate(blocks, axis=-1)

    rows_flat = block_input.reshape(seqs * piece, model_width)
    row_block, row_slice = moves.pieces(rows_flat, 0)
    in_x = my_columns(input_proj[:, 0], after(row_slice))
    bounds = jnp.cumsum(doc_lengths, axis=-1)[:, :2, None, None]
    position, lane = (lax.broadcasted_iota(jnp.int32, (1, length, LANE), axis) for axis in (1, 2))
    other = jnp.where(lane < taps, position - lane, position + lane - taps)

    def document(at):
        return (at >= bounds[:, 0]).astype(jnp.int32) + (at >= bounds[:, 1]).astype(jnp.int32)

    masks = (document(position) == document(other)) & (other >= 0) & (other < length)
    masks = masks.astype(f32)

    vectors = jnp.concatenate(
        [
            mine(select_proj),
            mine(conv_weight),
            mine(decay_log),
            mine(conv_bias)[:, None],
            mine(step_bias)[:, None],
            mine(skip_weight)[:, None],
        ],
        axis=1,
    )
    vectors = jnp.pad(vectors, ((0, 0), (0, 2 * LANE - vectors.shape[1])))
    flat = [in_x, my_columns(step_proj, 0), vectors.reshape(-1, inner), norm_gain.reshape(-1, inner)]
    flat = [jnp.pad(f, ((0, -f.shape[0] % 16), (0, 0))) for f in flat]
    window = line_gather(jnp.concatenate(flat, axis=0), "shards")
    proj_x, proj_step, vectors, gain = unpacked(window, [f.shape[0] for f in flat], shard[None], masks)
    gain = gain[:, : norm_gain.shape[0] // inner].reshape(model_width).astype(f32)
    normed, inv_rms = moves.normed(rows_flat, row_block, gain)
    proj_x = proj_x.reshape(model_width, inner)
    proj_step = proj_step[:, : step_proj.shape[0]].reshape(rank, inner)
    vectors = vectors[:, : 2 * LANE * part // inner].reshape(inner, 2 * LANE)
    proj_select = vectors[:, :selected]
    rest = vectors[:, selected:].astype(f32)
    decay_rate = -jnp.exp(rest[:, taps : taps + states])
    at = taps + states
    conv_vec = jnp.concatenate([rest[:, :taps].T, rest[:, at][None], jnp.zeros((7 - taps, inner), f32)], axis=0)
    scan_vec = jnp.concatenate([rest[:, at + 1 : at + 3].T, jnp.zeros((6, inner), f32)], axis=0)
    select_low, select_state = proj_select[:, :rank], proj_select[:, rank:]

    grad_flat = output_grad.reshape(seqs * piece, model_width)

    in_z = my_columns(input_proj[:, 1], after(window[len(window) // 2 - 1]))
    out_own = mine(output_proj)
    out_own = [out_own[:, i * inner : (i + 1) * inner] for i in range(model_width // inner)]
    others = jnp.concatenate([in_z] + out_own + [jnp.zeros((16, inner), bf16)], axis=0)
    others = lax.dynamic_slice_in_dim(others, after(proj_x) * 16, others.shape[0] - 16, 0)
    others = line_gather_at_once(others, "shards")

    x_part, values, projected = convolve(
        normed, proj_x, conv_vec, masks, select_low, select_state.T, moves.place, taps
    )

    def total(packed, begin):
        return moves.total(packed.reshape(-1, LANE), begin).reshape(packed.shape)

    projected = total(projected, 0)
    grad_block = moves.pieces(grad_flat, after(row_block))[0]

    hot = hot_rows()

    def by_group(array, begin=0.0):
        return (array.T + begin).reshape(states, inner // LANE, LANE).swapaxes(0, 1)

    ssm_out, step, starts = scan_forward(
        projected, values, masks, proj_step, scan_vec, by_group(decay_rate * LOG2E), hot
    )

    proj_z = others[:, :depth].reshape(model_width, inner)
    proj_out = [others[:, depth + i * part : depth + (i + 1) * part] for i in range(model_width // inner)]
    proj_out = jnp.concatenate(proj_out, axis=-1).reshape(inner, model_width)
    grad_all = moves.pieces_done(grad_flat, grad_block)
    gated, grad_z, grad_ssm = gates(normed, grad_all, proj_z, proj_out, ssm_out, moves.place)

    def weight_grad(lefts, rights):
        return sum(t_dot(a, b) for a, b in zip(lefts, rights)).astype(bf16)

    early = lax.all_to_all(weight_grad(normed, grad_z).reshape(shards, depth, inner), "shards", 0, 0)
    middle = lax.all_to_all(weight_grad(gated, grad_all).reshape(shards, part, model_width), "shards", 0, 0)
    def chosen(weights, blocks, axis, begin=0):
        return jnp.concatenate(
            [lax.dynamic_slice_in_dim(weights, (b + begin) * share_width, share_width, axis) for b in blocks], axis
        )

    out_sums = moves.share_begin(lambda blocks: [dot(g, chosen(proj_out, blocks, 1), bf16) for g in gated])
    out_sums_2 = moves.share_middle(out_sums)
    out_share = moves.share_end(out_sums_2)
    own_columns = tensor * share_width
    input_share = lax.dynamic_slice_in_dim(block_input, own_columns, share_width, 2).astype(f32)
    block_output = (input_share + out_share.reshape(input_share.shape)).astype(bf16)

    grad_step_pre, grad_direct, partial_grad, grad_decay, scan_sums = scan_backward(
        projected,
        values,
        step,
        grad_ssm,
        masks,
        proj_step,
        scan_vec,
        by_group(decay_rate * LOG2E),
        by_group(decay_rate, after(*out_sums).astype(f32)),
        hot,
        starts,
    )
    grad_decay_log = grad_decay.T * decay_rate
    step_low = projected[:, :, :rank].reshape(tokens, rank).astype(bf16)
    grad_step_proj = t_dot(step_low, grad_step_pre.reshape(tokens, inner))
    pulled = after(early, partial_grad, *out_sums_2)
    grad_in_z = jnp.sum(early.astype(f32), axis=0) + pulled.astype(f32)
    z_pair = moves.both(grad_in_z.astype(bf16))
    partial_grad = total(partial_grad, pulled)

    grad_x, conv_sums, grad_selected = convolve_back(
        partial_grad,
        grad_direct,
        x_part,
        conv_vec + after(block_output, partial_grad).astype(f32),
        masks,
        select_low,
        jnp.pad(select_state, ((0, 0), (0, LANE - select_state.shape[1]))),
        moves.place,
        len(normed),
        taps,
    )
    grad_select = t_dot(values.reshape(tokens, inner), grad_selected.reshape(tokens, -1))[:, :selected]

    small = jnp.concatenate(
        [
            grad_select,
            conv_sums[:taps].T,
            grad_decay_log,
            conv_sums[taps][:, None],
            scan_sums[:2].T,
        ],
        axis=1,
    ).astype(bf16)
    sent = after(middle, grad_x[0])
    small = small + sent.astype(bf16)
    out_pair = moves.both((jnp.sum(middle.astype(f32), axis=0) + sent.astype(f32)).astype(bf16))
    small = jnp.pad(small, ((0, 0), (0, 2 * LANE - small.shape[1])))
    late_local = jnp.concatenate(
        [
            weight_grad(normed, grad_x).reshape(shards, depth, inner),
            grad_step_proj.astype(bf16).reshape(shards, -1, inner),
            small.reshape(shards, -1, inner),
        ],
        axis=1,
    )
    begin = after(late_local, z_pair)

    def normed_part(blocks):
        blocks = jnp.stack([jnp.asarray(b, jnp.int32) + begin for b in blocks])
        return products(grad_x, grad_z, proj_x, proj_z, blocks, share_width)

    grad_normed = moves.share_end(moves.share_middle(moves.share_begin(normed_part))).reshape(seqs, piece, share_width)
    inv_rms = inv_rms[:, :1].reshape(seqs, piece, 1)
    unit_share = input_share * inv_rms
    weighted = grad_normed * lax.dynamic_slice_in_dim(gain, own_columns, share_width, 0)
    row_dots = moves.row_total(jnp.sum(unit_share * weighted, axis=-1))[:, :, None]
    grad_share = lax.dynamic_slice_in_dim(output_grad, own_columns, share_width, 2).astype(f32)
    input_grad = grad_share + inv_rms * (weighted - unit_share * (row_dots / model_width))

    late = line_scatter(late_local, "shards") + after(grad_normed, z_pair, out_pair).astype(f32)
    grad_in_x = late[:depth]
    gain_part = jnp.sum(in_x.astype(f32) * grad_in_x, axis=1) + jnp.sum(in_z.astype(f32) * grad_in_z, axis=1)
    grad_gain = moves.vector_total(gain_part) / norm_gain.astype(f32)

    def columns_of(pair):
        pair = pair.astype(f32).reshape(pair.shape[:-1] + (shards, part))
        return jnp.moveaxis(pair, 0, -2).reshape(pair.shape[1], -1)

    late = moves.both(late.astype(bf16))
    grad_in = interleaved(late, z_pair, depth, part)
    grad_step_proj = columns_of(late[:, depth : depth + step_proj.shape[0]])
    small = late[:, depth + step_proj.shape[0] :].reshape(contexts * part, 2 * LANE).astype(f32)
    grad_out_proj = out_pair.reshape(contexts * part, model_width).astype(f32)
    at = selected + taps + states
    return (
        block_output,
        input_grad,
        grad_gain,
        grad_in,
        small[:, selected : selected + taps],
        small[:, at],
        small[:, :selected],
        grad_step_proj,
        small[:, at + 1],
        small[:, selected + taps : at],
        small[:, at + 2],
        grad_out_proj,
    )


def solution(mesh):
    placed = (
        P("shards", "context", None),
        P("shards", "context", None),
        P("shards", None),
        P("shards"),
        P("shards", None, "tensor"),
        P(("tensor", "shards"), None),
        P(("tensor", "shards")),
        P(("tensor", "shards"), None),
        P("shards", "tensor"),
        P(("tensor", "shards")),
        P(("tensor", "shards"), None),
        P(("tensor", "shards")),
        P(("tensor", "shards"), None),
    )
    return jax.shard_map(
        on_device,
        mesh=mesh,
        in_specs=placed,
        out_specs=(
            P("shards", "context", "tensor"),
            P("shards", "context", "tensor"),
            P("shards"),
            P("shards", None, "tensor"),
            P(("tensor", "shards"), None),
            P(("tensor", "shards")),
            P(("tensor", "shards"), None),
            P("shards", "tensor"),
            P(("tensor", "shards")),
            P(("tensor", "shards"), None),
            P(("tensor", "shards")),
            P(("tensor", "shards"), None),
        ),
        check_vma=False,
    )
```

```python
import functools

import jax
import jax.numpy as jnp
from jax import lax
from jax.experimental import pallas as pl
from jax.experimental.pallas import tpu as pltpu
from jax.sharding import PartitionSpec as P

EPS = 1e-05
LANE = 128
LOG2E = 1.4426950408889634
BREAK = 1e6
f32 = jnp.float32
bf16 = jnp.bfloat16


def row8(ref, s, i, k, g):
    return jnp.broadcast_to(ref[s, i, k : k + 1, g * LANE : (g + 1) * LANE], (8, LANE))


def mm(a, b):
    return jnp.dot(a, b, preferred_element_type=f32)


def mm_t(a, b):
    return lax.dot_general(a, b, (((1,), (1,)), ((), ())), preferred_element_type=f32)


def iota(shape, axis):
    return lax.broadcasted_iota(jnp.int32, shape, axis)


def cost(us):
    return pl.CostEstimate(flops=int(us * 1.15e8), bytes_accessed=int(us * 3.6e5), transcendentals=0)


PARAMS = pltpu.CompilerParams(vmem_limit_bytes=58 << 20)


def whole(*shape):
    return pl.BlockSpec(shape, lambda *_: (0,) * len(shape))


def joined_halves(first, second, place):
    half, width = first.shape
    size = min(half, 128)
    count = half // size

    def kernel(place_ref, first_ref, second_ref, out_ref):
        this = (pl.program_id(0) // count) == place_ref[0]

        def put(ref):
            out_ref[...] = ref[...]

        @pl.when(this)
        def _():
            put(first_ref)

        @pl.when(jnp.logical_not(this))
        def _():
            put(second_ref)

    def spec(which):
        def index(i, place):
            start = (place[0] ^ which) * count
            return (jnp.clip(i - start, 0, count - 1), 0)

        return pl.BlockSpec((size, width), index)

    return pl.pallas_call(
        kernel,
        grid_spec=pltpu.PrefetchScalarGridSpec(
            num_scalar_prefetch=1,
            grid=(2 * count,),
            in_specs=[spec(0), spec(1)],
            out_specs=pl.BlockSpec((size, width), lambda i, place: (i, 0)),
        ),
        out_shape=jax.ShapeDtypeStruct((2 * half, width), bf16),
        cost_estimate=cost(4),
        compiler_params=PARAMS,
    )(place, first, second)


def normalised_rows(blocks, place, gain):
    count, width = blocks[0].shape
    size = min(count, 256)
    per = count // size
    half = per // 2
    n = 1 if len(blocks) == 1 else 2

    def kernel(place_ref, *refs):
        ins, (gain_ref, out_ref, inv_ref) = refs[: len(blocks)], refs[len(blocks) :]
        i = pl.program_id(0)

        def inverse(ref):
            wide = ref[...].astype(f32)
            inv_rms = lax.rsqrt(jnp.mean(wide * wide, axis=-1, keepdims=True) + EPS)
            out_ref[0] = (wide * inv_rms * gain_ref[...]).astype(bf16)
            return inv_rms

        @pl.when(i < per)
        def _():
            inv_ref[...] = jnp.broadcast_to(inverse(ins[0]), inv_ref.shape)

        for which, ref in enumerate(ins[1:]):
            start = per + (place_ref[0] ^ which) * half

            @pl.when((i >= start) & (i < start + half))
            def _(ref=ref):
                inverse(ref)

    def spec(which):
        def index(i, place):
            if which == 0:
                return (jnp.minimum(i, per - 1), 0)
            return (jnp.clip(i - per - (place[0] ^ (which - 1)) * half, 0, half - 1), 0)

        return pl.BlockSpec((size, width), index)

    return pl.pallas_call(
        kernel,
        grid_spec=pltpu.PrefetchScalarGridSpec(
            num_scalar_prefetch=1,
            grid=(n * per,),
            in_specs=[spec(i) for i in range(len(blocks))] + [whole(1, width)],
            out_specs=[
                pl.BlockSpec((1, size, width), lambda i, place: (i // per, lax.rem(i, per), 0)),
                pl.BlockSpec((size, LANE), lambda i, place: (jnp.minimum(i, per - 1), 0)),
            ],
        ),
        out_shape=[jax.ShapeDtypeStruct((n, count, width), bf16), jax.ShapeDtypeStruct((count, LANE), f32)],
        cost_estimate=cost(8),
        compiler_params=PARAMS,
    )(place, *blocks, gain.reshape(1, width))


def unpacked(window, counts, place, *before):
    slots = len(window)
    count = (slots + 1) // 2
    width = window[0].shape[1]
    starts = [sum(counts[:i]) for i in range(len(counts))]

    def kernel(place_ref, *refs):
        ins, outs = refs[:slots], refs[slots + len(before) :]
        wanted = pl.program_id(0) + count - 1 - place_ref[0]
        for slot, ref in enumerate(ins):

            @pl.when(wanted == slot)
            def _(ref=ref):
                for out, start, rows in zip(outs, starts, counts):
                    out[0] = ref[start : start + rows]

    return pl.pallas_call(
        kernel,
        grid_spec=pltpu.PrefetchScalarGridSpec(
            num_scalar_prefetch=1,
            grid=(count,),
            in_specs=[whole(*window[0].shape) for _ in window] + [pl.BlockSpec(memory_space=pl.ANY) for _ in before],
            out_specs=[pl.BlockSpec((1, rows, width), lambda j, place: (j, 0, 0)) for rows in counts],
        ),
        out_shape=[jax.ShapeDtypeStruct((count, rows, width), bf16) for rows in counts],
        cost_estimate=cost(3),
        compiler_params=PARAMS,
    )(place, *window, *before)


def products(lefts, more_lefts, right, more_right, blocks, width):
    n, count, inner = lefts.shape
    size = min(count, 512)

    def kernel(blocks_ref, *refs):
        a, b, (w, v), outs = refs[:n], refs[n : 2 * n], refs[2 * n : 2 * n + 2], refs[2 * n + 2 :]
        for i in range(n):
            outs[i][...] = (mm_t(a[i][0], w[...]) + mm_t(b[i][0], v[...])).astype(bf16)

    rows = [pl.BlockSpec((1, size, inner), lambda j, i, blocks, which=which: (which, i, 0)) for which in range(n)]
    weights = pl.BlockSpec((width, inner), lambda j, i, blocks: (blocks[j], 0))
    return pl.pallas_call(
        kernel,
        grid_spec=pltpu.PrefetchScalarGridSpec(
            num_scalar_prefetch=1,
            grid=(blocks.shape[0], count // size),
            in_specs=rows * 2 + [weights] * 2,
            out_specs=[pl.BlockSpec((size, width), lambda j, i, blocks: (i, j))] * n,
        ),
        out_shape=[jax.ShapeDtypeStruct((count, width * blocks.shape[0]), bf16)] * n,
        cost_estimate=cost(5),
        compiler_params=PARAMS,
    )(blocks, *[lefts] * n, *[more_lefts] * n, right, more_right)


def interleaved(first, second, depth, part):
    contexts, _, inner = first.shape
    shards = inner // part
    size = 64

    def kernel(a_ref, b_ref, out_ref):
        for which, ref in enumerate((a_ref, b_ref)):
            columns = [
                ref[c, :, s * part : (s + 1) * part].astype(f32) for s in range(shards) for c in range(contexts)
            ]
            out_ref[:, which, :] = jnp.concatenate(columns, axis=1)

    return pl.pallas_call(
        kernel,
        grid=(depth // size,),
        in_specs=[pl.BlockSpec((contexts, size, inner), lambda i: (0, i, 0))] * 2,
        out_specs=pl.BlockSpec((size, 2, contexts * inner), lambda i: (i, 0, 0)),
        out_shape=jax.ShapeDtypeStruct((depth, 2, contexts * inner), f32),
        cost_estimate=cost(5),
        compiler_params=PARAMS,
    )(first, second)


class Rows:
    def __init__(self, seqs, length, arrays, size, reverse=False):
        self.pieces = arrays
        self.size = size
        self.count = length // size
        self.per = self.count // arrays
        self.grid = (seqs, self.count)
        self.reverse = reverse

    def at(self, i):
        return self.count - 1 - i if self.reverse else i

    def spec(self, which, width):
        def index(s, i, place):
            low = (place[0] ^ which) * self.per
            return (s * self.per + jnp.clip(self.at(i) - low, 0, self.per - 1), 0)

        return pl.BlockSpec((self.size, width), index)

    def stacked(self, width):
        def index(s, i, place):
            turn = self.at(i) // self.per
            return (turn ^ place[0] if self.pieces > 1 else turn, s * self.per + lax.rem(self.at(i), self.per), 0)

        return pl.BlockSpec((1, self.size, width), index)

    def is_turn(self, which, place_ref):
        return (self.at(pl.program_id(1)) // self.per) == (place_ref[0] ^ which)

    def block(self, width):
        return pl.BlockSpec((1, self.size, width), lambda s, i, place: (s, self.at(i), 0))

    def packed(self, rows):
        return pl.BlockSpec((1, self.size // LANE, rows, LANE), lambda s, i, place: (s, self.at(i), 0, 0))


def convolved(xs, masks_ref, vec_ref, size, taps):
    total = vec_ref[taps : taps + 1]
    for by in range(taps):
        term = xs[8 - by : 8 - by + size] * vec_ref[taps - 1 - by : taps - by]
        total = total + (term * masks_ref[0, :, by : by + 1] if by else term)
    return total


def convolve(normed, proj_x, vec, masks, select_low, select_state, place, taps):
    seqs, length = masks.shape[:2]
    width, inner = proj_x.shape
    size = min(256, length)
    rows = Rows(seqs, length, normed.shape[0], size)
    packed = select_low.shape[1] + select_state.shape[0]

    def kernel(place_ref, in_ref, w_ref, vec_ref, masks_ref, low_ref, state_ref, x_ref, u_ref, p_ref, xs):
        fresh = pl.program_id(1) == 0

        @pl.when(fresh)
        def _():
            xs[0:8] = jnp.zeros((8, inner), f32)

        @pl.when(jnp.logical_not(fresh))
        def _():
            xs[0:8] = xs[size : size + 8]

        x = mm(in_ref[0], w_ref[...]).astype(bf16)
        x_ref[0] = x
        xs[8 : 8 + size] = x.astype(f32)
        pre = convolved(xs, masks_ref, vec_ref, size, taps)
        u = (pre / (1.0 + jnp.exp(-pre))).astype(bf16)
        u_ref[0] = u
        low = mm(u, low_ref[...])
        state = mm_t(state_ref[...], u)
        for j in range(size // LANE):
            p_ref[0, j, 0:LANE] = low[j * LANE : (j + 1) * LANE]
            p_ref[0, j, LANE:packed] = state[:, j * LANE : (j + 1) * LANE]

    return pl.pallas_call(
        kernel,
        grid_spec=pltpu.PrefetchScalarGridSpec(
            num_scalar_prefetch=1,
            grid=rows.grid,
            in_specs=[rows.stacked(width)]
            + [whole(width, inner), whole(8, inner), rows.block(LANE), whole(*select_low.shape), whole(*select_state.shape)],
            out_specs=[rows.block(inner), rows.block(inner), rows.packed(packed)],
            scratch_shapes=[pltpu.VMEM((size + 8, inner), f32)],
        ),
        out_shape=[
            jax.ShapeDtypeStruct((seqs, length, inner), bf16),
            jax.ShapeDtypeStruct((seqs, length, inner), bf16),
            jax.ShapeDtypeStruct((seqs, length // LANE, packed, LANE), f32),
        ],
        cost_estimate=cost(9),
        compiler_params=PARAMS,
    )(place, normed, proj_x, vec, masks, select_low, select_state)


def gates(normed, grads, proj_z, proj_out, ssm_out, place):
    seqs, length, inner = ssm_out.shape
    width = proj_z.shape[0]
    size = min(256, length)
    n = len(grads)
    rows = Rows(seqs, length, n, size)

    def kernel(place_ref, a_ref, *refs):
        g_refs, (z_ref, o_ref, s_ref, gated_ref, grad_z_ref, grad_ref) = refs[:n], refs[n:]
        for which in range(n):

            @pl.when(rows.is_turn(which, place_ref))
            def _(which=which):
                z = mm(a_ref[0], z_ref[...]).astype(bf16).astype(f32)
                grad = mm_t(g_refs[which][...], o_ref[...])
                ssm = s_ref[0]
                sigmoid = 1.0 / (1.0 + jnp.exp(-z))
                gate = z * sigmoid
                gated_ref[0] = (ssm * gate).astype(bf16)
                grad_z_ref[0] = (grad * ssm * sigmoid * (1.0 + z * (1.0 - sigmoid))).astype(bf16)
                grad_ref[0] = grad * gate

    total = seqs * length // n
    return pl.pallas_call(
        kernel,
        grid_spec=pltpu.PrefetchScalarGridSpec(
            num_scalar_prefetch=1,
            grid=rows.grid,
            in_specs=[rows.stacked(width)]
            + [rows.spec(i, width) for i in range(n)]
            + [whole(width, inner), whole(inner, width), rows.block(inner)],
            out_specs=[rows.stacked(inner)] * 2 + [rows.block(inner)],
        ),
        out_shape=[jax.ShapeDtypeStruct((n, total, inner), bf16)] * 2 + [jax.ShapeDtypeStruct((seqs, length, inner), f32)],
        cost_estimate=cost(14),
        compiler_params=PARAMS,
    )(place, normed, *grads, proj_z, proj_out, ssm_out)


def convolve_back(packed, direct, x_part, vec, masks, select_low, select_state, place, n, taps):
    seqs, length, inner = x_part.shape
    size = min(256, length)
    rows = Rows(seqs, length, n, size, reverse=True)
    states = (packed.shape[2] - LANE) // 2

    def kernel(place_ref, p_ref, d_ref, x_ref, edge_ref, vec_ref, masks_ref, low_ref, state_ref, *rest):
        out_ref, sum_ref, tok_ref, xs, ds = rest
        fresh = pl.program_id(1) == 0

        @pl.when(jnp.logical_and(fresh, pl.program_id(0) == 0))
        def _():
            sum_ref[...] = jnp.zeros_like(sum_ref)

        @pl.when(fresh)
        def _():
            ds[size : size + 8] = jnp.zeros((8, inner), f32)

        @pl.when(jnp.logical_not(fresh))
        def _():
            ds[size : size + 8] = ds[0:8]

        copy = (iota((LANE, 16), 0) // 8 == iota((LANE, 16), 1)).astype(bf16)
        place_of = (iota((LANE, LANE), 1) // 16) == lax.rem(iota((LANE, LANE), 0), 8)
        by_state = lax.rem(iota((LANE, LANE), 0), 16)
        for j in range(size // LANE):
            at = slice(j * LANE, (j + 1) * LANE)
            tok_ref[0, at, 0:LANE] = p_ref[0, j, 0:LANE].astype(bf16)
            token = jnp.zeros((LANE, LANE), f32)
            for q in range(2):
                part = p_ref[0, j, LANE + q * states : LANE + (q + 1) * states].astype(bf16)
                spread = jnp.where(place_of, mm(copy, part), 0.0).astype(bf16)
                token = token + mm(spread, (by_state + q * states == iota((LANE, LANE), 1)).astype(bf16))
            tok_ref[0, at, LANE : 2 * LANE] = token.astype(bf16)
        xs[0:8] = edge_ref[0, 8:16].astype(f32)
        xs[8 : 8 + size] = x_ref[0].astype(f32)
        pre = convolved(xs, masks_ref, vec_ref, size, taps)
        sigmoid = 1.0 / (1.0 + jnp.exp(-pre))
        grad = mm_t(tok_ref[0, :, 0:LANE], low_ref[...]) + mm_t(tok_ref[0, :, LANE : 2 * LANE], state_ref[...]) + d_ref[0]
        grad = grad * sigmoid * (1.0 + pre * (1.0 - sigmoid))
        ds[0:size] = grad
        total = grad * vec_ref[taps - 1 : taps]
        sum_ref[taps : taps + 1] += jnp.sum(grad, axis=0, keepdims=True)
        sum_ref[taps - 1 : taps] += jnp.sum(grad * xs[8 : 8 + size], axis=0, keepdims=True)
        for by in range(1, taps):
            tap = taps - 1 - by
            total = total + ds[by : by + size] * masks_ref[0, :, taps + by : taps + by + 1] * vec_ref[tap : tap + 1]
            joint = grad * xs[8 - by : 8 - by + size] * masks_ref[0, :, by : by + 1]
            sum_ref[tap : tap + 1] += jnp.sum(joint, axis=0, keepdims=True)
        out_ref[0] = total.astype(bf16)

    edge = pl.BlockSpec((1, 16, inner), lambda s, i, place: (s, jnp.maximum(rows.at(i) * (size // 16) - 1, 0), 0))
    return pl.pallas_call(
        kernel,
        grid_spec=pltpu.PrefetchScalarGridSpec(
            num_scalar_prefetch=1,
            grid=rows.grid,
            in_specs=[
                rows.packed(packed.shape[2]),
                rows.block(inner),
                rows.block(inner),
                edge,
                whole(8, inner),
                rows.block(LANE),
                whole(inner, LANE),
                whole(inner, LANE),
            ],
            out_specs=[rows.stacked(inner), whole(8, inner), rows.block(2 * LANE)],
            scratch_shapes=[pltpu.VMEM((size + 8, inner), f32)] * 2,
        ),
        out_shape=[jax.ShapeDtypeStruct((n, seqs * length // n, inner), bf16)]
        + [jax.ShapeDtypeStruct((8, inner), f32), jax.ShapeDtypeStruct((seqs, length, 2 * LANE), bf16)],
        cost_estimate=cost(10),
        compiler_params=PARAMS,
    )(place, packed, direct, x_part, x_part, vec, masks, select_low, select_state)


def log_one_plus(v):
    small = v * (1.0 - v * (0.5 - v * (1.0 / 3.0 - v * 0.25)))
    return jnp.where(v < 0.01, small, jnp.log(1.0 + v))


def softplus(v):
    return jnp.maximum(v, 0.0) + log_one_plus(jnp.exp(-jnp.abs(v)))


def sigmoid_of_step(step):
    small = step * (1.0 - step * (0.5 - step * (1.0 / 6.0 - step * (1.0 / 24.0))))
    return jnp.where(step < 0.02, small, 1.0 - jnp.exp(-step))


def hot_rows():
    row, col = iota((LANE, 8 * LANE), 0), iota((LANE, 8 * LANE), 1)
    return ((lax.rem(row, 8) == col // LANE) & (row < 16)).astype(bf16)


def spread(state, hot, wide, s, blocks):
    high = state.astype(bf16).astype(f32)
    rest = state - high
    lane = iota(state.shape, 1)
    parts = []
    for i in range(blocks):
        a = pltpu.roll(high, (LANE - 8 * i) % LANE, 1)
        b = pltpu.roll(rest, (LANE + 8 - 8 * i) % LANE, 1)
        parts.append(jnp.where(lane < 8, a, b).astype(bf16))
    wide[s] = mm(jnp.concatenate(parts, axis=0), hot).reshape(blocks, state.shape[0], 8 * LANE)


def forward_kernel(
    S, G, p_ref, u_ref, masks_ref, proj_ref, vec_ref, rate_ref, hot_ref, y_ref, step_ref, start_ref, h_s, wide, w_s, se_s, su_s
):
    blocks = LANE // 8
    C = G * LANE

    @pl.when(pl.program_id(0) == 0)
    def _():
        h_s[...] = jnp.zeros_like(h_s)

    start_ref[0] = h_s[...]
    for s in range(S):
        step = softplus(mm(p_ref[s, 0, 0:LANE].astype(bf16), proj_ref[...]) + vec_ref[0:1])
        step_ref[s] = step
        u = u_ref[s].astype(f32)
        se_s[s] = jnp.where(masks_ref[s, :, 1:2] > 0.5, step, BREAK).reshape(blocks, 8, C)
        su_s[s] = (step * u).reshape(blocks, 8, C)
        spread(p_ref[s, 0, LANE : LANE + 32], hot_ref[...], wide, s, blocks)
    keys = [(s, g, j) for s in range(S) for g in range(G) for j in range(2)]

    def body(i, carry):
        hs = dict(zip(keys, carry))
        for k in range(8):
            for s in range(S):
                lanes = slice(k * LANE, (k + 1) * LANE)
                b = [wide[s, i, j * 8 : (j + 1) * 8, lanes] for j in range(2)]
                c = [wide[s, i, 16 + j * 8 : 16 + (j + 1) * 8, lanes] for j in range(2)]
                for g in range(G):
                    se, su = row8(se_s, s, i, k, g), row8(su_s, s, i, k, g)
                    prod = []
                    for j in range(2):
                        a = jnp.exp2(se * rate_ref[g, j * 8 : (j + 1) * 8])
                        hs[s, g, j] = a * hs[s, g, j] + su * b[j]
                        prod.append(c[j] * hs[s, g, j])
                    w_s[i, s, k * 16 : (k + 1) * 16, g * LANE : (g + 1) * LANE] = jnp.concatenate(prod, 0).astype(bf16)
        return tuple(hs.values())

    out = lax.fori_loop(0, blocks, body, tuple(h_s[q * 8 : (q + 1) * 8] for q in range(len(keys))))
    pick = (iota((16, 2 * LANE), 0) == iota((16, 2 * LANE), 1) // 16).astype(bf16)
    for s in range(S):
        for i in range(blocks // 2):
            both = jnp.concatenate([w_s[2 * i, s], w_s[2 * i + 1, s]], axis=0)
            y_ref[s, i * 16 : (i + 1) * 16] = mm(pick, both)
        y_ref[s] = y_ref[s] + vec_ref[1:2] * u_ref[s].astype(f32)
    for q in range(len(keys)):
        h_s[q * 8 : (q + 1) * 8] = out[q]


def backward_kernel(
    S, G, p_ref, u_ref, step_ref, ds_ref, masks_ref, proj_ref, vec_ref, rate_ref, rate2_ref, hot_ref, start_ref,
    dsp_ref, du_ref, p2_ref, dlog_ref, sum_ref, ag_s, h_s, wide, se_s, su_s, s_s, q_s, d_s, r_s
):
    blocks = LANE // 8
    C = G * LANE
    keys = [(s, g, j) for s in range(S) for g in range(G) for j in range(2)]

    @pl.when(pl.program_id(0) == 0)
    def _():
        ag_s[...] = jnp.zeros_like(ag_s)
        dlog_ref[...] = jnp.zeros_like(dlog_ref)
        sum_ref[...] = jnp.zeros_like(sum_ref)

    for s in range(S):
        step = step_ref[s]
        u = u_ref[s].astype(f32)
        se_s[s] = jnp.where(masks_ref[s, :, 1:2] > 0.5, step, BREAK).reshape(blocks, 8, C)
        su_s[s] = (step * u).reshape(blocks, 8, C)
        d_s[s] = ds_ref[s].reshape(blocks, 8, C)
        spread(p_ref[s, 0, LANE : LANE + 32], hot_ref[...], wide, s, blocks)

    def again(i, carry):
        hs = dict(zip(keys, carry))
        for k in range(8):
            for s in range(S):
                b = [wide[s, i, j * 8 : (j + 1) * 8, k * LANE : (k + 1) * LANE] for j in range(2)]
                for g in range(G):
                    se, su = row8(se_s, s, i, k, g), row8(su_s, s, i, k, g)
                    h_s[i * 8 + k, s * G + g] = jnp.concatenate([hs[s, g, 0], hs[s, g, 1]], 0).astype(bf16)
                    for j in range(2):
                        a = jnp.exp2(se * rate_ref[g, j * 8 : (j + 1) * 8])
                        hs[s, g, j] = a * hs[s, g, j] + su * b[j]
        return tuple(hs.values())

    out = lax.fori_loop(0, blocks, again, tuple(start_ref[0, q * 8 : (q + 1) * 8] for q in range(len(keys))))
    for s in range(S):
        for g in range(G):
            q = (s * G + g) * 2
            h_s[LANE, s * G + g] = jnp.concatenate([out[q], out[q + 1]], 0).astype(bf16)

    def two(v):
        return jnp.concatenate([v, v], 0).astype(bf16)

    pick = (iota((16, 2 * LANE), 0) == iota((16, 2 * LANE), 1) // 16).astype(bf16)
    fold = (lax.rem(iota((16, 2 * LANE), 1), 16) == iota((16, 2 * LANE), 0)).astype(bf16)
    one = jnp.ones((16, LANE), bf16)
    lane, row = iota((8, LANE), 1), iota((8, LANE), 0)

    def across_rows(product):
        found = product[0:8]
        for v in range(1, 16):
            found = jnp.where(lane >= 8 * v, product[8 * v : 8 * v + 8], found)
        found = jnp.sum(jnp.where(lax.rem(lane, 8) == row, found, 0.0), axis=0, keepdims=True)
        return jnp.broadcast_to(found, (8, LANE))

    def body(r, carry):
        low = blocks - 2 - 2 * r
        ags = dict(zip(keys, carry))
        tq, ts, tl, tb, tc = {}, {}, {}, {}, {}
        for t in reversed(range(16)):
            i, k = low + t // 8, t % 8
            for s in range(S):
                lanes = slice(k * LANE, (k + 1) * LANE)
                b16 = wide[s, i, 0:16, lanes].astype(bf16)
                c = [wide[s, i, 16 + j * 8 : 16 + (j + 1) * 8, lanes] for j in range(2)]
                for g in range(G):
                    se, su, ds = row8(se_s, s, i, k, g), row8(su_s, s, i, k, g), row8(d_s, s, i, k, g)
                    a = [jnp.exp2(se * rate_ref[g, j * 8 : (j + 1) * 8]) for j in range(2)]
                    gr = [c[j] * ds + ags[s, g, j] for j in range(2)]
                    for j in range(2):
                        ags[s, g, j] = a[j] * gr[j]
                    gb = jnp.concatenate(gr, 0).astype(bf16)
                    ab = jnp.concatenate(a, 0).astype(bf16)
                    gq = gb * (ab * h_s[i * 8 + k, s * G + g])
                    tq[s, g, t] = gq * rate2_ref[g]
                    tl[s, g, t] = gq * two(se)
                    ts[s, g, t] = gb * b16
                    tb[s, g, t] = gb * two(su)
                    tc[s, g, t] = h_s[i * 8 + k + 1, s * G + g] * two(ds)

        def mat(m, s):
            return jnp.concatenate([jnp.concatenate([m[s, g, t] for t in range(16)], 0) for g in range(G)], 1)

        def msum(m, s):
            return jnp.concatenate([sum(m[s, g, t] for g in range(G)) for t in range(16)], 0)

        for s in range(S):
            q = mm(pick, mat(tq, s))
            v = mm(pick, mat(ts, s))
            for h in range(2):
                q_s[s, low + h] = q[h * 8 : (h + 1) * 8]
                s_s[s, low + h] = v[h * 8 : (h + 1) * 8]
            dlog_ref[...] += mm(fold, mat(tl, s))
            for kind, m in enumerate((tb, tc)):
                found = mm_t(one, msum(m, s))[0:8]
                for h in range(2):
                    r_s[s, kind, low + h] = found[:, h * LANE : (h + 1) * LANE]
        return tuple(ags.values())

    ags = lax.fori_loop(0, blocks // 2, body, tuple(ag_s[q * 8 : (q + 1) * 8] for q in range(len(keys))))
    for q in range(len(keys)):
        ag_s[q * 8 : (q + 1) * 8] = ags[q]
    for s in range(S):
        step = step_ref[s]
        u = u_ref[s].astype(f32)
        ds = ds_ref[s]
        sums = s_s[s].reshape(LANE, C)
        dsp = ((q_s[s].reshape(LANE, C) + u * sums) * sigmoid_of_step(step)).astype(bf16)
        dsp_ref[s] = dsp
        du_ref[s] = step * sums + ds * vec_ref[1:2]
        p2_ref[s, 0, 0:LANE] = mm_t(dsp, proj_ref[...])
        for kind in range(2):
            for i in range(blocks):
                p2_ref[s, 0, LANE + 16 * kind + i : LANE + 16 * kind + i + 1] = r_s[s, kind, i, 0:1]
        sum_ref[0:1] += jnp.sum(dsp.astype(f32), axis=0, keepdims=True)
        sum_ref[1:2] += jnp.sum(ds * u, axis=0, keepdims=True)


def scan_specs(S, T, C, reverse):
    at = (lambda i: T // LANE - 1 - i) if reverse else (lambda i: i)
    return dict(
        packed=pl.BlockSpec((S, 1, LANE + 32, LANE), lambda i: (0, at(i), 0, 0)),
        block=pl.BlockSpec((S, LANE, C), lambda i: (0, at(i), 0)),
        masks=pl.BlockSpec((S, LANE, LANE), lambda i: (0, at(i), 0)),
        start=pl.BlockSpec((1, S * C // LANE * 16, LANE), lambda i: (at(i), 0, 0)),
    )


def scan_forward(packed, u, masks, proj_step, vec, rate2e, hot):
    S, T, C = u.shape
    G = C // LANE
    sp = scan_specs(S, T, C, False)
    by_token = pltpu.VMEM((S, LANE // 8, 8, C), f32)
    return pl.pallas_call(
        functools.partial(forward_kernel, S, G),
        grid=(T // LANE,),
        in_specs=[
            sp["packed"], sp["block"], sp["masks"], whole(LANE, C), whole(8, C), whole(G, 16, LANE), whole(LANE, 8 * LANE)
        ],
        out_specs=[sp["block"], sp["block"], sp["start"]],
        out_shape=[jax.ShapeDtypeStruct((S, T, C), f32)] * 2 + [jax.ShapeDtypeStruct((T // LANE, S * G * 16, LANE), f32)],
        scratch_shapes=[
            pltpu.VMEM((S * G * 16, LANE), f32),
            pltpu.VMEM((S, LANE // 8, 32, 8 * LANE), f32),
            pltpu.VMEM((LANE // 8, S, LANE, C), bf16),
            by_token,
            by_token,
        ],
        cost_estimate=cost(30),
        compiler_params=PARAMS,
    )(packed, u, masks, proj_step, vec, rate2e, hot)


def scan_backward(packed, u, step, ds, masks, proj_step, vec, rate2e, rate, hot, starts):
    S, T, C = u.shape
    G = C // LANE
    sp = scan_specs(S, T, C, True)
    by_token = pltpu.VMEM((S, LANE // 8, 8, C), f32)
    return pl.pallas_call(
        functools.partial(backward_kernel, S, G),
        grid=(T // LANE,),
        in_specs=[
            sp["packed"], sp["block"], sp["block"], sp["block"], sp["masks"], whole(LANE, C), whole(8, C),
            whole(G, 16, LANE), whole(G, 16, LANE), whole(LANE, 8 * LANE), sp["start"]
        ],
        out_specs=[sp["block"], sp["block"], sp["packed"], whole(16, C), whole(8, C)],
        out_shape=[
            jax.ShapeDtypeStruct((S, T, C), bf16),
            jax.ShapeDtypeStruct((S, T, C), f32),
            jax.ShapeDtypeStruct((S, T // LANE, LANE + 32, LANE), f32),
            jax.ShapeDtypeStruct((16, C), f32),
            jax.ShapeDtypeStruct((8, C), f32),
        ],
        scratch_shapes=[
            pltpu.VMEM((S * G * 16, LANE), f32),
            pltpu.VMEM((LANE + 1, S * G, 16, LANE), bf16),
            pltpu.VMEM((S, LANE // 8, 32, 8 * LANE), f32),
        ]
        + [by_token] * 5
        + [pltpu.VMEM((S, 2, LANE // 8, 8, LANE), f32)],
        cost_estimate=cost(85),
        compiler_params=PARAMS,
    )(packed, u, step, ds, masks, proj_step, vec, rate2e, rate.astype(bf16), hot, starts)


def after(*arrays):
    def kernel(*refs):
        refs[-1][0] = 0

    return pl.pallas_call(
        kernel,
        in_specs=[pl.BlockSpec(memory_space=pl.ANY) for _ in arrays],
        out_specs=pl.BlockSpec(memory_space=pltpu.SMEM),
        out_shape=jax.ShapeDtypeStruct((1,), jnp.int32),
    )(*arrays)[0]


def line_gather(array, axis):
    count = lax.axis_size(axis)
    right, left = array, array
    window = [array]
    for step in range(1, count):
        right = lax.ppermute(right, axis, [(i, i + 1) for i in range(step - 1, count - 1)])
        left = lax.ppermute(left, axis, [(i, i - 1) for i in range(1, count - step + 1)])
        window = [right] + window + [left]
    return window


def line_gather_at_once(array, axis):
    count = lax.axis_size(axis)
    return lax.all_to_all(jnp.broadcast_to(array[None], (count,) + array.shape), axis, 0, 0)


def line_scatter(blocks, axis):
    return jnp.sum(lax.all_to_all(blocks, axis, 0, 0).astype(f32), axis=0)


class Paired:
    def __init__(self):
        self.context = lax.axis_index("context")
        self.tensor = lax.axis_index("tensor")
        self.core = self.tensor % 2
        self.place = self.context[None]

    def across(self, array):
        return lax.ppermute(array, "context", [(0, 1), (1, 0)])

    def near(self, array):
        return lax.ppermute(array, "tensor", [(0, 1), (1, 0), (2, 3), (3, 2)])

    def far(self, array):
        return lax.ppermute(array, "tensor", [(0, 2), (2, 0), (1, 3), (3, 1)])

    def pieces(self, array, begin):
        half = array.shape[0] // 2
        mine = lax.dynamic_slice_in_dim(array, (self.core + begin) * half, half, 0)
        return self.across(mine), mine

    def pieces_done(self, array, block):
        return [array, joined_halves(block, self.near(block), self.core[None])]

    def normed(self, array, block, gain):
        return normalised_rows([array, block, self.near(block)], self.core[None], gain)

    def total(self, array, begin):
        half = array.shape[0] // 2
        mine = lax.dynamic_slice_in_dim(array, self.core * half, half, 0)
        other = lax.dynamic_slice_in_dim(array, (1 - self.core + begin) * half, half, 0).astype(bf16)
        mine = mine + self.near(other).astype(f32)
        first, second = mine[: half // 2], mine[half // 2 :]
        first = first + self.far(first.astype(bf16)).astype(f32)
        second = second + self.across(second.astype(bf16)).astype(f32)
        first = first + self.across(first.astype(bf16)).astype(f32)
        second = second + self.far(second.astype(bf16)).astype(f32)
        mine = jnp.concatenate([first, second], axis=0)
        other = self.near(mine.astype(bf16)).astype(f32)
        zero = self.core == 0
        return jnp.concatenate([jnp.where(zero, mine, other), jnp.where(zero, other, mine)])

    def share_begin(self, product):
        keep = product((self.tensor, self.tensor ^ 2))
        give = product((self.tensor ^ 1, self.tensor ^ 3))
        return [(k.astype(f32) + self.near(g).astype(f32)) for k, g in zip(keep, give)]

    def share_middle(self, sums):
        own, other = sums
        rows, width = own.shape
        half, width = rows // 2, width // 2
        far = self.far(jnp.stack([own[:half, width:], other[:half, width:]]).astype(bf16))
        across = self.across(other[half:].astype(bf16))
        first = own[:half, :width] + far[0].astype(f32)
        give = other[:half, :width] + far[1].astype(f32)
        second = own[half:] + across.astype(f32)
        return first, give, second

    def share_end(self, sums):
        first, give, second = sums
        width = first.shape[1]
        first = first + self.across(give.astype(bf16)).astype(f32)
        second = second[:, :width] + self.far(second[:, width:].astype(bf16)).astype(f32)
        return jnp.concatenate([first, second], axis=0)

    def row_total(self, array):
        array = array + self.near(array)
        return array + self.far(array)

    def vector_total(self, array):
        return self.row_total(array + self.across(array))

    def both(self, array):
        other = self.across(array)
        zero = self.context == 0
        return jnp.stack([jnp.where(zero, array, other), jnp.where(zero, other, array)])


class General:
    def __init__(self, seqs):
        self.seqs = seqs
        self.place = jnp.zeros((1,), jnp.int32)

    def pieces(self, array, begin):
        return lax.all_gather(array, "context", tiled=True), array

    def pieces_done(self, array, block):
        return [self.in_order([block], self.seqs).reshape(block.shape)]

    def normed(self, array, block, gain):
        inv_rms = normalised_rows([array], self.place, gain)[1]
        return normalised_rows(self.pieces_done(array, block), self.place, gain)[0], inv_rms

    def in_order(self, arrays, seqs):
        array = arrays[0].reshape(lax.axis_size("context"), seqs, -1, arrays[0].shape[-1])
        return array.swapaxes(0, 1).reshape(seqs, -1, array.shape[-1])

    def total(self, array, begin):
        return lax.psum(array, ("context", "tensor"))

    def share_begin(self, product):
        return [product((block,))[0].astype(f32) for block in range(lax.axis_size("tensor"))]

    def share_middle(self, sums):
        return sums

    def share_end(self, sums):
        parts = jnp.concatenate(sums, axis=-1)
        shape = parts.shape
        parts = parts.reshape(self.seqs, lax.axis_size("context"), -1, shape[-1]).swapaxes(0, 1).reshape(shape)
        parts = lax.psum_scatter(parts, "context", scatter_dimension=0, tiled=True)
        return lax.psum_scatter(parts, "tensor", scatter_dimension=1, tiled=True)

    def row_total(self, array):
        return lax.psum(array, "tensor")

    def vector_total(self, array):
        return lax.psum(array, ("context", "tensor"))

    def both(self, array):
        return lax.all_gather(array, "context")


def dot(a, b, out=f32):
    return jnp.dot(a, b, preferred_element_type=f32).astype(out)


def dot_t(a, b, out=f32):
    return lax.dot_general(a, b, (((1,), (1,)), ((), ())), preferred_element_type=f32).astype(out)


def t_dot(a, b, out=f32):
    return lax.dot_general(a, b, (((0,), (0,)), ((), ())), preferred_element_type=f32).astype(out)


def on_device(
    block_input,
    output_grad,
    doc_lengths,
    norm_gain,
    input_proj,
    conv_weight,
    conv_bias,
    select_proj,
    step_proj,
    step_bias,
    decay_log,
    skip_weight,
    output_proj,
):
    seqs, piece, model_width = block_input.shape
    shards, contexts, tensors = (lax.axis_size(axis) for axis in ("shards", "context", "tensor"))
    shard, context, tensor = (lax.axis_index(axis) for axis in ("shards", "context", "tensor"))
    moves = Paired() if (contexts, tensors) == (2, 4) else General(seqs)
    length = piece * contexts
    tokens = seqs * length
    depth = input_proj.shape[0]
    part = conv_weight.shape[0] // contexts
    inner = part * shards
    states = decay_log.shape[1]
    rank = step_proj.shape[0] * shards
    selected = select_proj.shape[1]
    taps = conv_weight.shape[1]
    share_width = model_width // tensors

    def mine(array):
        return lax.dynamic_slice_in_dim(array, context * part, part, 0)

    def my_columns(array, begin):
        blocks = [
            lax.dynamic_slice_in_dim(array, (block * contexts + context + begin) * part, part, array.ndim - 1)
            for block in range(shards)
        ]
        return jnp.concatenate(blocks, axis=-1)

    rows_flat = block_input.reshape(seqs * piece, model_width)
    row_block, row_slice = moves.pieces(rows_flat, 0)
    in_x = my_columns(input_proj[:, 0], after(row_slice))
    bounds = jnp.cumsum(doc_lengths, axis=-1)[:, :2, None, None]
    position, lane = (lax.broadcasted_iota(jnp.int32, (1, length, LANE), axis) for axis in (1, 2))
    other = jnp.where(lane < taps, position - lane, position + lane - taps)

    def document(at):
        return (at >= bounds[:, 0]).astype(jnp.int32) + (at >= bounds[:, 1]).astype(jnp.int32)

    masks = (document(position) == document(other)) & (other >= 0) & (other < length)
    masks = masks.astype(f32)

    vectors = jnp.concatenate(
        [
            mine(select_proj),
            mine(conv_weight),
            mine(decay_log),
            mine(conv_bias)[:, None],
            mine(step_bias)[:, None],
            mine(skip_weight)[:, None],
        ],
        axis=1,
    )
    vectors = jnp.pad(vectors, ((0, 0), (0, 2 * LANE - vectors.shape[1])))
    flat = [in_x, my_columns(step_proj, 0), vectors.reshape(-1, inner), norm_gain.reshape(-1, inner)]
    flat = [jnp.pad(f, ((0, -f.shape[0] % 16), (0, 0))) for f in flat]
    window = line_gather(jnp.concatenate(flat, axis=0), "shards")
    proj_x, proj_step, vectors, gain = unpacked(window, [f.shape[0] for f in flat], shard[None], masks)
    gain = gain[:, : norm_gain.shape[0] // inner].reshape(model_width).astype(f32)
    normed, inv_rms = moves.normed(rows_flat, row_block, gain)
    proj_x = proj_x.reshape(model_width, inner)
    proj_step = proj_step[:, : step_proj.shape[0]].reshape(rank, inner)
    vectors = vectors[:, : 2 * LANE * part // inner].reshape(inner, 2 * LANE)
    proj_select = vectors[:, :selected]
    rest = vectors[:, selected:].astype(f32)
    decay_rate = -jnp.exp(rest[:, taps : taps + states])
    at = taps + states
    conv_vec = jnp.concatenate([rest[:, :taps].T, rest[:, at][None], jnp.zeros((7 - taps, inner), f32)], axis=0)
    scan_vec = jnp.concatenate([rest[:, at + 1 : at + 3].T, jnp.zeros((6, inner), f32)], axis=0)
    select_low, select_state = proj_select[:, :rank], proj_select[:, rank:]

    grad_flat = output_grad.reshape(seqs * piece, model_width)

    in_z = my_columns(input_proj[:, 1], after(window[len(window) // 2 - 1]))
    out_own = mine(output_proj)
    out_own = [out_own[:, i * inner : (i + 1) * inner] for i in range(model_width // inner)]
    others = jnp.concatenate([in_z] + out_own + [jnp.zeros((16, inner), bf16)], axis=0)
    others = lax.dynamic_slice_in_dim(others, after(proj_x) * 16, others.shape[0] - 16, 0)
    others = line_gather_at_once(others, "shards")

    x_part, values, projected = convolve(
        normed, proj_x, conv_vec, masks, select_low, select_state.T, moves.place, taps
    )

    def total(packed, begin):
        return moves.total(packed.reshape(-1, LANE), begin).reshape(packed.shape)

    projected = total(projected, 0)
    grad_block = moves.pieces(grad_flat, after(row_block))[0]

    hot = hot_rows()

    def by_group(array, begin=0.0):
        return (array.T + begin).reshape(states, inner // LANE, LANE).swapaxes(0, 1)

    ssm_out, step, starts = scan_forward(
        projected, values, masks, proj_step, scan_vec, by_group(decay_rate * LOG2E), hot
    )

    proj_z = others[:, :depth].reshape(model_width, inner)
    proj_out = [others[:, depth + i * part : depth + (i + 1) * part] for i in range(model_width // inner)]
    proj_out = jnp.concatenate(proj_out, axis=-1).reshape(inner, model_width)
    grad_all = moves.pieces_done(grad_flat, grad_block)
    gated, grad_z, grad_ssm = gates(normed, grad_all, proj_z, proj_out, ssm_out, moves.place)

    def weight_grad(lefts, rights):
        if not isinstance(rights, list):
            lefts, rights = ([a.reshape(-1, a.shape[-1])] for a in (lefts, rights))
        return sum(t_dot(a, b) for a, b in zip(lefts, rights)).astype(bf16)

    early = lax.all_to_all(weight_grad(normed, grad_z).reshape(shards, depth, inner), "shards", 0, 0)
    middle = lax.all_to_all(weight_grad(gated, grad_all).reshape(shards, part, model_width), "shards", 0, 0)
    def chosen(weights, blocks, axis, begin=0):
        return jnp.concatenate(
            [lax.dynamic_slice_in_dim(weights, (b + begin) * share_width, share_width, axis) for b in blocks], axis
        )

    out_sums = moves.share_begin(lambda blocks: [dot(gated[i], chosen(proj_out, blocks, 1), bf16) for i in range(gated.shape[0])])
    out_sums_2 = moves.share_middle(out_sums)
    out_share = moves.share_end(out_sums_2)
    own_columns = tensor * share_width
    input_share = lax.dynamic_slice_in_dim(block_input, own_columns, share_width, 2).astype(f32)
    block_output = (input_share + out_share.reshape(input_share.shape)).astype(bf16)

    grad_step_pre, grad_direct, partial_grad, grad_decay, scan_sums = scan_backward(
        projected,
        values,
        step,
        grad_ssm,
        masks,
        proj_step,
        scan_vec,
        by_group(decay_rate * LOG2E),
        by_group(decay_rate, after(*out_sums).astype(f32)),
        hot,
        starts,
    )
    grad_decay_log = grad_decay.T * decay_rate
    step_low = projected[:, :, :rank].reshape(tokens, rank).astype(bf16)
    grad_step_proj = t_dot(step_low, grad_step_pre.reshape(tokens, inner))
    pulled = after(early, partial_grad, *out_sums_2)
    grad_in_z = jnp.sum(early.astype(f32), axis=0) + pulled.astype(f32)
    z_pair = moves.both(grad_in_z.astype(bf16))
    partial_grad = total(partial_grad, pulled)

    grad_x, conv_sums, grad_selected = convolve_back(
        partial_grad,
        grad_direct,
        x_part,
        conv_vec + after(block_output, partial_grad).astype(f32),
        masks,
        select_low,
        jnp.pad(select_state, ((0, 0), (0, LANE - select_state.shape[1]))),
        moves.place,
        normed.shape[0],
        taps,
    )
    grad_select = t_dot(values.reshape(tokens, inner), grad_selected.reshape(tokens, -1))[:, :selected]

    small = jnp.concatenate(
        [
            grad_select,
            conv_sums[:taps].T,
            grad_decay_log,
            conv_sums[taps][:, None],
            scan_sums[:2].T,
        ],
        axis=1,
    ).astype(bf16)
    sent = after(middle, grad_x[0])
    small = small + sent.astype(bf16)
    out_pair = moves.both((jnp.sum(middle.astype(f32), axis=0) + sent.astype(f32)).astype(bf16))
    small = jnp.pad(small, ((0, 0), (0, 2 * LANE - small.shape[1])))
    late_local = jnp.concatenate(
        [
            weight_grad(normed, grad_x).reshape(shards, depth, inner),
            grad_step_proj.astype(bf16).reshape(shards, -1, inner),
            small.reshape(shards, -1, inner),
        ],
        axis=1,
    )
    begin = after(late_local, z_pair)

    def normed_part(blocks):
        blocks = jnp.stack([jnp.asarray(b, jnp.int32) + begin for b in blocks])
        return products(grad_x, grad_z, proj_x, proj_z, blocks, share_width)

    grad_normed = moves.share_end(moves.share_middle(moves.share_begin(normed_part))).reshape(seqs, piece, share_width)
    inv_rms = inv_rms[:, :1].reshape(seqs, piece, 1)
    unit_share = input_share * inv_rms
    weighted = grad_normed * lax.dynamic_slice_in_dim(gain, own_columns, share_width, 0)
    row_dots = moves.row_total(jnp.sum(unit_share * weighted, axis=-1))[:, :, None]
    grad_share = lax.dynamic_slice_in_dim(output_grad, own_columns, share_width, 2).astype(f32)
    input_grad = grad_share + inv_rms * (weighted - unit_share * (row_dots / model_width))

    late = line_scatter(late_local, "shards") + after(grad_normed, z_pair, out_pair).astype(f32)
    grad_in_x = late[:depth]
    gain_part = jnp.sum(in_x.astype(f32) * grad_in_x, axis=1) + jnp.sum(in_z.astype(f32) * grad_in_z, axis=1)
    grad_gain = moves.vector_total(gain_part) / norm_gain.astype(f32)

    def columns_of(pair):
        pair = pair.astype(f32).reshape(pair.shape[:-1] + (shards, part))
        return jnp.moveaxis(pair, 0, -2).reshape(pair.shape[1], -1)

    late = moves.both(late.astype(bf16))
    grad_in = interleaved(late, z_pair, depth, part)
    grad_step_proj = columns_of(late[:, depth : depth + step_proj.shape[0]])
    small = late[:, depth + step_proj.shape[0] :].reshape(contexts * part, 2 * LANE).astype(f32)
    grad_out_proj = out_pair.reshape(contexts * part, model_width).astype(f32)
    at = selected + taps + states
    return (
        block_output,
        input_grad,
        grad_gain,
        grad_in,
        small[:, selected : selected + taps],
        small[:, at],
        small[:, :selected],
        grad_step_proj,
        small[:, at + 1],
        small[:, selected + taps : at],
        small[:, at + 2],
        grad_out_proj,
    )


def solution(mesh):
    placed = (
        P("shards", "context", None),
        P("shards", "context", None),
        P("shards", None),
        P("shards"),
        P("shards", None, "tensor"),
        P(("tensor", "shards"), None),
        P(("tensor", "shards")),
        P(("tensor", "shards"), None),
        P("shards", "tensor"),
        P(("tensor", "shards")),
        P(("tensor", "shards"), None),
        P(("tensor", "shards")),
        P(("tensor", "shards"), None),
    )
    return jax.shard_map(
        on_device,
        mesh=mesh,
        in_specs=placed,
        out_specs=(
            P("shards", "context", "tensor"),
            P("shards", "context", "tensor"),
            P("shards"),
            P("shards", None, "tensor"),
            P(("tensor", "shards"), None),
            P(("tensor", "shards")),
            P(("tensor", "shards"), None),
            P("shards", "tensor"),
            P(("tensor", "shards")),
            P(("tensor", "shards"), None),
            P(("tensor", "shards")),
            P(("tensor", "shards"), None),
        ),
        check_vma=False,
    )
```

```python
import functools

import jax
import jax.numpy as jnp
from jax import lax
from jax.experimental import pallas as pl
from jax.experimental.pallas import tpu as pltpu
from jax.sharding import PartitionSpec as P

EPS = 1e-05
LANE = 128
LOG2E = 1.4426950408889634
BREAK = 1e6
f32 = jnp.float32
bf16 = jnp.bfloat16


def row8(ref, s, i, k, g):
    return jnp.broadcast_to(ref[s, i, k : k + 1, g * LANE : (g + 1) * LANE], (8, LANE))


def mm(a, b):
    return jnp.dot(a, b, preferred_element_type=f32)


def mm_t(a, b):
    return lax.dot_general(a, b, (((1,), (1,)), ((), ())), preferred_element_type=f32)


def iota(shape, axis):
    return lax.broadcasted_iota(jnp.int32, shape, axis)


def cost(us):
    return pl.CostEstimate(flops=int(us * 1.15e8), bytes_accessed=int(us * 3.6e5), transcendentals=0)


PARAMS = pltpu.CompilerParams(vmem_limit_bytes=58 << 20)


def whole(*shape):
    return pl.BlockSpec(shape, lambda *_: (0,) * len(shape))


def joined_halves(first, second, place):
    half, width = first.shape
    size = min(half, 128)
    count = half // size

    def kernel(place_ref, first_ref, second_ref, out_ref):
        this = (pl.program_id(0) // count) == place_ref[0]

        def put(ref):
            out_ref[...] = ref[...]

        @pl.when(this)
        def _():
            put(first_ref)

        @pl.when(jnp.logical_not(this))
        def _():
            put(second_ref)

    def spec(which):
        def index(i, place):
            start = (place[0] ^ which) * count
            return (jnp.clip(i - start, 0, count - 1), 0)

        return pl.BlockSpec((size, width), index)

    return pl.pallas_call(
        kernel,
        grid_spec=pltpu.PrefetchScalarGridSpec(
            num_scalar_prefetch=1,
            grid=(2 * count,),
            in_specs=[spec(0), spec(1)],
            out_specs=pl.BlockSpec((size, width), lambda i, place: (i, 0)),
        ),
        out_shape=jax.ShapeDtypeStruct((2 * half, width), bf16),
        cost_estimate=cost(4),
        compiler_params=PARAMS,
    )(place, first, second)


def normalised_rows(blocks, place, gain):
    count, width = blocks[0].shape
    size = min(count, 256)
    per = count // size
    half = per // 2
    n = 1 if len(blocks) == 1 else 2

    def kernel(place_ref, *refs):
        ins, (gain_ref, out_ref, inv_ref) = refs[: len(blocks)], refs[len(blocks) :]
        i = pl.program_id(0)

        def inverse(ref):
            wide = ref[...].astype(f32)
            inv_rms = lax.rsqrt(jnp.mean(wide * wide, axis=-1, keepdims=True) + EPS)
            out_ref[0] = (wide * inv_rms * gain_ref[...]).astype(bf16)
            return inv_rms

        @pl.when(i < per)
        def _():
            inv_ref[...] = jnp.broadcast_to(inverse(ins[0]), inv_ref.shape)

        for which, ref in enumerate(ins[1:]):
            start = per + (place_ref[0] ^ which) * half

            @pl.when((i >= start) & (i < start + half))
            def _(ref=ref):
                inverse(ref)

    def spec(which):
        def index(i, place):
            if which == 0:
                return (jnp.minimum(i, per - 1), 0)
            return (jnp.clip(i - per - (place[0] ^ (which - 1)) * half, 0, half - 1), 0)

        return pl.BlockSpec((size, width), index)

    return pl.pallas_call(
        kernel,
        grid_spec=pltpu.PrefetchScalarGridSpec(
            num_scalar_prefetch=1,
            grid=(n * per,),
            in_specs=[spec(i) for i in range(len(blocks))] + [whole(1, width)],
            out_specs=[
                pl.BlockSpec((1, size, width), lambda i, place: (i // per, lax.rem(i, per), 0)),
                pl.BlockSpec((size, LANE), lambda i, place: (jnp.minimum(i, per - 1), 0)),
            ],
        ),
        out_shape=[jax.ShapeDtypeStruct((n, count, width), bf16), jax.ShapeDtypeStruct((count, LANE), f32)],
        cost_estimate=cost(8),
        compiler_params=PARAMS,
    )(place, *blocks, gain.reshape(1, width))


def unpacked(window, counts, place, *before):
    slots = len(window)
    count = (slots + 1) // 2
    width = window[0].shape[1]
    starts = [sum(counts[:i]) for i in range(len(counts))]

    def kernel(place_ref, *refs):
        ins, outs = refs[:slots], refs[slots + len(before) :]
        wanted = pl.program_id(0) + count - 1 - place_ref[0]
        for slot, ref in enumerate(ins):

            @pl.when(wanted == slot)
            def _(ref=ref):
                for out, start, rows in zip(outs, starts, counts):
                    out[0] = ref[start : start + rows]

    return pl.pallas_call(
        kernel,
        grid_spec=pltpu.PrefetchScalarGridSpec(
            num_scalar_prefetch=1,
            grid=(count,),
            in_specs=[whole(*window[0].shape) for _ in window] + [pl.BlockSpec(memory_space=pl.ANY) for _ in before],
            out_specs=[pl.BlockSpec((1, rows, width), lambda j, place: (j, 0, 0)) for rows in counts],
        ),
        out_shape=[jax.ShapeDtypeStruct((count, rows, width), bf16) for rows in counts],
        cost_estimate=cost(3),
        compiler_params=PARAMS,
    )(place, *window, *before)


def products(lefts, more_lefts, right, more_right, blocks, width):
    n, count, inner = lefts.shape
    size = min(count, 512)

    def kernel(blocks_ref, *refs):
        a, b, (w, v), outs = refs[:n], refs[n : 2 * n], refs[2 * n : 2 * n + 2], refs[2 * n + 2 :]
        for i in range(n):
            outs[i][...] = (mm_t(a[i][0], w[...]) + mm_t(b[i][0], v[...])).astype(bf16)

    rows = [pl.BlockSpec((1, size, inner), lambda j, i, blocks, which=which: (which, i, 0)) for which in range(n)]
    weights = pl.BlockSpec((width, inner), lambda j, i, blocks: (blocks[j], 0))
    return pl.pallas_call(
        kernel,
        grid_spec=pltpu.PrefetchScalarGridSpec(
            num_scalar_prefetch=1,
            grid=(blocks.shape[0], count // size),
            in_specs=rows * 2 + [weights] * 2,
            out_specs=[pl.BlockSpec((size, width), lambda j, i, blocks: (i, j))] * n,
        ),
        out_shape=[jax.ShapeDtypeStruct((count, width * blocks.shape[0]), bf16)] * n,
        cost_estimate=cost(5),
        compiler_params=PARAMS,
    )(blocks, *[lefts] * n, *[more_lefts] * n, right, more_right)


def interleaved(first, second, depth, part):
    contexts, _, inner = first.shape
    shards = inner // part
    size = 64

    def kernel(a_ref, b_ref, out_ref):
        for which, ref in enumerate((a_ref, b_ref)):
            columns = [
                ref[c, :, s * part : (s + 1) * part].astype(f32) for s in range(shards) for c in range(contexts)
            ]
            out_ref[:, which, :] = jnp.concatenate(columns, axis=1)

    return pl.pallas_call(
        kernel,
        grid=(depth // size,),
        in_specs=[pl.BlockSpec((contexts, size, inner), lambda i: (0, i, 0))] * 2,
        out_specs=pl.BlockSpec((size, 2, contexts * inner), lambda i: (i, 0, 0)),
        out_shape=jax.ShapeDtypeStruct((depth, 2, contexts * inner), f32),
        cost_estimate=cost(5),
        compiler_params=PARAMS,
    )(first, second)


class Rows:
    def __init__(self, seqs, length, arrays, size, reverse=False):
        self.pieces = arrays
        self.size = size
        self.count = length // size
        self.per = self.count // arrays
        self.grid = (seqs, self.count)
        self.reverse = reverse

    def at(self, i):
        return self.count - 1 - i if self.reverse else i

    def spec(self, which, width):
        def index(s, i, place):
            low = (place[0] ^ which) * self.per
            return (s * self.per + jnp.clip(self.at(i) - low, 0, self.per - 1), 0)

        return pl.BlockSpec((self.size, width), index)

    def stacked(self, width):
        def index(s, i, place):
            turn = self.at(i) // self.per
            return (turn ^ place[0] if self.pieces > 1 else turn, s * self.per + lax.rem(self.at(i), self.per), 0)

        return pl.BlockSpec((1, self.size, width), index)

    def is_turn(self, which, place_ref):
        return (self.at(pl.program_id(1)) // self.per) == (place_ref[0] ^ which)

    def block(self, width):
        return pl.BlockSpec((1, self.size, width), lambda s, i, place: (s, self.at(i), 0))

    def packed(self, rows):
        return pl.BlockSpec((1, self.size // LANE, rows, LANE), lambda s, i, place: (s, self.at(i), 0, 0))


def convolved(xs, masks_ref, vec_ref, size, taps):
    total = vec_ref[taps : taps + 1]
    for by in range(taps):
        term = xs[8 - by : 8 - by + size] * vec_ref[taps - 1 - by : taps - by]
        total = total + (term * masks_ref[0, :, by : by + 1] if by else term)
    return total


def convolve(normed, proj_x, vec, masks, select_low, select_state, place, taps):
    seqs, length = masks.shape[:2]
    width, inner = proj_x.shape
    size = min(256, length)
    rows = Rows(seqs, length, normed.shape[0], size)
    packed = select_low.shape[1] + select_state.shape[0]

    def kernel(place_ref, in_ref, w_ref, vec_ref, masks_ref, low_ref, state_ref, x_ref, u_ref, p_ref, xs):
        fresh = pl.program_id(1) == 0

        @pl.when(fresh)
        def _():
            xs[0:8] = jnp.zeros((8, inner), f32)

        @pl.when(jnp.logical_not(fresh))
        def _():
            xs[0:8] = xs[size : size + 8]

        x = mm(in_ref[0], w_ref[...]).astype(bf16)
        x_ref[0] = x
        xs[8 : 8 + size] = x.astype(f32)
        pre = convolved(xs, masks_ref, vec_ref, size, taps)
        u = (pre / (1.0 + jnp.exp(-pre))).astype(bf16)
        u_ref[0] = u
        low = mm(u, low_ref[...])
        state = mm_t(state_ref[...], u)
        for j in range(size // LANE):
            p_ref[0, j, 0:LANE] = low[j * LANE : (j + 1) * LANE]
            p_ref[0, j, LANE:packed] = state[:, j * LANE : (j + 1) * LANE]

    return pl.pallas_call(
        kernel,
        grid_spec=pltpu.PrefetchScalarGridSpec(
            num_scalar_prefetch=1,
            grid=rows.grid,
            in_specs=[rows.stacked(width)]
            + [whole(width, inner), whole(8, inner), rows.block(LANE), whole(*select_low.shape), whole(*select_state.shape)],
            out_specs=[rows.block(inner), rows.block(inner), rows.packed(packed)],
            scratch_shapes=[pltpu.VMEM((size + 8, inner), f32)],
        ),
        out_shape=[
            jax.ShapeDtypeStruct((seqs, length, inner), bf16),
            jax.ShapeDtypeStruct((seqs, length, inner), bf16),
            jax.ShapeDtypeStruct((seqs, length // LANE, packed, LANE), f32),
        ],
        cost_estimate=cost(9),
        compiler_params=PARAMS,
    )(place, normed, proj_x, vec, masks, select_low, select_state)


def gates(normed, grads, proj_z, proj_out, ssm_out, place):
    seqs, length, inner = ssm_out.shape
    width = proj_z.shape[0]
    size = min(256, length)
    n = len(grads)
    rows = Rows(seqs, length, n, size)

    def kernel(place_ref, a_ref, *refs):
        g_refs, (z_ref, o_ref, s_ref, gated_ref, grad_z_ref, grad_ref) = refs[:n], refs[n:]
        for which in range(n):

            @pl.when(rows.is_turn(which, place_ref))
            def _(which=which):
                z = mm(a_ref[0], z_ref[...]).astype(bf16).astype(f32)
                grad = mm_t(g_refs[which][...], o_ref[...])
                ssm = s_ref[0]
                sigmoid = 1.0 / (1.0 + jnp.exp(-z))
                gate = z * sigmoid
                gated_ref[0] = (ssm * gate).astype(bf16)
                grad_z_ref[0] = (grad * ssm * sigmoid * (1.0 + z * (1.0 - sigmoid))).astype(bf16)
                grad_ref[0] = grad * gate

    total = seqs * length // n
    return pl.pallas_call(
        kernel,
        grid_spec=pltpu.PrefetchScalarGridSpec(
            num_scalar_prefetch=1,
            grid=rows.grid,
            in_specs=[rows.stacked(width)]
            + [rows.spec(i, width) for i in range(n)]
            + [whole(width, inner), whole(inner, width), rows.block(inner)],
            out_specs=[rows.stacked(inner)] * 2 + [rows.block(inner)],
        ),
        out_shape=[jax.ShapeDtypeStruct((n, total, inner), bf16)] * 2 + [jax.ShapeDtypeStruct((seqs, length, inner), f32)],
        cost_estimate=cost(14),
        compiler_params=PARAMS,
    )(place, normed, *grads, proj_z, proj_out, ssm_out)


def convolve_back(packed, direct, x_part, vec, masks, select_low, select_state, place, n, taps):
    seqs, length, inner = x_part.shape
    size = min(256, length)
    rows = Rows(seqs, length, n, size, reverse=True)
    states = (packed.shape[2] - LANE) // 2

    def kernel(place_ref, p_ref, d_ref, x_ref, edge_ref, vec_ref, masks_ref, low_ref, state_ref, *rest):
        out_ref, sum_ref, tok_ref, xs, ds = rest
        fresh = pl.program_id(1) == 0

        @pl.when(jnp.logical_and(fresh, pl.program_id(0) == 0))
        def _():
            sum_ref[...] = jnp.zeros_like(sum_ref)

        @pl.when(fresh)
        def _():
            ds[size : size + 8] = jnp.zeros((8, inner), f32)

        @pl.when(jnp.logical_not(fresh))
        def _():
            ds[size : size + 8] = ds[0:8]

        copy = (iota((LANE, 16), 0) // 8 == iota((LANE, 16), 1)).astype(bf16)
        place_of = (iota((LANE, LANE), 1) // 16) == lax.rem(iota((LANE, LANE), 0), 8)
        by_state = lax.rem(iota((LANE, LANE), 0), 16)
        for j in range(size // LANE):
            at = slice(j * LANE, (j + 1) * LANE)
            tok_ref[0, at, 0:LANE] = p_ref[0, j, 0:LANE].astype(bf16)
            token = jnp.zeros((LANE, LANE), f32)
            for q in range(2):
                part = p_ref[0, j, LANE + q * states : LANE + (q + 1) * states].astype(bf16)
                spread = jnp.where(place_of, mm(copy, part), 0.0).astype(bf16)
                token = token + mm(spread, (by_state + q * states == iota((LANE, LANE), 1)).astype(bf16))
            tok_ref[0, at, LANE : 2 * LANE] = token.astype(bf16)
        xs[0:8] = edge_ref[0, 8:16].astype(f32)
        xs[8 : 8 + size] = x_ref[0].astype(f32)
        pre = convolved(xs, masks_ref, vec_ref, size, taps)
        sigmoid = 1.0 / (1.0 + jnp.exp(-pre))
        grad = mm_t(tok_ref[0, :, 0:LANE], low_ref[...]) + mm_t(tok_ref[0, :, LANE : 2 * LANE], state_ref[...]) + d_ref[0]
        grad = grad * sigmoid * (1.0 + pre * (1.0 - sigmoid))
        ds[0:size] = grad
        total = grad * vec_ref[taps - 1 : taps]
        sum_ref[taps : taps + 1] += jnp.sum(grad, axis=0, keepdims=True)
        sum_ref[taps - 1 : taps] += jnp.sum(grad * xs[8 : 8 + size], axis=0, keepdims=True)
        for by in range(1, taps):
            tap = taps - 1 - by
            total = total + ds[by : by + size] * masks_ref[0, :, taps + by : taps + by + 1] * vec_ref[tap : tap + 1]
            joint = grad * xs[8 - by : 8 - by + size] * masks_ref[0, :, by : by + 1]
            sum_ref[tap : tap + 1] += jnp.sum(joint, axis=0, keepdims=True)
        out_ref[0] = total.astype(bf16)

    edge = pl.BlockSpec((1, 16, inner), lambda s, i, place: (s, jnp.maximum(rows.at(i) * (size // 16) - 1, 0), 0))
    return pl.pallas_call(
        kernel,
        grid_spec=pltpu.PrefetchScalarGridSpec(
            num_scalar_prefetch=1,
            grid=rows.grid,
            in_specs=[
                rows.packed(packed.shape[2]),
                rows.block(inner),
                rows.block(inner),
                edge,
                whole(8, inner),
                rows.block(LANE),
                whole(inner, LANE),
                whole(inner, LANE),
            ],
            out_specs=[rows.stacked(inner), whole(8, inner), rows.block(2 * LANE)],
            scratch_shapes=[pltpu.VMEM((size + 8, inner), f32)] * 2,
        ),
        out_shape=[jax.ShapeDtypeStruct((n, seqs * length // n, inner), bf16)]
        + [jax.ShapeDtypeStruct((8, inner), f32), jax.ShapeDtypeStruct((seqs, length, 2 * LANE), bf16)],
        cost_estimate=cost(160),
        compiler_params=PARAMS,
    )(place, packed, direct, x_part, x_part, vec, masks, select_low, select_state)


def log_one_plus(v):
    small = v * (1.0 - v * (0.5 - v * (1.0 / 3.0 - v * 0.25)))
    return jnp.where(v < 0.01, small, jnp.log(1.0 + v))


def softplus(v):
    return jnp.maximum(v, 0.0) + log_one_plus(jnp.exp(-jnp.abs(v)))


def sigmoid_of_step(step):
    small = step * (1.0 - step * (0.5 - step * (1.0 / 6.0 - step * (1.0 / 24.0))))
    return jnp.where(step < 0.02, small, 1.0 - jnp.exp(-step))


def hot_rows():
    row, col = iota((LANE, 8 * LANE), 0), iota((LANE, 8 * LANE), 1)
    return ((lax.rem(row, 8) == col // LANE) & (row < 16)).astype(bf16)


def spread(state, hot, wide, s, blocks):
    high = state.astype(bf16).astype(f32)
    rest = state - high
    lane = iota(state.shape, 1)
    parts = []
    for i in range(blocks):
        a = pltpu.roll(high, (LANE - 8 * i) % LANE, 1)
        b = pltpu.roll(rest, (LANE + 8 - 8 * i) % LANE, 1)
        parts.append(jnp.where(lane < 8, a, b).astype(bf16))
    wide[s] = mm(jnp.concatenate(parts, axis=0), hot).reshape(blocks, state.shape[0], 8 * LANE)


def forward_kernel(
    S, G, p_ref, u_ref, masks_ref, proj_ref, vec_ref, rate_ref, hot_ref, y_ref, step_ref, start_ref, h_s, wide, w_s, se_s, su_s
):
    blocks = LANE // 8
    C = G * LANE

    @pl.when(pl.program_id(0) == 0)
    def _():
        h_s[...] = jnp.zeros_like(h_s)

    start_ref[0] = h_s[...]
    for s in range(S):
        step = softplus(mm(p_ref[s, 0, 0:LANE].astype(bf16), proj_ref[...]) + vec_ref[0:1])
        step_ref[s] = step
        u = u_ref[s].astype(f32)
        se_s[s] = jnp.where(masks_ref[s, :, 1:2] > 0.5, step, BREAK).reshape(blocks, 8, C)
        su_s[s] = (step * u).reshape(blocks, 8, C)
        spread(p_ref[s, 0, LANE : LANE + 32], hot_ref[...], wide, s, blocks)
    keys = [(s, g, j) for s in range(S) for g in range(G) for j in range(2)]

    def body(i, carry):
        hs = dict(zip(keys, carry))
        for k in range(8):
            for s in range(S):
                lanes = slice(k * LANE, (k + 1) * LANE)
                b = [wide[s, i, j * 8 : (j + 1) * 8, lanes] for j in range(2)]
                c = [wide[s, i, 16 + j * 8 : 16 + (j + 1) * 8, lanes] for j in range(2)]
                for g in range(G):
                    se, su = row8(se_s, s, i, k, g), row8(su_s, s, i, k, g)
                    prod = []
                    for j in range(2):
                        a = jnp.exp2(se * rate_ref[g, j * 8 : (j + 1) * 8])
                        hs[s, g, j] = a * hs[s, g, j] + su * b[j]
                        prod.append(c[j] * hs[s, g, j])
                    w_s[i, s, k * 16 : (k + 1) * 16, g * LANE : (g + 1) * LANE] = jnp.concatenate(prod, 0).astype(bf16)
        return tuple(hs.values())

    out = lax.fori_loop(0, blocks, body, tuple(h_s[q * 8 : (q + 1) * 8] for q in range(len(keys))))
    pick = (iota((16, 2 * LANE), 0) == iota((16, 2 * LANE), 1) // 16).astype(bf16)
    for s in range(S):
        for i in range(blocks // 2):
            both = jnp.concatenate([w_s[2 * i, s], w_s[2 * i + 1, s]], axis=0)
            y_ref[s, i * 16 : (i + 1) * 16] = mm(pick, both)
        y_ref[s] = y_ref[s] + vec_ref[1:2] * u_ref[s].astype(f32)
    for q in range(len(keys)):
        h_s[q * 8 : (q + 1) * 8] = out[q]


def backward_kernel(
    S, G, p_ref, u_ref, step_ref, ds_ref, masks_ref, proj_ref, vec_ref, rate_ref, rate2_ref, hot_ref, start_ref,
    dsp_ref, du_ref, p2_ref, dlog_ref, sum_ref, ag_s, h_s, wide, se_s, su_s, s_s, q_s, d_s, r_s
):
    blocks = LANE // 8
    C = G * LANE
    keys = [(s, g, j) for s in range(S) for g in range(G) for j in range(2)]

    @pl.when(pl.program_id(0) == 0)
    def _():
        ag_s[...] = jnp.zeros_like(ag_s)
        dlog_ref[...] = jnp.zeros_like(dlog_ref)
        sum_ref[...] = jnp.zeros_like(sum_ref)

    for s in range(S):
        step = step_ref[s]
        u = u_ref[s].astype(f32)
        se_s[s] = jnp.where(masks_ref[s, :, 1:2] > 0.5, step, BREAK).reshape(blocks, 8, C)
        su_s[s] = (step * u).reshape(blocks, 8, C)
        d_s[s] = ds_ref[s].reshape(blocks, 8, C)
        spread(p_ref[s, 0, LANE : LANE + 32], hot_ref[...], wide, s, blocks)

    def again(i, carry):
        hs = dict(zip(keys, carry))
        for k in range(8):
            for s in range(S):
                b = [wide[s, i, j * 8 : (j + 1) * 8, k * LANE : (k + 1) * LANE] for j in range(2)]
                for g in range(G):
                    se, su = row8(se_s, s, i, k, g), row8(su_s, s, i, k, g)
                    h_s[i * 8 + k, s * G + g] = jnp.concatenate([hs[s, g, 0], hs[s, g, 1]], 0).astype(bf16)
                    for j in range(2):
                        a = jnp.exp2(se * rate_ref[g, j * 8 : (j + 1) * 8])
                        hs[s, g, j] = a * hs[s, g, j] + su * b[j]
        return tuple(hs.values())

    out = lax.fori_loop(0, blocks, again, tuple(start_ref[0, q * 8 : (q + 1) * 8] for q in range(len(keys))))
    for s in range(S):
        for g in range(G):
            q = (s * G + g) * 2
            h_s[LANE, s * G + g] = jnp.concatenate([out[q], out[q + 1]], 0).astype(bf16)

    def two(v):
        return jnp.concatenate([v, v], 0).astype(bf16)

    pick = (iota((16, 2 * LANE), 0) == iota((16, 2 * LANE), 1) // 16).astype(bf16)
    fold = (lax.rem(iota((16, 2 * LANE), 1), 16) == iota((16, 2 * LANE), 0)).astype(bf16)
    one = jnp.ones((16, LANE), bf16)
    lane, row = iota((8, LANE), 1), iota((8, LANE), 0)

    def across_rows(product):
        found = product[0:8]
        for v in range(1, 16):
            found = jnp.where(lane >= 8 * v, product[8 * v : 8 * v + 8], found)
        found = jnp.sum(jnp.where(lax.rem(lane, 8) == row, found, 0.0), axis=0, keepdims=True)
        return jnp.broadcast_to(found, (8, LANE))

    def body(r, carry):
        low = blocks - 2 - 2 * r
        ags = dict(zip(keys, carry))
        tq, ts, tl, tb, tc = {}, {}, {}, {}, {}
        for t in reversed(range(16)):
            i, k = low + t // 8, t % 8
            for s in range(S):
                lanes = slice(k * LANE, (k + 1) * LANE)
                b16 = wide[s, i, 0:16, lanes].astype(bf16)
                c = [wide[s, i, 16 + j * 8 : 16 + (j + 1) * 8, lanes] for j in range(2)]
                for g in range(G):
                    se, su, ds = row8(se_s, s, i, k, g), row8(su_s, s, i, k, g), row8(d_s, s, i, k, g)
                    a = [jnp.exp2(se * rate_ref[g, j * 8 : (j + 1) * 8]) for j in range(2)]
                    gr = [c[j] * ds + ags[s, g, j] for j in range(2)]
                    for j in range(2):
                        ags[s, g, j] = a[j] * gr[j]
                    gb = jnp.concatenate(gr, 0).astype(bf16)
                    ab = jnp.concatenate(a, 0).astype(bf16)
                    gq = gb * (ab * h_s[i * 8 + k, s * G + g])
                    tq[s, g, t] = gq * rate2_ref[g]
                    tl[s, g, t] = gq * two(se)
                    ts[s, g, t] = gb * b16
                    tb[s, g, t] = gb * two(su)
                    tc[s, g, t] = h_s[i * 8 + k + 1, s * G + g] * two(ds)

        def mat(m, s):
            return jnp.concatenate([jnp.concatenate([m[s, g, t] for t in range(16)], 0) for g in range(G)], 1)

        def msum(m, s):
            return jnp.concatenate([sum(m[s, g, t] for g in range(G)) for t in range(16)], 0)

        for s in range(S):
            q = mm(pick, mat(tq, s))
            v = mm(pick, mat(ts, s))
            for h in range(2):
                q_s[s, low + h] = q[h * 8 : (h + 1) * 8]
                s_s[s, low + h] = v[h * 8 : (h + 1) * 8]
            dlog_ref[...] += mm(fold, mat(tl, s))
            for kind, m in enumerate((tb, tc)):
                found = mm_t(one, msum(m, s))[0:8]
                for h in range(2):
                    r_s[s, kind, low + h] = found[:, h * LANE : (h + 1) * LANE]
        return tuple(ags.values())

    ags = lax.fori_loop(0, blocks // 2, body, tuple(ag_s[q * 8 : (q + 1) * 8] for q in range(len(keys))))
    for q in range(len(keys)):
        ag_s[q * 8 : (q + 1) * 8] = ags[q]
    for s in range(S):
        step = step_ref[s]
        u = u_ref[s].astype(f32)
        ds = ds_ref[s]
        sums = s_s[s].reshape(LANE, C)
        dsp = ((q_s[s].reshape(LANE, C) + u * sums) * sigmoid_of_step(step)).astype(bf16)
        dsp_ref[s] = dsp
        du_ref[s] = step * sums + ds * vec_ref[1:2]
        p2_ref[s, 0, 0:LANE] = mm_t(dsp, proj_ref[...])
        for kind in range(2):
            for i in range(blocks):
                p2_ref[s, 0, LANE + 16 * kind + i : LANE + 16 * kind + i + 1] = r_s[s, kind, i, 0:1]
        sum_ref[0:1] += jnp.sum(dsp.astype(f32), axis=0, keepdims=True)
        sum_ref[1:2] += jnp.sum(ds * u, axis=0, keepdims=True)


def scan_specs(S, T, C, reverse):
    at = (lambda i: T // LANE - 1 - i) if reverse else (lambda i: i)
    return dict(
        packed=pl.BlockSpec((S, 1, LANE + 32, LANE), lambda i: (0, at(i), 0, 0)),
        block=pl.BlockSpec((S, LANE, C), lambda i: (0, at(i), 0)),
        masks=pl.BlockSpec((S, LANE, LANE), lambda i: (0, at(i), 0)),
        start=pl.BlockSpec((1, S * C // LANE * 16, LANE), lambda i: (at(i), 0, 0)),
    )


def scan_forward(packed, u, masks, proj_step, vec, rate2e, hot):
    S, T, C = u.shape
    G = C // LANE
    sp = scan_specs(S, T, C, False)
    by_token = pltpu.VMEM((S, LANE // 8, 8, C), f32)
    return pl.pallas_call(
        functools.partial(forward_kernel, S, G),
        grid=(T // LANE,),
        in_specs=[
            sp["packed"], sp["block"], sp["masks"], whole(LANE, C), whole(8, C), whole(G, 16, LANE), whole(LANE, 8 * LANE)
        ],
        out_specs=[sp["block"], sp["block"], sp["start"]],
        out_shape=[jax.ShapeDtypeStruct((S, T, C), f32)] * 2 + [jax.ShapeDtypeStruct((T // LANE, S * G * 16, LANE), f32)],
        scratch_shapes=[
            pltpu.VMEM((S * G * 16, LANE), f32),
            pltpu.VMEM((S, LANE // 8, 32, 8 * LANE), f32),
            pltpu.VMEM((LANE // 8, S, LANE, C), bf16),
            by_token,
            by_token,
        ],
        cost_estimate=cost(30),
        compiler_params=PARAMS,
    )(packed, u, masks, proj_step, vec, rate2e, hot)


def scan_backward(packed, u, step, ds, masks, proj_step, vec, rate2e, rate, hot, starts):
    S, T, C = u.shape
    G = C // LANE
    sp = scan_specs(S, T, C, True)
    by_token = pltpu.VMEM((S, LANE // 8, 8, C), f32)
    return pl.pallas_call(
        functools.partial(backward_kernel, S, G),
        grid=(T // LANE,),
        in_specs=[
            sp["packed"], sp["block"], sp["block"], sp["block"], sp["masks"], whole(LANE, C), whole(8, C),
            whole(G, 16, LANE), whole(G, 16, LANE), whole(LANE, 8 * LANE), sp["start"]
        ],
        out_specs=[sp["block"], sp["block"], sp["packed"], whole(16, C), whole(8, C)],
        out_shape=[
            jax.ShapeDtypeStruct((S, T, C), bf16),
            jax.ShapeDtypeStruct((S, T, C), f32),
            jax.ShapeDtypeStruct((S, T // LANE, LANE + 32, LANE), f32),
            jax.ShapeDtypeStruct((16, C), f32),
            jax.ShapeDtypeStruct((8, C), f32),
        ],
        scratch_shapes=[
            pltpu.VMEM((S * G * 16, LANE), f32),
            pltpu.VMEM((LANE + 1, S * G, 16, LANE), bf16),
            pltpu.VMEM((S, LANE // 8, 32, 8 * LANE), f32),
        ]
        + [by_token] * 5
        + [pltpu.VMEM((S, 2, LANE // 8, 8, LANE), f32)],
        cost_estimate=cost(85),
        compiler_params=PARAMS,
    )(packed, u, step, ds, masks, proj_step, vec, rate2e, rate.astype(bf16), hot, starts)


def after(*arrays):
    def kernel(*refs):
        refs[-1][0] = 0

    return pl.pallas_call(
        kernel,
        in_specs=[pl.BlockSpec(memory_space=pl.ANY) for _ in arrays],
        out_specs=pl.BlockSpec(memory_space=pltpu.SMEM),
        out_shape=jax.ShapeDtypeStruct((1,), jnp.int32),
    )(*arrays)[0]


def line_gather(array, axis):
    count = lax.axis_size(axis)
    right, left = array, array
    window = [array]
    for step in range(1, count):
        right = lax.ppermute(right, axis, [(i, i + 1) for i in range(step - 1, count - 1)])
        left = lax.ppermute(left, axis, [(i, i - 1) for i in range(1, count - step + 1)])
        window = [right] + window + [left]
    return window


def line_gather_at_once(array, axis):
    count = lax.axis_size(axis)
    return lax.all_to_all(jnp.broadcast_to(array[None], (count,) + array.shape), axis, 0, 0)


def line_scatter(blocks, axis):
    return jnp.sum(lax.all_to_all(blocks, axis, 0, 0).astype(f32), axis=0)


class Paired:
    def __init__(self):
        self.context = lax.axis_index("context")
        self.tensor = lax.axis_index("tensor")
        self.core = self.tensor % 2
        self.place = self.context[None]

    def across(self, array):
        return lax.ppermute(array, "context", [(0, 1), (1, 0)])

    def near(self, array):
        return lax.ppermute(array, "tensor", [(0, 1), (1, 0), (2, 3), (3, 2)])

    def far(self, array):
        return lax.ppermute(array, "tensor", [(0, 2), (2, 0), (1, 3), (3, 1)])

    def pieces(self, array, begin):
        half = array.shape[0] // 2
        mine = lax.dynamic_slice_in_dim(array, (self.core + begin) * half, half, 0)
        return self.across(mine), mine

    def pieces_done(self, array, block):
        return [array, joined_halves(block, self.near(block), self.core[None])]

    def normed(self, array, block, gain):
        return normalised_rows([array, block, self.near(block)], self.core[None], gain)

    def total(self, array, begin):
        half = array.shape[0] // 2
        mine = lax.dynamic_slice_in_dim(array, self.core * half, half, 0)
        other = lax.dynamic_slice_in_dim(array, (1 - self.core + begin) * half, half, 0).astype(bf16)
        mine = mine + self.near(other).astype(f32)
        first, second = mine[: half // 2], mine[half // 2 :]
        first = first + self.far(first.astype(bf16)).astype(f32)
        second = second + self.across(second.astype(bf16)).astype(f32)
        first = first + self.across(first.astype(bf16)).astype(f32)
        second = second + self.far(second.astype(bf16)).astype(f32)
        mine = jnp.concatenate([first, second], axis=0)
        other = self.near(mine.astype(bf16)).astype(f32)
        zero = self.core == 0
        return jnp.concatenate([jnp.where(zero, mine, other), jnp.where(zero, other, mine)])

    def share_begin(self, product):
        keep = product((self.tensor, self.tensor ^ 2))
        give = product((self.tensor ^ 1, self.tensor ^ 3))
        return [(k.astype(f32) + self.near(g).astype(f32)) for k, g in zip(keep, give)]

    def share_middle(self, sums):
        own, other = sums
        rows, width = own.shape
        half, width = rows // 2, width // 2
        far = self.far(jnp.stack([own[:half, width:], other[:half, width:]]).astype(bf16))
        across = self.across(other[half:].astype(bf16))
        first = own[:half, :width] + far[0].astype(f32)
        give = other[:half, :width] + far[1].astype(f32)
        second = own[half:] + across.astype(f32)
        return first, give, second

    def share_end(self, sums):
        first, give, second = sums
        width = first.shape[1]
        first = first + self.across(give.astype(bf16)).astype(f32)
        second = second[:, :width] + self.far(second[:, width:].astype(bf16)).astype(f32)
        return jnp.concatenate([first, second], axis=0)

    def row_total(self, array):
        array = array + self.near(array)
        return array + self.far(array)

    def vector_total(self, array):
        return self.row_total(array + self.across(array))

    def both(self, array):
        other = self.across(array)
        zero = self.context == 0
        return jnp.stack([jnp.where(zero, array, other), jnp.where(zero, other, array)])


class General:
    def __init__(self, seqs):
        self.seqs = seqs
        self.place = jnp.zeros((1,), jnp.int32)

    def pieces(self, array, begin):
        return lax.all_gather(array, "context", tiled=True), array

    def pieces_done(self, array, block):
        return [self.in_order([block], self.seqs).reshape(block.shape)]

    def normed(self, array, block, gain):
        inv_rms = normalised_rows([array], self.place, gain)[1]
        return normalised_rows(self.pieces_done(array, block), self.place, gain)[0], inv_rms

    def in_order(self, arrays, seqs):
        array = arrays[0].reshape(lax.axis_size("context"), seqs, -1, arrays[0].shape[-1])
        return array.swapaxes(0, 1).reshape(seqs, -1, array.shape[-1])

    def total(self, array, begin):
        return lax.psum(array, ("context", "tensor"))

    def share_begin(self, product):
        return [product((block,))[0].astype(f32) for block in range(lax.axis_size("tensor"))]

    def share_middle(self, sums):
        return sums

    def share_end(self, sums):
        parts = jnp.concatenate(sums, axis=-1)
        shape = parts.shape
        parts = parts.reshape(self.seqs, lax.axis_size("context"), -1, shape[-1]).swapaxes(0, 1).reshape(shape)
        parts = lax.psum_scatter(parts, "context", scatter_dimension=0, tiled=True)
        return lax.psum_scatter(parts, "tensor", scatter_dimension=1, tiled=True)

    def row_total(self, array):
        return lax.psum(array, "tensor")

    def vector_total(self, array):
        return lax.psum(array, ("context", "tensor"))

    def both(self, array):
        return lax.all_gather(array, "context")


def dot(a, b, out=f32):
    return jnp.dot(a, b, preferred_element_type=f32).astype(out)


def dot_t(a, b, out=f32):
    return lax.dot_general(a, b, (((1,), (1,)), ((), ())), preferred_element_type=f32).astype(out)


def t_dot(a, b, out=f32):
    return lax.dot_general(a, b, (((0,), (0,)), ((), ())), preferred_element_type=f32).astype(out)


def on_device(
    block_input,
    output_grad,
    doc_lengths,
    norm_gain,
    input_proj,
    conv_weight,
    conv_bias,
    select_proj,
    step_proj,
    step_bias,
    decay_log,
    skip_weight,
    output_proj,
):
    seqs, piece, model_width = block_input.shape
    shards, contexts, tensors = (lax.axis_size(axis) for axis in ("shards", "context", "tensor"))
    shard, context, tensor = (lax.axis_index(axis) for axis in ("shards", "context", "tensor"))
    moves = Paired() if (contexts, tensors) == (2, 4) else General(seqs)
    length = piece * contexts
    tokens = seqs * length
    depth = input_proj.shape[0]
    part = conv_weight.shape[0] // contexts
    inner = part * shards
    states = decay_log.shape[1]
    rank = step_proj.shape[0] * shards
    selected = select_proj.shape[1]
    taps = conv_weight.shape[1]
    share_width = model_width // tensors

    def mine(array):
        return lax.dynamic_slice_in_dim(array, context * part, part, 0)

    def my_columns(array, begin):
        blocks = [
            lax.dynamic_slice_in_dim(array, (block * contexts + context + begin) * part, part, array.ndim - 1)
            for block in range(shards)
        ]
        return jnp.concatenate(blocks, axis=-1)

    rows_flat = block_input.reshape(seqs * piece, model_width)
    row_block, row_slice = moves.pieces(rows_flat, 0)
    in_x = my_columns(input_proj[:, 0], after(row_slice))
    bounds = jnp.cumsum(doc_lengths, axis=-1)[:, :2, None, None]
    position, lane = (lax.broadcasted_iota(jnp.int32, (1, length, LANE), axis) for axis in (1, 2))
    other = jnp.where(lane < taps, position - lane, position + lane - taps)

    def document(at):
        return (at >= bounds[:, 0]).astype(jnp.int32) + (at >= bounds[:, 1]).astype(jnp.int32)

    masks = (document(position) == document(other)) & (other >= 0) & (other < length)
    masks = masks.astype(f32)

    vectors = jnp.concatenate(
        [
            mine(select_proj),
            mine(conv_weight),
            mine(decay_log),
            mine(conv_bias)[:, None],
            mine(step_bias)[:, None],
            mine(skip_weight)[:, None],
        ],
        axis=1,
    )
    vectors = jnp.pad(vectors, ((0, 0), (0, 2 * LANE - vectors.shape[1])))
    flat = [in_x, my_columns(step_proj, 0), vectors.reshape(-1, inner), norm_gain.reshape(-1, inner)]
    flat = [jnp.pad(f, ((0, -f.shape[0] % 16), (0, 0))) for f in flat]
    window = line_gather(jnp.concatenate(flat, axis=0), "shards")
    proj_x, proj_step, vectors, gain = unpacked(window, [f.shape[0] for f in flat], shard[None], masks)
    gain = gain[:, : norm_gain.shape[0] // inner].reshape(model_width).astype(f32)
    normed, inv_rms = moves.normed(rows_flat, row_block, gain)
    proj_x = proj_x.reshape(model_width, inner)
    proj_step = proj_step[:, : step_proj.shape[0]].reshape(rank, inner)
    vectors = vectors[:, : 2 * LANE * part // inner].reshape(inner, 2 * LANE)
    proj_select = vectors[:, :selected]
    rest = vectors[:, selected:].astype(f32)
    decay_rate = -jnp.exp(rest[:, taps : taps + states])
    at = taps + states
    conv_vec = jnp.concatenate([rest[:, :taps].T, rest[:, at][None], jnp.zeros((7 - taps, inner), f32)], axis=0)
    scan_vec = jnp.concatenate([rest[:, at + 1 : at + 3].T, jnp.zeros((6, inner), f32)], axis=0)
    select_low, select_state = proj_select[:, :rank], proj_select[:, rank:]

    grad_flat = output_grad.reshape(seqs * piece, model_width)

    in_z = my_columns(input_proj[:, 1], after(window[len(window) // 2 - 1]))
    out_own = mine(output_proj)
    out_own = [out_own[:, i * inner : (i + 1) * inner] for i in range(model_width // inner)]
    others = jnp.concatenate([in_z] + out_own + [jnp.zeros((16, inner), bf16)], axis=0)
    others = lax.dynamic_slice_in_dim(others, after(proj_x) * 16, others.shape[0] - 16, 0)
    others = line_gather_at_once(others, "shards")

    x_part, values, projected = convolve(
        normed, proj_x, conv_vec, masks, select_low, select_state.T, moves.place, taps
    )

    def total(packed, begin):
        return moves.total(packed.reshape(-1, LANE), begin).reshape(packed.shape)

    projected = total(projected, 0)
    grad_block = moves.pieces(grad_flat, after(row_block))[0]

    hot = hot_rows()

    def by_group(array, begin=0.0):
        return (array.T + begin).reshape(states, inner // LANE, LANE).swapaxes(0, 1)

    ssm_out, step, starts = scan_forward(
        projected, values, masks, proj_step, scan_vec, by_group(decay_rate * LOG2E), hot
    )

    proj_z = others[:, :depth].reshape(model_width, inner)
    proj_out = [others[:, depth + i * part : depth + (i + 1) * part] for i in range(model_width // inner)]
    proj_out = jnp.concatenate(proj_out, axis=-1).reshape(inner, model_width)
    grad_all = moves.pieces_done(grad_flat, grad_block)
    gated, grad_z, grad_ssm = gates(normed, grad_all, proj_z, proj_out, ssm_out, moves.place)

    def weight_grad(lefts, rights):
        if not isinstance(rights, list):
            lefts, rights = ([a.reshape(-1, a.shape[-1])] for a in (lefts, rights))
        return sum(t_dot(a, b) for a, b in zip(lefts, rights)).astype(bf16)

    early = lax.all_to_all(weight_grad(normed, grad_z).reshape(shards, depth, inner), "shards", 0, 0)
    middle = lax.all_to_all(weight_grad(gated, grad_all).reshape(shards, part, model_width), "shards", 0, 0)
    def chosen(weights, blocks, axis, begin=0):
        return jnp.concatenate(
            [lax.dynamic_slice_in_dim(weights, (b + begin) * share_width, share_width, axis) for b in blocks], axis
        )

    out_sums = moves.share_begin(lambda blocks: [dot(gated[i], chosen(proj_out, blocks, 1), bf16) for i in range(gated.shape[0])])
    out_sums_2 = moves.share_middle(out_sums)
    out_share = moves.share_end(out_sums_2)
    own_columns = tensor * share_width
    input_share = lax.dynamic_slice_in_dim(block_input, own_columns, share_width, 2).astype(f32)
    block_output = (input_share + out_share.reshape(input_share.shape)).astype(bf16)

    grad_step_pre, grad_direct, partial_grad, grad_decay, scan_sums = scan_backward(
        projected,
        values,
        step,
        grad_ssm,
        masks,
        proj_step,
        scan_vec,
        by_group(decay_rate * LOG2E),
        by_group(decay_rate, after(*out_sums).astype(f32)),
        hot,
        starts,
    )
    grad_decay_log = grad_decay.T * decay_rate
    step_low = projected[:, :, :rank].reshape(tokens, rank).astype(bf16)
    grad_step_proj = t_dot(step_low, grad_step_pre.reshape(tokens, inner))
    pulled = after(early, partial_grad, *out_sums_2)
    grad_in_z = jnp.sum(early.astype(f32), axis=0) + pulled.astype(f32)
    z_pair = moves.both(grad_in_z.astype(bf16))
    partial_grad = total(partial_grad, pulled)

    grad_x, conv_sums, grad_selected = convolve_back(
        partial_grad,
        grad_direct,
        x_part,
        conv_vec + after(block_output, partial_grad).astype(f32),
        masks,
        select_low,
        jnp.pad(select_state, ((0, 0), (0, LANE - select_state.shape[1]))),
        moves.place,
        normed.shape[0],
        taps,
    )
    grad_select = t_dot(values.reshape(tokens, inner), grad_selected.reshape(tokens, -1))[:, :selected]

    small = jnp.concatenate(
        [
            grad_select,
            conv_sums[:taps].T,
            grad_decay_log,
            conv_sums[taps][:, None],
            scan_sums[:2].T,
        ],
        axis=1,
    ).astype(bf16)
    sent = after(middle, conv_sums)
    small = small + sent.astype(bf16)
    out_pair = moves.both((jnp.sum(middle.astype(f32), axis=0) + sent.astype(f32)).astype(bf16))
    small = jnp.pad(small, ((0, 0), (0, 2 * LANE - small.shape[1])))
    late_local = jnp.concatenate(
        [
            weight_grad(normed, grad_x).reshape(shards, depth, inner),
            grad_step_proj.astype(bf16).reshape(shards, -1, inner),
            small.reshape(shards, -1, inner),
        ],
        axis=1,
    )
    begin = after(late_local, z_pair)

    def normed_part(blocks):
        blocks = jnp.stack([jnp.asarray(b, jnp.int32) + begin for b in blocks])
        return products(grad_x, grad_z, proj_x, proj_z, blocks, share_width)

    grad_normed = moves.share_end(moves.share_middle(moves.share_begin(normed_part))).reshape(seqs, piece, share_width)
    inv_rms = inv_rms[:, :1].reshape(seqs, piece, 1)
    unit_share = input_share * inv_rms
    weighted = grad_normed * lax.dynamic_slice_in_dim(gain, own_columns, share_width, 0)
    row_dots = moves.row_total(jnp.sum(unit_share * weighted, axis=-1))[:, :, None]
    grad_share = lax.dynamic_slice_in_dim(output_grad, own_columns, share_width, 2).astype(f32)
    input_grad = grad_share + inv_rms * (weighted - unit_share * (row_dots / model_width))

    late = line_scatter(late_local, "shards") + after(grad_normed, z_pair, out_pair).astype(f32)
    grad_in_x = late[:depth]
    gain_part = jnp.sum(in_x.astype(f32) * grad_in_x, axis=1) + jnp.sum(in_z.astype(f32) * grad_in_z, axis=1)
    grad_gain = moves.vector_total(gain_part) / norm_gain.astype(f32)

    def columns_of(pair):
        pair = pair.astype(f32).reshape(pair.shape[:-1] + (shards, part))
        return jnp.moveaxis(pair, 0, -2).reshape(pair.shape[1], -1)

    late = moves.both(late.astype(bf16))
    grad_in = interleaved(late, z_pair, depth, part)
    grad_step_proj = columns_of(late[:, depth : depth + step_proj.shape[0]])
    small = late[:, depth + step_proj.shape[0] :].reshape(contexts * part, 2 * LANE).astype(f32)
    grad_out_proj = out_pair.reshape(contexts * part, model_width).astype(f32)
    at = selected + taps + states
    return (
        block_output,
        input_grad,
        grad_gain,
        grad_in,
        small[:, selected : selected + taps],
        small[:, at],
        small[:, :selected],
        grad_step_proj,
        small[:, at + 1],
        small[:, selected + taps : at],
        small[:, at + 2],
        grad_out_proj,
    )


def solution(mesh):
    placed = (
        P("shards", "context", None),
        P("shards", "context", None),
        P("shards", None),
        P("shards"),
        P("shards", None, "tensor"),
        P(("tensor", "shards"), None),
        P(("tensor", "shards")),
        P(("tensor", "shards"), None),
        P("shards", "tensor"),
        P(("tensor", "shards")),
        P(("tensor", "shards"), None),
        P(("tensor", "shards")),
        P(("tensor", "shards"), None),
    )
    return jax.shard_map(
        on_device,
        mesh=mesh,
        in_specs=placed,
        out_specs=(
            P("shards", "context", "tensor"),
            P("shards", "context", "tensor"),
            P("shards"),
            P("shards", None, "tensor"),
            P(("tensor", "shards"), None),
            P(("tensor", "shards")),
            P(("tensor", "shards"), None),
            P("shards", "tensor"),
            P(("tensor", "shards")),
            P(("tensor", "shards"), None),
            P(("tensor", "shards")),
            P(("tensor", "shards"), None),
        ),
        check_vma=False,
    )
```

```python
import functools

import jax
import jax.numpy as jnp
from jax import lax
from jax.experimental import pallas as pl
from jax.experimental.pallas import tpu as pltpu
from jax.sharding import PartitionSpec as P

EPS = 1e-05
LANE = 128
LOG2E = 1.4426950408889634
BREAK = 1e6
f32 = jnp.float32
bf16 = jnp.bfloat16


def row8(ref, s, i, k, g):
    return jnp.broadcast_to(ref[s, i, k : k + 1, g * LANE : (g + 1) * LANE], (8, LANE))


def mm(a, b):
    return jnp.dot(a, b, preferred_element_type=f32)


def mm_t(a, b):
    return lax.dot_general(a, b, (((1,), (1,)), ((), ())), preferred_element_type=f32)


def iota(shape, axis):
    return lax.broadcasted_iota(jnp.int32, shape, axis)


def cost(us):
    return pl.CostEstimate(flops=int(us * 1.15e8), bytes_accessed=int(us * 3.6e5), transcendentals=0)


PARAMS = pltpu.CompilerParams(vmem_limit_bytes=58 << 20)


def whole(*shape):
    return pl.BlockSpec(shape, lambda *_: (0,) * len(shape))


def joined_halves(first, second, place):
    half, width = first.shape
    size = min(half, 128)
    count = half // size

    def kernel(place_ref, first_ref, second_ref, out_ref):
        this = (pl.program_id(0) // count) == place_ref[0]

        def put(ref):
            out_ref[...] = ref[...]

        @pl.when(this)
        def _():
            put(first_ref)

        @pl.when(jnp.logical_not(this))
        def _():
            put(second_ref)

    def spec(which):
        def index(i, place):
            start = (place[0] ^ which) * count
            return (jnp.clip(i - start, 0, count - 1), 0)

        return pl.BlockSpec((size, width), index)

    return pl.pallas_call(
        kernel,
        grid_spec=pltpu.PrefetchScalarGridSpec(
            num_scalar_prefetch=1,
            grid=(2 * count,),
            in_specs=[spec(0), spec(1)],
            out_specs=pl.BlockSpec((size, width), lambda i, place: (i, 0)),
        ),
        out_shape=jax.ShapeDtypeStruct((2 * half, width), bf16),
        cost_estimate=cost(4),
        compiler_params=PARAMS,
    )(place, first, second)


def normalised_rows(blocks, place, gain):
    count, width = blocks[0].shape
    size = min(count, 256)
    per = count // size
    half = per // 2
    n = 1 if len(blocks) == 1 else 2

    def kernel(place_ref, *refs):
        ins, (gain_ref, out_ref, inv_ref) = refs[: len(blocks)], refs[len(blocks) :]
        i = pl.program_id(0)

        def inverse(ref):
            wide = ref[...].astype(f32)
            inv_rms = lax.rsqrt(jnp.mean(wide * wide, axis=-1, keepdims=True) + EPS)
            out_ref[0] = (wide * inv_rms * gain_ref[...]).astype(bf16)
            return inv_rms

        @pl.when(i < per)
        def _():
            inv_ref[...] = jnp.broadcast_to(inverse(ins[0]), inv_ref.shape)

        for which, ref in enumerate(ins[1:]):
            start = per + (place_ref[0] ^ which) * half

            @pl.when((i >= start) & (i < start + half))
            def _(ref=ref):
                inverse(ref)

    def spec(which):
        def index(i, place):
            if which == 0:
                return (jnp.minimum(i, per - 1), 0)
            return (jnp.clip(i - per - (place[0] ^ (which - 1)) * half, 0, half - 1), 0)

        return pl.BlockSpec((size, width), index)

    return pl.pallas_call(
        kernel,
        grid_spec=pltpu.PrefetchScalarGridSpec(
            num_scalar_prefetch=1,
            grid=(n * per,),
            in_specs=[spec(i) for i in range(len(blocks))] + [whole(1, width)],
            out_specs=[
                pl.BlockSpec((1, size, width), lambda i, place: (i // per, lax.rem(i, per), 0)),
                pl.BlockSpec((size, LANE), lambda i, place: (jnp.minimum(i, per - 1), 0)),
            ],
        ),
        out_shape=[jax.ShapeDtypeStruct((n, count, width), bf16), jax.ShapeDtypeStruct((count, LANE), f32)],
        cost_estimate=cost(8),
        compiler_params=PARAMS,
    )(place, *blocks, gain.reshape(1, width))


def unpacked(window, counts, place, *before):
    slots = len(window)
    count = (slots + 1) // 2
    width = window[0].shape[1]
    starts = [sum(counts[:i]) for i in range(len(counts))]

    def kernel(place_ref, *refs):
        ins, outs = refs[:slots], refs[slots + len(before) :]
        wanted = pl.program_id(0) + count - 1 - place_ref[0]
        for slot, ref in enumerate(ins):

            @pl.when(wanted == slot)
            def _(ref=ref):
                for out, start, rows in zip(outs, starts, counts):
                    out[0] = ref[start : start + rows]

    return pl.pallas_call(
        kernel,
        grid_spec=pltpu.PrefetchScalarGridSpec(
            num_scalar_prefetch=1,
            grid=(count,),
            in_specs=[whole(*window[0].shape) for _ in window] + [pl.BlockSpec(memory_space=pl.ANY) for _ in before],
            out_specs=[pl.BlockSpec((1, rows, width), lambda j, place: (j, 0, 0)) for rows in counts],
        ),
        out_shape=[jax.ShapeDtypeStruct((count, rows, width), bf16) for rows in counts],
        cost_estimate=cost(3),
        compiler_params=PARAMS,
    )(place, *window, *before)


def products(lefts, more_lefts, right, more_right, blocks, width):
    n, count, inner = lefts.shape
    size = min(count, 512)

    def kernel(blocks_ref, *refs):
        a, b, (w, v), outs = refs[:n], refs[n : 2 * n], refs[2 * n : 2 * n + 2], refs[2 * n + 2 :]
        for i in range(n):
            outs[i][...] = (mm_t(a[i][0], w[...]) + mm_t(b[i][0], v[...])).astype(bf16)

    rows = [pl.BlockSpec((1, size, inner), lambda j, i, blocks, which=which: (which, i, 0)) for which in range(n)]
    weights = pl.BlockSpec((width, inner), lambda j, i, blocks: (blocks[j], 0))
    return pl.pallas_call(
        kernel,
        grid_spec=pltpu.PrefetchScalarGridSpec(
            num_scalar_prefetch=1,
            grid=(blocks.shape[0], count // size),
            in_specs=rows * 2 + [weights] * 2,
            out_specs=[pl.BlockSpec((size, width), lambda j, i, blocks: (i, j))] * n,
        ),
        out_shape=[jax.ShapeDtypeStruct((count, width * blocks.shape[0]), bf16)] * n,
        cost_estimate=cost(0),
        compiler_params=PARAMS,
    )(blocks, *[lefts] * n, *[more_lefts] * n, right, more_right)


def interleaved(first, second, depth, part):
    contexts, _, inner = first.shape
    shards = inner // part
    size = 64

    def kernel(a_ref, b_ref, out_ref):
        for which, ref in enumerate((a_ref, b_ref)):
            columns = [
                ref[c, :, s * part : (s + 1) * part].astype(f32) for s in range(shards) for c in range(contexts)
            ]
            out_ref[:, which, :] = jnp.concatenate(columns, axis=1)

    return pl.pallas_call(
        kernel,
        grid=(depth // size,),
        in_specs=[pl.BlockSpec((contexts, size, inner), lambda i: (0, i, 0))] * 2,
        out_specs=pl.BlockSpec((size, 2, contexts * inner), lambda i: (i, 0, 0)),
        out_shape=jax.ShapeDtypeStruct((depth, 2, contexts * inner), f32),
        cost_estimate=cost(5),
        compiler_params=PARAMS,
    )(first, second)


class Rows:
    def __init__(self, seqs, length, arrays, size, reverse=False):
        self.pieces = arrays
        self.size = size
        self.count = length // size
        self.per = self.count // arrays
        self.grid = (seqs, self.count)
        self.reverse = reverse

    def at(self, i):
        return self.count - 1 - i if self.reverse else i

    def spec(self, which, width):
        def index(s, i, place):
            low = (place[0] ^ which) * self.per
            return (s * self.per + jnp.clip(self.at(i) - low, 0, self.per - 1), 0)

        return pl.BlockSpec((self.size, width), index)

    def stacked(self, width):
        def index(s, i, place):
            turn = self.at(i) // self.per
            return (turn ^ place[0] if self.pieces > 1 else turn, s * self.per + lax.rem(self.at(i), self.per), 0)

        return pl.BlockSpec((1, self.size, width), index)

    def is_turn(self, which, place_ref):
        return (self.at(pl.program_id(1)) // self.per) == (place_ref[0] ^ which)

    def block(self, width):
        return pl.BlockSpec((1, self.size, width), lambda s, i, place: (s, self.at(i), 0))

    def packed(self, rows):
        return pl.BlockSpec((1, self.size // LANE, rows, LANE), lambda s, i, place: (s, self.at(i), 0, 0))


def convolved(xs, masks_ref, vec_ref, size, taps):
    total = vec_ref[taps : taps + 1]
    for by in range(taps):
        term = xs[8 - by : 8 - by + size] * vec_ref[taps - 1 - by : taps - by]
        total = total + (term * masks_ref[0, :, by : by + 1] if by else term)
    return total


def convolve(normed, proj_x, vec, masks, select_low, select_state, place, taps):
    seqs, length = masks.shape[:2]
    width, inner = proj_x.shape
    size = min(256, length)
    rows = Rows(seqs, length, normed.shape[0], size)
    packed = select_low.shape[1] + select_state.shape[0]

    def kernel(place_ref, in_ref, w_ref, vec_ref, masks_ref, low_ref, state_ref, x_ref, u_ref, p_ref, xs):
        fresh = pl.program_id(1) == 0

        @pl.when(fresh)
        def _():
            xs[0:8] = jnp.zeros((8, inner), f32)

        @pl.when(jnp.logical_not(fresh))
        def _():
            xs[0:8] = xs[size : size + 8]

        x = mm(in_ref[0], w_ref[...]).astype(bf16)
        x_ref[0] = x
        xs[8 : 8 + size] = x.astype(f32)
        pre = convolved(xs, masks_ref, vec_ref, size, taps)
        u = (pre / (1.0 + jnp.exp(-pre))).astype(bf16)
        u_ref[0] = u
        low = mm(u, low_ref[...])
        state = mm_t(state_ref[...], u)
        for j in range(size // LANE):
            p_ref[0, j, 0:LANE] = low[j * LANE : (j + 1) * LANE]
            p_ref[0, j, LANE:packed] = state[:, j * LANE : (j + 1) * LANE]

    return pl.pallas_call(
        kernel,
        grid_spec=pltpu.PrefetchScalarGridSpec(
            num_scalar_prefetch=1,
            grid=rows.grid,
            in_specs=[rows.stacked(width)]
            + [whole(width, inner), whole(8, inner), rows.block(LANE), whole(*select_low.shape), whole(*select_state.shape)],
            out_specs=[rows.block(inner), rows.block(inner), rows.packed(packed)],
            scratch_shapes=[pltpu.VMEM((size + 8, inner), f32)],
        ),
        out_shape=[
            jax.ShapeDtypeStruct((seqs, length, inner), bf16),
            jax.ShapeDtypeStruct((seqs, length, inner), bf16),
            jax.ShapeDtypeStruct((seqs, length // LANE, packed, LANE), f32),
        ],
        cost_estimate=cost(9),
        compiler_params=PARAMS,
    )(place, normed, proj_x, vec, masks, select_low, select_state)


def gates(normed, grads, proj_z, proj_out, ssm_out, place):
    seqs, length, inner = ssm_out.shape
    width = proj_z.shape[0]
    size = min(256, length)
    n = len(grads)
    rows = Rows(seqs, length, n, size)

    def kernel(place_ref, a_ref, *refs):
        g_refs, (z_ref, o_ref, s_ref, gated_ref, grad_z_ref, grad_ref) = refs[:n], refs[n:]
        for which in range(n):

            @pl.when(rows.is_turn(which, place_ref))
            def _(which=which):
                z = mm(a_ref[0], z_ref[...]).astype(bf16).astype(f32)
                grad = mm_t(g_refs[which][...], o_ref[...])
                ssm = s_ref[0]
                sigmoid = 1.0 / (1.0 + jnp.exp(-z))
                gate = z * sigmoid
                gated_ref[0] = (ssm * gate).astype(bf16)
                grad_z_ref[0] = (grad * ssm * sigmoid * (1.0 + z * (1.0 - sigmoid))).astype(bf16)
                grad_ref[0] = grad * gate

    total = seqs * length // n
    return pl.pallas_call(
        kernel,
        grid_spec=pltpu.PrefetchScalarGridSpec(
            num_scalar_prefetch=1,
            grid=rows.grid,
            in_specs=[rows.stacked(width)]
            + [rows.spec(i, width) for i in range(n)]
            + [whole(width, inner), whole(inner, width), rows.block(inner)],
            out_specs=[rows.stacked(inner)] * 2 + [rows.block(inner)],
        ),
        out_shape=[jax.ShapeDtypeStruct((n, total, inner), bf16)] * 2 + [jax.ShapeDtypeStruct((seqs, length, inner), f32)],
        cost_estimate=cost(14),
        compiler_params=PARAMS,
    )(place, normed, *grads, proj_z, proj_out, ssm_out)


def convolve_back(packed, direct, x_part, vec, masks, select_low, select_state, place, n, taps):
    seqs, length, inner = x_part.shape
    size = min(256, length)
    rows = Rows(seqs, length, n, size, reverse=True)
    states = (packed.shape[2] - LANE) // 2

    def kernel(place_ref, p_ref, d_ref, x_ref, edge_ref, vec_ref, masks_ref, low_ref, state_ref, *rest):
        out_ref, sum_ref, tok_ref, xs, ds = rest
        fresh = pl.program_id(1) == 0

        @pl.when(jnp.logical_and(fresh, pl.program_id(0) == 0))
        def _():
            sum_ref[...] = jnp.zeros_like(sum_ref)

        @pl.when(fresh)
        def _():
            ds[size : size + 8] = jnp.zeros((8, inner), f32)

        @pl.when(jnp.logical_not(fresh))
        def _():
            ds[size : size + 8] = ds[0:8]

        copy = (iota((LANE, 16), 0) // 8 == iota((LANE, 16), 1)).astype(bf16)
        place_of = (iota((LANE, LANE), 1) // 16) == lax.rem(iota((LANE, LANE), 0), 8)
        by_state = lax.rem(iota((LANE, LANE), 0), 16)
        for j in range(size // LANE):
            at = slice(j * LANE, (j + 1) * LANE)
            tok_ref[0, at, 0:LANE] = p_ref[0, j, 0:LANE].astype(bf16)
            token = jnp.zeros((LANE, LANE), f32)
            for q in range(2):
                part = p_ref[0, j, LANE + q * states : LANE + (q + 1) * states].astype(bf16)
                spread = jnp.where(place_of, mm(copy, part), 0.0).astype(bf16)
                token = token + mm(spread, (by_state + q * states == iota((LANE, LANE), 1)).astype(bf16))
            tok_ref[0, at, LANE : 2 * LANE] = token.astype(bf16)
        xs[0:8] = edge_ref[0, 8:16].astype(f32)
        xs[8 : 8 + size] = x_ref[0].astype(f32)
        pre = convolved(xs, masks_ref, vec_ref, size, taps)
        sigmoid = 1.0 / (1.0 + jnp.exp(-pre))
        grad = mm_t(tok_ref[0, :, 0:LANE], low_ref[...]) + mm_t(tok_ref[0, :, LANE : 2 * LANE], state_ref[...]) + d_ref[0]
        grad = grad * sigmoid * (1.0 + pre * (1.0 - sigmoid))
        ds[0:size] = grad
        total = grad * vec_ref[taps - 1 : taps]
        sum_ref[taps : taps + 1] += jnp.sum(grad, axis=0, keepdims=True)
        sum_ref[taps - 1 : taps] += jnp.sum(grad * xs[8 : 8 + size], axis=0, keepdims=True)
        for by in range(1, taps):
            tap = taps - 1 - by
            total = total + ds[by : by + size] * masks_ref[0, :, taps + by : taps + by + 1] * vec_ref[tap : tap + 1]
            joint = grad * xs[8 - by : 8 - by + size] * masks_ref[0, :, by : by + 1]
            sum_ref[tap : tap + 1] += jnp.sum(joint, axis=0, keepdims=True)
        out_ref[0] = total.astype(bf16)

    edge = pl.BlockSpec((1, 16, inner), lambda s, i, place: (s, jnp.maximum(rows.at(i) * (size // 16) - 1, 0), 0))
    return pl.pallas_call(
        kernel,
        grid_spec=pltpu.PrefetchScalarGridSpec(
            num_scalar_prefetch=1,
            grid=rows.grid,
            in_specs=[
                rows.packed(packed.shape[2]),
                rows.block(inner),
                rows.block(inner),
                edge,
                whole(8, inner),
                rows.block(LANE),
                whole(inner, LANE),
                whole(inner, LANE),
            ],
            out_specs=[rows.stacked(inner), whole(8, inner), rows.block(2 * LANE)],
            scratch_shapes=[pltpu.VMEM((size + 8, inner), f32)] * 2,
        ),
        out_shape=[jax.ShapeDtypeStruct((n, seqs * length // n, inner), bf16)]
        + [jax.ShapeDtypeStruct((8, inner), f32), jax.ShapeDtypeStruct((seqs, length, 2 * LANE), bf16)],
        cost_estimate=cost(160),
        compiler_params=PARAMS,
    )(place, packed, direct, x_part, x_part, vec, masks, select_low, select_state)


def log_one_plus(v):
    small = v * (1.0 - v * (0.5 - v * (1.0 / 3.0 - v * 0.25)))
    return jnp.where(v < 0.01, small, jnp.log(1.0 + v))


def softplus(v):
    return jnp.maximum(v, 0.0) + log_one_plus(jnp.exp(-jnp.abs(v)))


def sigmoid_of_step(step):
    small = step * (1.0 - step * (0.5 - step * (1.0 / 6.0 - step * (1.0 / 24.0))))
    return jnp.where(step < 0.02, small, 1.0 - jnp.exp(-step))


def hot_rows():
    row, col = iota((LANE, 8 * LANE), 0), iota((LANE, 8 * LANE), 1)
    return ((lax.rem(row, 8) == col // LANE) & (row < 16)).astype(bf16)


def spread(state, hot, wide, s, blocks):
    high = state.astype(bf16).astype(f32)
    rest = state - high
    lane = iota(state.shape, 1)
    parts = []
    for i in range(blocks):
        a = pltpu.roll(high, (LANE - 8 * i) % LANE, 1)
        b = pltpu.roll(rest, (LANE + 8 - 8 * i) % LANE, 1)
        parts.append(jnp.where(lane < 8, a, b).astype(bf16))
    wide[s] = mm(jnp.concatenate(parts, axis=0), hot).reshape(blocks, state.shape[0], 8 * LANE)


def forward_kernel(
    S, G, p_ref, u_ref, masks_ref, proj_ref, vec_ref, rate_ref, hot_ref, y_ref, step_ref, start_ref, h_s, wide, w_s, se_s, su_s
):
    blocks = LANE // 8
    C = G * LANE

    @pl.when(pl.program_id(0) == 0)
    def _():
        h_s[...] = jnp.zeros_like(h_s)

    start_ref[0] = h_s[...]
    for s in range(S):
        step = softplus(mm(p_ref[s, 0, 0:LANE].astype(bf16), proj_ref[...]) + vec_ref[0:1])
        step_ref[s] = step
        u = u_ref[s].astype(f32)
        se_s[s] = jnp.where(masks_ref[s, :, 1:2] > 0.5, step, BREAK).reshape(blocks, 8, C)
        su_s[s] = (step * u).reshape(blocks, 8, C)
        spread(p_ref[s, 0, LANE : LANE + 32], hot_ref[...], wide, s, blocks)
    keys = [(s, g, j) for s in range(S) for g in range(G) for j in range(2)]

    def body(i, carry):
        hs = dict(zip(keys, carry))
        for k in range(8):
            for s in range(S):
                lanes = slice(k * LANE, (k + 1) * LANE)
                b = [wide[s, i, j * 8 : (j + 1) * 8, lanes] for j in range(2)]
                c = [wide[s, i, 16 + j * 8 : 16 + (j + 1) * 8, lanes] for j in range(2)]
                for g in range(G):
                    se, su = row8(se_s, s, i, k, g), row8(su_s, s, i, k, g)
                    prod = []
                    for j in range(2):
                        a = jnp.exp2(se * rate_ref[g, j * 8 : (j + 1) * 8])
                        hs[s, g, j] = a * hs[s, g, j] + su * b[j]
                        prod.append(c[j] * hs[s, g, j])
                    w_s[i, s, k * 16 : (k + 1) * 16, g * LANE : (g + 1) * LANE] = jnp.concatenate(prod, 0).astype(bf16)
        return tuple(hs.values())

    out = lax.fori_loop(0, blocks, body, tuple(h_s[q * 8 : (q + 1) * 8] for q in range(len(keys))))
    pick = (iota((16, 2 * LANE), 0) == iota((16, 2 * LANE), 1) // 16).astype(bf16)
    for s in range(S):
        for i in range(blocks // 2):
            both = jnp.concatenate([w_s[2 * i, s], w_s[2 * i + 1, s]], axis=0)
            y_ref[s, i * 16 : (i + 1) * 16] = mm(pick, both)
        y_ref[s] = y_ref[s] + vec_ref[1:2] * u_ref[s].astype(f32)
    for q in range(len(keys)):
        h_s[q * 8 : (q + 1) * 8] = out[q]


def backward_kernel(
    S, G, p_ref, u_ref, step_ref, ds_ref, masks_ref, proj_ref, vec_ref, rate_ref, rate2_ref, hot_ref, start_ref,
    dsp_ref, du_ref, p2_ref, dlog_ref, sum_ref, ag_s, h_s, wide, se_s, su_s, s_s, q_s, d_s, r_s
):
    blocks = LANE // 8
    C = G * LANE
    keys = [(s, g, j) for s in range(S) for g in range(G) for j in range(2)]

    @pl.when(pl.program_id(0) == 0)
    def _():
        ag_s[...] = jnp.zeros_like(ag_s)
        dlog_ref[...] = jnp.zeros_like(dlog_ref)
        sum_ref[...] = jnp.zeros_like(sum_ref)

    for s in range(S):
        step = step_ref[s]
        u = u_ref[s].astype(f32)
        se_s[s] = jnp.where(masks_ref[s, :, 1:2] > 0.5, step, BREAK).reshape(blocks, 8, C)
        su_s[s] = (step * u).reshape(blocks, 8, C)
        d_s[s] = ds_ref[s].reshape(blocks, 8, C)
        spread(p_ref[s, 0, LANE : LANE + 32], hot_ref[...], wide, s, blocks)

    def again(i, carry):
        hs = dict(zip(keys, carry))
        for k in range(8):
            for s in range(S):
                b = [wide[s, i, j * 8 : (j + 1) * 8, k * LANE : (k + 1) * LANE] for j in range(2)]
                for g in range(G):
                    se, su = row8(se_s, s, i, k, g), row8(su_s, s, i, k, g)
                    h_s[i * 8 + k, s * G + g] = jnp.concatenate([hs[s, g, 0], hs[s, g, 1]], 0).astype(bf16)
                    for j in range(2):
                        a = jnp.exp2(se * rate_ref[g, j * 8 : (j + 1) * 8])
                        hs[s, g, j] = a * hs[s, g, j] + su * b[j]
        return tuple(hs.values())

    out = lax.fori_loop(0, blocks, again, tuple(start_ref[0, q * 8 : (q + 1) * 8] for q in range(len(keys))))
    for s in range(S):
        for g in range(G):
            q = (s * G + g) * 2
            h_s[LANE, s * G + g] = jnp.concatenate([out[q], out[q + 1]], 0).astype(bf16)

    def two(v):
        return jnp.concatenate([v, v], 0).astype(bf16)

    pick = (iota((16, 2 * LANE), 0) == iota((16, 2 * LANE), 1) // 16).astype(bf16)
    fold = (lax.rem(iota((16, 2 * LANE), 1), 16) == iota((16, 2 * LANE), 0)).astype(bf16)
    one = jnp.ones((16, LANE), bf16)
    lane, row = iota((8, LANE), 1), iota((8, LANE), 0)

    def across_rows(product):
        found = product[0:8]
        for v in range(1, 16):
            found = jnp.where(lane >= 8 * v, product[8 * v : 8 * v + 8], found)
        found = jnp.sum(jnp.where(lax.rem(lane, 8) == row, found, 0.0), axis=0, keepdims=True)
        return jnp.broadcast_to(found, (8, LANE))

    def body(r, carry):
        low = blocks - 2 - 2 * r
        ags = dict(zip(keys, carry))
        tq, ts, tl, tb, tc = {}, {}, {}, {}, {}
        for t in reversed(range(16)):
            i, k = low + t // 8, t % 8
            for s in range(S):
                lanes = slice(k * LANE, (k + 1) * LANE)
                b16 = wide[s, i, 0:16, lanes].astype(bf16)
                c = [wide[s, i, 16 + j * 8 : 16 + (j + 1) * 8, lanes] for j in range(2)]
                for g in range(G):
                    se, su, ds = row8(se_s, s, i, k, g), row8(su_s, s, i, k, g), row8(d_s, s, i, k, g)
                    a = [jnp.exp2(se * rate_ref[g, j * 8 : (j + 1) * 8]) for j in range(2)]
                    gr = [c[j] * ds + ags[s, g, j] for j in range(2)]
                    for j in range(2):
                        ags[s, g, j] = a[j] * gr[j]
                    gb = jnp.concatenate(gr, 0).astype(bf16)
                    ab = jnp.concatenate(a, 0).astype(bf16)
                    gq = gb * (ab * h_s[i * 8 + k, s * G + g])
                    tq[s, g, t] = gq * rate2_ref[g]
                    tl[s, g, t] = gq * two(se)
                    ts[s, g, t] = gb * b16
                    tb[s, g, t] = gb * two(su)
                    tc[s, g, t] = h_s[i * 8 + k + 1, s * G + g] * two(ds)

        def mat(m, s):
            return jnp.concatenate([jnp.concatenate([m[s, g, t] for t in range(16)], 0) for g in range(G)], 1)

        def msum(m, s):
            return jnp.concatenate([sum(m[s, g, t] for g in range(G)) for t in range(16)], 0)

        for s in range(S):
            q = mm(pick, mat(tq, s))
            v = mm(pick, mat(ts, s))
            for h in range(2):
                q_s[s, low + h] = q[h * 8 : (h + 1) * 8]
                s_s[s, low + h] = v[h * 8 : (h + 1) * 8]
            dlog_ref[...] += mm(fold, mat(tl, s))
            for kind, m in enumerate((tb, tc)):
                found = mm_t(one, msum(m, s))[0:8]
                for h in range(2):
                    r_s[s, kind, low + h] = found[:, h * LANE : (h + 1) * LANE]
        return tuple(ags.values())

    ags = lax.fori_loop(0, blocks // 2, body, tuple(ag_s[q * 8 : (q + 1) * 8] for q in range(len(keys))))
    for q in range(len(keys)):
        ag_s[q * 8 : (q + 1) * 8] = ags[q]
    for s in range(S):
        step = step_ref[s]
        u = u_ref[s].astype(f32)
        ds = ds_ref[s]
        sums = s_s[s].reshape(LANE, C)
        dsp = ((q_s[s].reshape(LANE, C) + u * sums) * sigmoid_of_step(step)).astype(bf16)
        dsp_ref[s] = dsp
        du_ref[s] = step * sums + ds * vec_ref[1:2]
        p2_ref[s, 0, 0:LANE] = mm_t(dsp, proj_ref[...])
        for kind in range(2):
            for i in range(blocks):
                p2_ref[s, 0, LANE + 16 * kind + i : LANE + 16 * kind + i + 1] = r_s[s, kind, i, 0:1]
        sum_ref[0:1] += jnp.sum(dsp.astype(f32), axis=0, keepdims=True)
        sum_ref[1:2] += jnp.sum(ds * u, axis=0, keepdims=True)


def scan_specs(S, T, C, reverse):
    at = (lambda i: T // LANE - 1 - i) if reverse else (lambda i: i)
    return dict(
        packed=pl.BlockSpec((S, 1, LANE + 32, LANE), lambda i: (0, at(i), 0, 0)),
        block=pl.BlockSpec((S, LANE, C), lambda i: (0, at(i), 0)),
        masks=pl.BlockSpec((S, LANE, LANE), lambda i: (0, at(i), 0)),
        start=pl.BlockSpec((1, S * C // LANE * 16, LANE), lambda i: (at(i), 0, 0)),
    )


def scan_forward(packed, u, masks, proj_step, vec, rate2e, hot):
    S, T, C = u.shape
    G = C // LANE
    sp = scan_specs(S, T, C, False)
    by_token = pltpu.VMEM((S, LANE // 8, 8, C), f32)
    return pl.pallas_call(
        functools.partial(forward_kernel, S, G),
        grid=(T // LANE,),
        in_specs=[
            sp["packed"], sp["block"], sp["masks"], whole(LANE, C), whole(8, C), whole(G, 16, LANE), whole(LANE, 8 * LANE)
        ],
        out_specs=[sp["block"], sp["block"], sp["start"]],
        out_shape=[jax.ShapeDtypeStruct((S, T, C), f32)] * 2 + [jax.ShapeDtypeStruct((T // LANE, S * G * 16, LANE), f32)],
        scratch_shapes=[
            pltpu.VMEM((S * G * 16, LANE), f32),
            pltpu.VMEM((S, LANE // 8, 32, 8 * LANE), f32),
            pltpu.VMEM((LANE // 8, S, LANE, C), bf16),
            by_token,
            by_token,
        ],
        cost_estimate=cost(30),
        compiler_params=PARAMS,
    )(packed, u, masks, proj_step, vec, rate2e, hot)


def scan_backward(packed, u, step, ds, masks, proj_step, vec, rate2e, rate, hot, starts):
    S, T, C = u.shape
    G = C // LANE
    sp = scan_specs(S, T, C, True)
    by_token = pltpu.VMEM((S, LANE // 8, 8, C), f32)
    return pl.pallas_call(
        functools.partial(backward_kernel, S, G),
        grid=(T // LANE,),
        in_specs=[
            sp["packed"], sp["block"], sp["block"], sp["block"], sp["masks"], whole(LANE, C), whole(8, C),
            whole(G, 16, LANE), whole(G, 16, LANE), whole(LANE, 8 * LANE), sp["start"]
        ],
        out_specs=[sp["block"], sp["block"], sp["packed"], whole(16, C), whole(8, C)],
        out_shape=[
            jax.ShapeDtypeStruct((S, T, C), bf16),
            jax.ShapeDtypeStruct((S, T, C), f32),
            jax.ShapeDtypeStruct((S, T // LANE, LANE + 32, LANE), f32),
            jax.ShapeDtypeStruct((16, C), f32),
            jax.ShapeDtypeStruct((8, C), f32),
        ],
        scratch_shapes=[
            pltpu.VMEM((S * G * 16, LANE), f32),
            pltpu.VMEM((LANE + 1, S * G, 16, LANE), bf16),
            pltpu.VMEM((S, LANE // 8, 32, 8 * LANE), f32),
        ]
        + [by_token] * 5
        + [pltpu.VMEM((S, 2, LANE // 8, 8, LANE), f32)],
        cost_estimate=cost(85),
        compiler_params=PARAMS,
    )(packed, u, step, ds, masks, proj_step, vec, rate2e, rate.astype(bf16), hot, starts)


def after(*arrays):
    def kernel(*refs):
        refs[-1][0] = 0

    return pl.pallas_call(
        kernel,
        in_specs=[pl.BlockSpec(memory_space=pl.ANY) for _ in arrays],
        out_specs=pl.BlockSpec(memory_space=pltpu.SMEM),
        out_shape=jax.ShapeDtypeStruct((1,), jnp.int32),
    )(*arrays)[0]


def line_gather(array, axis):
    count = lax.axis_size(axis)
    right, left = array, array
    window = [array]
    for step in range(1, count):
        right = lax.ppermute(right, axis, [(i, i + 1) for i in range(step - 1, count - 1)])
        left = lax.ppermute(left, axis, [(i, i - 1) for i in range(1, count - step + 1)])
        window = [right] + window + [left]
    return window


def line_gather_at_once(array, axis):
    count = lax.axis_size(axis)
    return lax.all_to_all(jnp.broadcast_to(array[None], (count,) + array.shape), axis, 0, 0)


def line_scatter(blocks, axis):
    return jnp.sum(lax.all_to_all(blocks, axis, 0, 0).astype(f32), axis=0)


class Paired:
    def __init__(self):
        self.context = lax.axis_index("context")
        self.tensor = lax.axis_index("tensor")
        self.core = self.tensor % 2
        self.place = self.context[None]

    def across(self, array):
        return lax.ppermute(array, "context", [(0, 1), (1, 0)])

    def near(self, array):
        return lax.ppermute(array, "tensor", [(0, 1), (1, 0), (2, 3), (3, 2)])

    def far(self, array):
        return lax.ppermute(array, "tensor", [(0, 2), (2, 0), (1, 3), (3, 1)])

    def pieces(self, array, begin):
        half = array.shape[0] // 2
        mine = lax.dynamic_slice_in_dim(array, (self.core + begin) * half, half, 0)
        return self.across(mine), mine

    def pieces_done(self, array, block):
        return [array, joined_halves(block, self.near(block), self.core[None])]

    def normed(self, array, block, gain):
        return normalised_rows([array, block, self.near(block)], self.core[None], gain)

    def total(self, array, begin):
        half = array.shape[0] // 2
        mine = lax.dynamic_slice_in_dim(array, self.core * half, half, 0)
        other = lax.dynamic_slice_in_dim(array, (1 - self.core + begin) * half, half, 0).astype(bf16)
        mine = mine + self.near(other).astype(f32)
        first, second = mine[: half // 2], mine[half // 2 :]
        first = first + self.far(first.astype(bf16)).astype(f32)
        second = second + self.across(second.astype(bf16)).astype(f32)
        first = first + self.across(first.astype(bf16)).astype(f32)
        second = second + self.far(second.astype(bf16)).astype(f32)
        mine = jnp.concatenate([first, second], axis=0)
        other = self.near(mine.astype(bf16)).astype(f32)
        zero = self.core == 0
        return jnp.concatenate([jnp.where(zero, mine, other), jnp.where(zero, other, mine)])

    def share_begin(self, product):
        keep = product((self.tensor, self.tensor ^ 2))
        give = product((self.tensor ^ 1, self.tensor ^ 3))
        return [(k.astype(f32) + self.near(g).astype(f32)) for k, g in zip(keep, give)]

    def share_middle(self, sums):
        own, other = sums
        rows, width = own.shape
        half, width = rows // 2, width // 2
        far = self.far(jnp.stack([own[:half, width:], other[:half, width:]]).astype(bf16))
        across = self.across(other[half:].astype(bf16))
        first = own[:half, :width] + far[0].astype(f32)
        give = other[:half, :width] + far[1].astype(f32)
        second = own[half:] + across.astype(f32)
        return first, give, second

    def share_end(self, sums):
        first, give, second = sums
        width = first.shape[1]
        first = first + self.across(give.astype(bf16)).astype(f32)
        second = second[:, :width] + self.far(second[:, width:].astype(bf16)).astype(f32)
        return jnp.concatenate([first, second], axis=0)

    def row_total(self, array):
        array = array + self.near(array)
        return array + self.far(array)

    def vector_total(self, array):
        return self.row_total(array + self.across(array))

    def both(self, array):
        other = self.across(array)
        zero = self.context == 0
        return jnp.stack([jnp.where(zero, array, other), jnp.where(zero, other, array)])


class General:
    def __init__(self, seqs):
        self.seqs = seqs
        self.place = jnp.zeros((1,), jnp.int32)

    def pieces(self, array, begin):
        return lax.all_gather(array, "context", tiled=True), array

    def pieces_done(self, array, block):
        return [self.in_order([block], self.seqs).reshape(block.shape)]

    def normed(self, array, block, gain):
        inv_rms = normalised_rows([array], self.place, gain)[1]
        return normalised_rows(self.pieces_done(array, block), self.place, gain)[0], inv_rms

    def in_order(self, arrays, seqs):
        array = arrays[0].reshape(lax.axis_size("context"), seqs, -1, arrays[0].shape[-1])
        return array.swapaxes(0, 1).reshape(seqs, -1, array.shape[-1])

    def total(self, array, begin):
        return lax.psum(array, ("context", "tensor"))

    def share_begin(self, product):
        return [product((block,))[0].astype(f32) for block in range(lax.axis_size("tensor"))]

    def share_middle(self, sums):
        return sums

    def share_end(self, sums):
        parts = jnp.concatenate(sums, axis=-1)
        shape = parts.shape
        parts = parts.reshape(self.seqs, lax.axis_size("context"), -1, shape[-1]).swapaxes(0, 1).reshape(shape)
        parts = lax.psum_scatter(parts, "context", scatter_dimension=0, tiled=True)
        return lax.psum_scatter(parts, "tensor", scatter_dimension=1, tiled=True)

    def row_total(self, array):
        return lax.psum(array, "tensor")

    def vector_total(self, array):
        return lax.psum(array, ("context", "tensor"))

    def both(self, array):
        return lax.all_gather(array, "context")


def dot(a, b, out=f32):
    return jnp.dot(a, b, preferred_element_type=f32).astype(out)


def dot_t(a, b, out=f32):
    return lax.dot_general(a, b, (((1,), (1,)), ((), ())), preferred_element_type=f32).astype(out)


def t_dot(a, b, out=f32):
    return lax.dot_general(a, b, (((0,), (0,)), ((), ())), preferred_element_type=f32).astype(out)


def on_device(
    block_input,
    output_grad,
    doc_lengths,
    norm_gain,
    input_proj,
    conv_weight,
    conv_bias,
    select_proj,
    step_proj,
    step_bias,
    decay_log,
    skip_weight,
    output_proj,
):
    seqs, piece, model_width = block_input.shape
    shards, contexts, tensors = (lax.axis_size(axis) for axis in ("shards", "context", "tensor"))
    shard, context, tensor = (lax.axis_index(axis) for axis in ("shards", "context", "tensor"))
    moves = Paired() if (contexts, tensors) == (2, 4) else General(seqs)
    length = piece * contexts
    tokens = seqs * length
    depth = input_proj.shape[0]
    part = conv_weight.shape[0] // contexts
    inner = part * shards
    states = decay_log.shape[1]
    rank = step_proj.shape[0] * shards
    selected = select_proj.shape[1]
    taps = conv_weight.shape[1]
    share_width = model_width // tensors

    def mine(array):
        return lax.dynamic_slice_in_dim(array, context * part, part, 0)

    def my_columns(array, begin):
        blocks = [
            lax.dynamic_slice_in_dim(array, (block * contexts + context + begin) * part, part, array.ndim - 1)
            for block in range(shards)
        ]
        return jnp.concatenate(blocks, axis=-1)

    rows_flat = block_input.reshape(seqs * piece, model_width)
    row_block, row_slice = moves.pieces(rows_flat, 0)
    in_x = my_columns(input_proj[:, 0], after(row_slice))
    bounds = jnp.cumsum(doc_lengths, axis=-1)[:, :2, None, None]
    position, lane = (lax.broadcasted_iota(jnp.int32, (1, length, LANE), axis) for axis in (1, 2))
    other = jnp.where(lane < taps, position - lane, position + lane - taps)

    def document(at):
        return (at >= bounds[:, 0]).astype(jnp.int32) + (at >= bounds[:, 1]).astype(jnp.int32)

    masks = (document(position) == document(other)) & (other >= 0) & (other < length)
    masks = masks.astype(f32)

    vectors = jnp.concatenate(
        [
            mine(select_proj),
            mine(conv_weight),
            mine(decay_log),
            mine(conv_bias)[:, None],
            mine(step_bias)[:, None],
            mine(skip_weight)[:, None],
        ],
        axis=1,
    )
    vectors = jnp.pad(vectors, ((0, 0), (0, 2 * LANE - vectors.shape[1])))
    flat = [in_x, my_columns(step_proj, 0), vectors.reshape(-1, inner), norm_gain.reshape(-1, inner)]
    flat = [jnp.pad(f, ((0, -f.shape[0] % 16), (0, 0))) for f in flat]
    window = line_gather(jnp.concatenate(flat, axis=0), "shards")
    proj_x, proj_step, vectors, gain = unpacked(window, [f.shape[0] for f in flat], shard[None], masks)
    gain = gain[:, : norm_gain.shape[0] // inner].reshape(model_width).astype(f32)
    normed, inv_rms = moves.normed(rows_flat, row_block, gain)
    proj_x = proj_x.reshape(model_width, inner)
    proj_step = proj_step[:, : step_proj.shape[0]].reshape(rank, inner)
    vectors = vectors[:, : 2 * LANE * part // inner].reshape(inner, 2 * LANE)
    proj_select = vectors[:, :selected]
    rest = vectors[:, selected:].astype(f32)
    decay_rate = -jnp.exp(rest[:, taps : taps + states])
    at = taps + states
    conv_vec = jnp.concatenate([rest[:, :taps].T, rest[:, at][None], jnp.zeros((7 - taps, inner), f32)], axis=0)
    scan_vec = jnp.concatenate([rest[:, at + 1 : at + 3].T, jnp.zeros((6, inner), f32)], axis=0)
    select_low, select_state = proj_select[:, :rank], proj_select[:, rank:]

    grad_flat = output_grad.reshape(seqs * piece, model_width)

    in_z = my_columns(input_proj[:, 1], after(window[len(window) // 2 - 1]))
    out_own = mine(output_proj)
    out_own = [out_own[:, i * inner : (i + 1) * inner] for i in range(model_width // inner)]
    others = jnp.concatenate([in_z] + out_own + [jnp.zeros((16, inner), bf16)], axis=0)
    others = lax.dynamic_slice_in_dim(others, after(proj_x) * 16, others.shape[0] - 16, 0)
    others = line_gather_at_once(others, "shards")

    x_part, values, projected = convolve(
        normed, proj_x, conv_vec, masks, select_low, select_state.T, moves.place, taps
    )

    def total(packed, begin):
        return moves.total(packed.reshape(-1, LANE), begin).reshape(packed.shape)

    projected = total(projected, 0)
    grad_block = moves.pieces(grad_flat, after(row_block))[0]

    hot = hot_rows()

    def by_group(array, begin=0.0):
        return (array.T + begin).reshape(states, inner // LANE, LANE).swapaxes(0, 1)

    ssm_out, step, starts = scan_forward(
        projected, values, masks, proj_step, scan_vec, by_group(decay_rate * LOG2E), hot
    )

    proj_z = others[:, :depth].reshape(model_width, inner)
    proj_out = [others[:, depth + i * part : depth + (i + 1) * part] for i in range(model_width // inner)]
    proj_out = jnp.concatenate(proj_out, axis=-1).reshape(inner, model_width)
    grad_all = moves.pieces_done(grad_flat, grad_block)
    gated, grad_z, grad_ssm = gates(normed, grad_all, proj_z, proj_out, ssm_out, moves.place)

    def weight_grad(lefts, rights):
        if not isinstance(rights, list):
            lefts, rights = ([a.reshape(-1, a.shape[-1])] for a in (lefts, rights))
        return sum(t_dot(a, b) for a, b in zip(lefts, rights)).astype(bf16)

    early = lax.all_to_all(weight_grad(normed, grad_z).reshape(shards, depth, inner), "shards", 0, 0)
    middle = lax.all_to_all(weight_grad(gated, grad_all).reshape(shards, part, model_width), "shards", 0, 0)
    def chosen(weights, blocks, axis, begin=0):
        return jnp.concatenate(
            [lax.dynamic_slice_in_dim(weights, (b + begin) * share_width, share_width, axis) for b in blocks], axis
        )

    out_sums = moves.share_begin(lambda blocks: [dot(gated[i], chosen(proj_out, blocks, 1), bf16) for i in range(gated.shape[0])])
    out_sums_2 = moves.share_middle(out_sums)
    out_share = moves.share_end(out_sums_2)
    own_columns = tensor * share_width
    input_share = lax.dynamic_slice_in_dim(block_input, own_columns, share_width, 2).astype(f32)
    block_output = (input_share + out_share.reshape(input_share.shape)).astype(bf16)

    grad_step_pre, grad_direct, partial_grad, grad_decay, scan_sums = scan_backward(
        projected,
        values,
        step,
        grad_ssm,
        masks,
        proj_step,
        scan_vec,
        by_group(decay_rate * LOG2E),
        by_group(decay_rate, after(*out_sums).astype(f32)),
        hot,
        starts,
    )
    grad_decay_log = grad_decay.T * decay_rate
    step_low = projected[:, :, :rank].reshape(tokens, rank).astype(bf16)
    grad_step_proj = t_dot(step_low, grad_step_pre.reshape(tokens, inner))
    pulled = after(early, partial_grad, *out_sums_2)
    grad_in_z = jnp.sum(early.astype(f32), axis=0) + pulled.astype(f32)
    z_pair = moves.both(grad_in_z.astype(bf16))
    partial_grad = total(partial_grad, pulled)

    grad_x, conv_sums, grad_selected = convolve_back(
        partial_grad,
        grad_direct,
        x_part,
        conv_vec + after(block_output, partial_grad).astype(f32),
        masks,
        select_low,
        jnp.pad(select_state, ((0, 0), (0, LANE - select_state.shape[1]))),
        moves.place,
        normed.shape[0],
        taps,
    )
    grad_select = t_dot(values.reshape(tokens, inner), grad_selected.reshape(tokens, -1))[:, :selected]

    small = jnp.concatenate(
        [
            grad_select,
            conv_sums[:taps].T,
            grad_decay_log,
            conv_sums[taps][:, None],
            scan_sums[:2].T,
        ],
        axis=1,
    ).astype(bf16)
    sent = after(middle, conv_sums)
    small = small + sent.astype(bf16)
    out_pair = moves.both((jnp.sum(middle.astype(f32), axis=0) + sent.astype(f32)).astype(bf16))
    small = jnp.pad(small, ((0, 0), (0, 2 * LANE - small.shape[1])))
    late_local = jnp.concatenate(
        [
            weight_grad(normed, grad_x).reshape(shards, depth, inner),
            grad_step_proj.astype(bf16).reshape(shards, -1, inner),
            small.reshape(shards, -1, inner),
        ],
        axis=1,
    )
    begin = after(late_local, z_pair)

    def normed_part(blocks):
        blocks = jnp.stack([jnp.asarray(b, jnp.int32) + begin for b in blocks])
        return products(grad_x, grad_z, proj_x, proj_z, blocks, share_width)

    grad_normed = moves.share_end(moves.share_middle(moves.share_begin(normed_part))).reshape(seqs, piece, share_width)
    inv_rms = inv_rms[:, :1].reshape(seqs, piece, 1)
    unit_share = input_share * inv_rms
    weighted = grad_normed * lax.dynamic_slice_in_dim(gain, own_columns, share_width, 0)
    row_dots = moves.row_total(jnp.sum(unit_share * weighted, axis=-1))[:, :, None]
    grad_share = lax.dynamic_slice_in_dim(output_grad, own_columns, share_width, 2).astype(f32)
    input_grad = grad_share + inv_rms * (weighted - unit_share * (row_dots / model_width))

    late = line_scatter(late_local, "shards") + after(grad_normed, z_pair, out_pair).astype(f32)
    grad_in_x = late[:depth]
    gain_part = jnp.sum(in_x.astype(f32) * grad_in_x, axis=1) + jnp.sum(in_z.astype(f32) * grad_in_z, axis=1)
    grad_gain = moves.vector_total(gain_part) / norm_gain.astype(f32)

    def columns_of(pair):
        pair = pair.astype(f32).reshape(pair.shape[:-1] + (shards, part))
        return jnp.moveaxis(pair, 0, -2).reshape(pair.shape[1], -1)

    late = moves.both(late.astype(bf16))
    grad_in = interleaved(late, z_pair, depth, part)
    grad_step_proj = columns_of(late[:, depth : depth + step_proj.shape[0]])
    small = late[:, depth + step_proj.shape[0] :].reshape(contexts * part, 2 * LANE).astype(f32)
    grad_out_proj = out_pair.reshape(contexts * part, model_width).astype(f32)
    at = selected + taps + states
    return (
        block_output,
        input_grad,
        grad_gain,
        grad_in,
        small[:, selected : selected + taps],
        small[:, at],
        small[:, :selected],
        grad_step_proj,
        small[:, at + 1],
        small[:, selected + taps : at],
        small[:, at + 2],
        grad_out_proj,
    )


def solution(mesh):
    placed = (
        P("shards", "context", None),
        P("shards", "context", None),
        P("shards", None),
        P("shards"),
        P("shards", None, "tensor"),
        P(("tensor", "shards"), None),
        P(("tensor", "shards")),
        P(("tensor", "shards"), None),
        P("shards", "tensor"),
        P(("tensor", "shards")),
        P(("tensor", "shards"), None),
        P(("tensor", "shards")),
        P(("tensor", "shards"), None),
    )
    return jax.shard_map(
        on_device,
        mesh=mesh,
        in_specs=placed,
        out_specs=(
            P("shards", "context", "tensor"),
            P("shards", "context", "tensor"),
            P("shards"),
            P("shards", None, "tensor"),
            P(("tensor", "shards"), None),
            P(("tensor", "shards")),
            P(("tensor", "shards"), None),
            P("shards", "tensor"),
            P(("tensor", "shards")),
            P(("tensor", "shards"), None),
            P(("tensor", "shards")),
            P(("tensor", "shards"), None),
        ),
        check_vma=False,
    )
```
